512 devices in a mesh: rows: 128 (over z, x_lo, y), cols: 4 (over x_hi, core).
Axes of the slice: x: 4 (x_hi: 2, x_lo: 2; x = x_hi * 2 + x_lo), y: 4, z: 16, core: 2. Of those that a mesh axis runs over, the one named last changes fastest.
Arguments:
- feature_one: bfloat16 [1024, 20480], P('rows', 'cols'), may hold values from -6 to 6
- feature_two: bfloat16 [512, 20480], P('rows', 'cols'), may hold values from -6 to 6
- feature_three: bfloat16 [256, 20480], P('rows', 'cols'), may hold values from -6 to 6
- feature_four: bfloat16 [128, 20480], P('rows', 'cols'), may hold values from -6 to 6
- kernel_one: bfloat16 [3, 3, 64, 64], replicated, may hold values from -0.25 to 0.25
- kernel_two: bfloat16 [3, 3, 128, 128], replicated, may hold values from -0.1875 to 0.1875
- kernel_three: bfloat16 [3, 3, 256, 256], replicated, may hold values from -0.125 to 0.125
- project_two: bfloat16 [128, 64], replicated, may hold values from -0.5 to 0.5
- project_three: bfloat16 [256, 64], replicated, may hold values from -0.375 to 0.375
- project_four: bfloat16 [512, 64], replicated, may hold values from -0.25 to 0.25
- cotangent: bfloat16 [1024, 20480], P('rows', 'cols'), may hold values from -6 to 6
Outputs:
- grad_feature_one: bfloat16 [1024, 20480], P('rows', 'cols')
- grad_feature_two: bfloat16 [512, 20480], P('rows', 'cols')
- grad_feature_three: bfloat16 [256, 20480], P('rows', 'cols')
- grad_feature_four: bfloat16 [128, 20480], P('rows', 'cols')
- grad_kernel_one: bfloat16 [3, 3, 64, 64], replicated
- grad_kernel_two: bfloat16 [3, 3, 128, 128], replicated
- grad_kernel_three: bfloat16 [3, 3, 256, 256], replicated
- grad_project_two: bfloat16 [128, 64], replicated
- grad_project_three: bfloat16 [256, 64], replicated
- grad_project_four: bfloat16 [512, 64], replicated
The draws below stay inside these ranges and needn't reach their ends.
All inputs are finite; a program needn't handle non-finite values.
Results may differ from the reference program's by a relative error of at most 0.017.
Values may be sent and summed in bfloat16 or wider, within the bound.
No kernel may reach another device: no remote copies, remote signals or barrier semaphores. Data moves between devices by JAX's collectives and lax.ppermute only.
A program may use at most 64 MiB of HBM per device.

```python
import jax
import jax.numpy as jnp
import numpy as np
from jax import lax

FEAT_ONE = 64
FEAT_TWO = 128
FEAT_THREE = 256
FEAT_FOUR = 512
GRID_ROWS = 1024
GRID_COLS = 320


def block_levels(own_key, dims, cuts, low, largest):
    loudness = 1.0
    for axis_at, parts in cuts:
        heights = jax.random.uniform(jax.random.fold_in(jax.random.fold_in(own_key, 6), axis_at), (parts,), jnp.float32, low / len(cuts), largest / len(cuts))
        loudness = loudness * jnp.repeat(jnp.exp(heights), dims[axis_at] // parts).reshape((-1,) + (1,) * (len(dims) - 1 - axis_at))
    return loudness


def normal_values(rng, extent, spread, bound, cuts=(), kind=jnp.bfloat16):
    values = spread * jax.random.normal(rng, extent, jnp.float32)
    if cuts:
        values = values * block_levels(rng, extent, cuts, -0.22, 0.18)
    return jnp.clip(values, -bound, bound).astype(kind)


def setup_inputs(seed: int = 0) -> dict:
    streams_of = jax.random.split(jax.random.key(seed), 12)
    return {
        "feature_one": normal_values(streams_of[0], (GRID_ROWS, GRID_COLS * FEAT_ONE), 1.0, 6.0, ((0, 128), (1, 4))),
        "feature_two": normal_values(streams_of[1], (GRID_ROWS // 2, GRID_COLS // 2 * FEAT_TWO), 1.0, 6.0, ((0, 128), (1, 4))),
        "feature_three": normal_values(streams_of[2], (GRID_ROWS // 4, GRID_COLS // 4 * FEAT_THREE), 1.0, 6.0, ((0, 128), (1, 4))),
        "feature_four": normal_values(streams_of[3], (GRID_ROWS // 8, GRID_COLS // 8 * FEAT_FOUR), 1.0, 6.0, ((0, 128), (1, 4))),
        "kernel_one": normal_values(streams_of[4], (3, 3, FEAT_ONE, FEAT_ONE), (9 * FEAT_ONE) ** -0.5, 0.25),
        "kernel_two": normal_values(streams_of[5], (3, 3, FEAT_TWO, FEAT_TWO), (9 * FEAT_TWO) ** -0.5, 0.1875),
        "kernel_three": normal_values(streams_of[6], (3, 3, FEAT_THREE, FEAT_THREE), (9 * FEAT_THREE) ** -0.5, 0.125),
        "project_two": normal_values(streams_of[7], (FEAT_TWO, FEAT_ONE), FEAT_TWO ** -0.5, 0.5),
        "project_three": normal_values(streams_of[8], (FEAT_THREE, FEAT_ONE), FEAT_THREE ** -0.5, 0.375),
        "project_four": normal_values(streams_of[9], (FEAT_FOUR, FEAT_ONE), FEAT_FOUR ** -0.5, 0.25),
        "cotangent": normal_values(streams_of[10], (GRID_ROWS, GRID_COLS * FEAT_ONE), 1.0, 6.0, ((0, 128), (1, 4))),
    }


def up_table(scale):
    places = (np.arange(scale) + 0.5) / scale - 0.5
    table = np.stack([np.maximum(-places, 0.0), 1.0 - np.abs(places), np.maximum(places, 0.0)], 1)
    return jnp.asarray(table, jnp.float32)

def upsample(padded, scale):
    table = up_table(scale)
    row_count = padded.shape[0] - 2
    col_count = padded.shape[1] - 2
    stacked = jnp.stack([padded[offset:offset + row_count] for offset in range(3)])
    finer = jnp.einsum('ij,jkmc->kimc', table, stacked, precision=lax.Precision.HIGHEST)
    finer = finer.reshape(row_count * scale, col_count + 2, -1)
    stacked = jnp.stack([finer[:, offset:offset + col_count] for offset in range(3)])
    finer = jnp.einsum('ij,jakc->akic', table, stacked, precision=lax.Precision.HIGHEST)
    return finer.reshape(row_count * scale, col_count * scale, -1)

def upsample_back(grad_fine, scale):
    table = up_table(scale)
    big_rows, big_cols, chans = grad_fine.shape
    row_count = big_rows // scale
    col_count = big_cols // scale
    split = grad_fine.reshape(big_rows, col_count, scale, chans)
    pieces = jnp.einsum('ij,akic->jakc', table, split, precision=lax.Precision.HIGHEST)
    middle = jnp.zeros((big_rows, col_count + 2, chans), jnp.float32)
    for offset in range(3):
        middle = middle.at[:, offset:offset + col_count].add(pieces[offset])
    split = middle.reshape(row_count, scale, col_count + 2, chans)
    pieces = jnp.einsum('ij,kimc->jkmc', table, split, precision=lax.Precision.HIGHEST)
    result = jnp.zeros((row_count + 2, col_count + 2, chans), jnp.float32)
    for offset in range(3):
        result = result.at[offset:offset + row_count].add(pieces[offset])
    return result

def clamp_fold(padded):
    inner = padded[1:-1].at[0].add(padded[0]).at[-1].add(padded[-1])
    inner = inner.at[:, 1].add(inner[:, 0]).at[:, -2].add(inner[:, -1])
    return inner[:, 1:-1]

def conv_taps(padded, kernel):
    row_count = padded.shape[0] - 2
    col_count = padded.shape[1] - 2
    total = jnp.zeros((row_count * col_count, kernel.shape[3]), jnp.float32)
    for tap_row in range(3):
        for tap_col in range(3):
            window = padded[tap_row:tap_row + row_count, tap_col:tap_col + col_count].reshape(row_count * col_count, -1)
            total = total + jnp.dot(window, kernel[tap_row, tap_col], preferred_element_type=jnp.float32)
    return total.reshape(row_count, col_count, -1)

def kernel_grad(padded, grad_pre):
    row_count, col_count, chans = grad_pre.shape
    flat_grad = grad_pre.reshape(row_count * col_count, chans)
    taps = []
    for tap_row in range(3):
        for tap_col in range(3):
            window = padded[tap_row:tap_row + row_count, tap_col:tap_col + col_count].reshape(row_count * col_count, -1)
            taps.append(lax.dot_general(window, flat_grad, (((0,), (0,)), ((), ())), preferred_element_type=jnp.float32))
    return jnp.stack(taps).reshape(3, 3, taps[0].shape[0], chans)

def zero_pad(values):
    return jnp.pad(values, ((1, 1), (1, 1), (0, 0)))

def gelu_back(values, grad_out):
    return jax.vjp(jax.nn.gelu, values)[1](grad_out)[0]

def reference(feature_one, feature_two, feature_three, feature_four, kernel_one, kernel_two, kernel_three, project_two, project_three, project_four, cotangent):
    widths = (FEAT_ONE, FEAT_TWO, FEAT_THREE, FEAT_FOUR)
    inputs = (feature_one, feature_two, feature_three, feature_four)
    maps = [arr.reshape(arr.shape[0], arr.shape[1] // chans, chans) for arr, chans in zip(inputs, widths)]
    kernels = (kernel_one, kernel_two, kernel_three)
    projects = (project_two, project_three, project_four)
    scales = (2, 4, 8)
    padded_in = []
    pres = []
    acts = []
    for branch in range(3):
        padded = zero_pad(maps[branch])
        pre_act = maps[branch].astype(jnp.float32) + conv_taps(padded, kernels[branch])
        padded_in.append(padded)
        pres.append(pre_act)
        acts.append(jax.nn.gelu(pre_act).astype(jnp.bfloat16))
    coarse_in = (acts[1], acts[2], maps[3])
    merged = acts[0].astype(jnp.float32)
    for branch in range(3):
        source = coarse_in[branch]
        shape_now = source.shape
        small = jnp.dot(source.reshape(-1, shape_now[2]), projects[branch], preferred_element_type=jnp.float32)
        small = small.astype(jnp.bfloat16).reshape(shape_now[0], shape_now[1], FEAT_ONE)
        edged = jnp.pad(small.astype(jnp.float32), ((1, 1), (1, 1), (0, 0)), mode='edge')
        merged = merged + upsample(edged, scales[branch])
    upstream_grad = cotangent.reshape(merged.shape).astype(jnp.float32)
    gate_grad = gelu_back(merged, upstream_grad).astype(jnp.bfloat16)
    gate_float = gate_grad.astype(jnp.float32)
    total_cells = GRID_ROWS * GRID_COLS
    proj_grads = []
    backs = []
    for branch in range(3):
        source = coarse_in[branch]
        shape_now = source.shape
        small_grad = clamp_fold(upsample_back(gate_float, scales[branch])).astype(jnp.bfloat16)
        flat = small_grad.reshape(-1, FEAT_ONE)
        summed = lax.dot_general(source.reshape(-1, shape_now[2]), flat, (((0,), (0,)), ((), ())), preferred_element_type=jnp.float32)
        cells = total_cells // 4 ** (branch + 1)
        proj_grads.append((summed * cells ** (-0.5)).astype(jnp.bfloat16))
        back = lax.dot_general(flat, projects[branch], (((1,), (1,)), ((), ())), preferred_element_type=jnp.float32)
        backs.append(back.reshape(shape_now))
    grad_four = backs[2].astype(jnp.bfloat16)
    upstream = (gate_float, backs[0], backs[1])
    feat_grads = []
    kern_grads = []
    for branch in range(3):
        grad_pre = gelu_back(pres[branch], upstream[branch]).astype(jnp.bfloat16)
        flipped = jnp.transpose(kernels[branch][::-1, ::-1], (0, 1, 3, 2))
        back = conv_taps(zero_pad(grad_pre), flipped)
        feat_grads.append((grad_pre.astype(jnp.float32) + back).astype(jnp.bfloat16))
        cells = total_cells // 4 ** branch
        kern_grads.append((kernel_grad(padded_in[branch], grad_pre) * cells ** (-0.5)).astype(jnp.bfloat16))
    outputs = [grad.reshape(arr.shape) for grad, arr in zip(feat_grads, inputs[:3])]
    return (outputs[0], outputs[1], outputs[2], grad_four.reshape(feature_four.shape), kern_grads[0], kern_grads[1], kern_grads[2], proj_grads[0], proj_grads[1], proj_grads[2])
```

```python
import jax
import jax.numpy as jnp
import numpy as np
from jax import lax
from jax.sharding import Mesh
from jax.sharding import PartitionSpec as P

FEAT_ONE = 64
FEAT_TWO = 128
FEAT_THREE = 256
FEAT_FOUR = 512

ROWS = ("z", "x_lo", "y")
COLS = ("x_hi", "core")
PLANE = ("x_lo", "y", "x_hi")
PACK_ROWS = 3328


def passed_along(block, axis, distance):
    devices = range(lax.axis_size(axis))
    route = [(i - distance, i) for i in devices if i - distance in devices]
    return lax.ppermute(block, axis, route)


def padded_2(cells, sides, width):
    for axis, dim in sides:
        count = lax.axis_size(axis)
        ends = count - 1
        head = lax.slice_in_dim(cells, 0, width, axis=dim)
        tail = lax.slice_in_dim(cells, cells.shape[dim] - width, cells.shape[dim], axis=dim)
        cells = jnp.concatenate(
            [
                lax.ppermute(tail, axis, [(i, (i + 1) % count) for i in range(ends)]),
                cells,
                lax.ppermute(head, axis, [((i + 1) % count, i) for i in range(ends)]),
            ],
            axis=dim,
        )
    return cells


def up_table(scale):
    places = (np.arange(scale) + 0.5) / scale - 0.5
    table = np.stack([np.maximum(-places, 0.0), 1.0 - np.abs(places), np.maximum(places, 0.0)], 1)
    return jnp.asarray(table, jnp.float32)


def upsample(padded, scale):
    table = up_table(scale)
    row_count = padded.shape[0] - 2
    col_count = padded.shape[1] - 2
    stacked = jnp.stack([padded[offset : offset + row_count] for offset in range(3)])
    finer = jnp.einsum("ij,jkmc->kimc", table, stacked, precision=lax.Precision.HIGHEST)
    finer = finer.reshape(row_count * scale, col_count + 2, -1)
    stacked = jnp.stack([finer[:, offset : offset + col_count] for offset in range(3)])
    finer = jnp.einsum("ij,jakc->akic", table, stacked, precision=lax.Precision.HIGHEST)
    return finer.reshape(row_count * scale, col_count * scale, -1)


def upsample_back(grad_fine, scale):
    table = up_table(scale)
    big_rows, big_cols, chans = grad_fine.shape
    row_count = big_rows // scale
    col_count = big_cols // scale
    split = grad_fine.reshape(big_rows, col_count, scale, chans)
    pieces = jnp.einsum("ij,akic->jakc", table, split, precision=lax.Precision.HIGHEST)
    middle = jnp.zeros((big_rows, col_count + 2, chans), jnp.float32)
    for offset in range(3):
        middle = middle.at[:, offset : offset + col_count].add(pieces[offset])
    split = middle.reshape(row_count, scale, col_count + 2, chans)
    pieces = jnp.einsum("ij,kimc->jkmc", table, split, precision=lax.Precision.HIGHEST)
    result = jnp.zeros((row_count + 2, col_count + 2, chans), jnp.float32)
    for offset in range(3):
        result = result.at[offset : offset + row_count].add(pieces[offset])
    return result


def conv_taps(padded, kernel):
    row_count = padded.shape[0] - 2
    col_count = padded.shape[1] - 2
    total = jnp.zeros((row_count * col_count, kernel.shape[3]), jnp.float32)
    for tap_row in range(3):
        for tap_col in range(3):
            window = padded[tap_row : tap_row + row_count, tap_col : tap_col + col_count].reshape(
                row_count * col_count, -1
            )
            total = total + jnp.dot(
                window, kernel[tap_row, tap_col], preferred_element_type=jnp.float32
            )
    return total.reshape(row_count, col_count, -1)


def kernel_grad(padded, grad_pre):
    row_count, col_count, chans = grad_pre.shape
    flat_grad = grad_pre.reshape(row_count * col_count, chans)
    taps = []
    for tap_row in range(3):
        for tap_col in range(3):
            window = padded[tap_row : tap_row + row_count, tap_col : tap_col + col_count].reshape(
                row_count * col_count, -1
            )
            taps.append(
                lax.dot_general(
                    window, flat_grad, (((0,), (0,)), ((), ())), preferred_element_type=jnp.float32
                )
            )
    return jnp.stack(taps).reshape(3, 3, taps[0].shape[0], chans)


def edge_fix(padded):
    at_top = lax.axis_index(ROWS) == 0
    at_bottom = lax.axis_index(ROWS) == lax.axis_size(ROWS) - 1
    at_left = lax.axis_index(COLS) == 0
    at_right = lax.axis_index(COLS) == lax.axis_size(COLS) - 1
    padded = padded.at[0].set(jnp.where(at_top, padded[1], padded[0]))
    padded = padded.at[-1].set(jnp.where(at_bottom, padded[-2], padded[-1]))
    padded = padded.at[:, 0].set(jnp.where(at_left, padded[:, 1], padded[:, 0]))
    padded = padded.at[:, -1].set(jnp.where(at_right, padded[:, -2], padded[:, -1]))
    return padded


def fold_rims(padded):
    from_above = passed_along(padded[-1], ROWS, 1)
    from_below = passed_along(padded[0], ROWS, -1)
    from_above = jnp.where(lax.axis_index(ROWS) == 0, padded[0], from_above)
    from_below = jnp.where(
        lax.axis_index(ROWS) == lax.axis_size(ROWS) - 1, padded[-1], from_below
    )
    inner = padded[1:-1].at[0].add(from_above).at[-1].add(from_below)
    from_left = passed_along(inner[:, -1], COLS, 1)
    from_right = passed_along(inner[:, 0], COLS, -1)
    from_left = jnp.where(lax.axis_index(COLS) == 0, inner[:, 0], from_left)
    from_right = jnp.where(
        lax.axis_index(COLS) == lax.axis_size(COLS) - 1, inner[:, -1], from_right
    )
    inner = inner[:, 1:-1]
    return inner.at[:, 0].add(from_left).at[:, -1].add(from_right)


def gelu_back(values, grad_out):
    return jax.vjp(jax.nn.gelu, values)[1](grad_out)[0]


def packed_sums(sums):
    first = sums[0].reshape(576, 64)
    rest = jnp.concatenate([first, sums[3], sums[4], sums[5]], axis=0)
    rest = jnp.concatenate(jnp.split(rest, 4, axis=0), axis=1)
    second = jnp.concatenate(jnp.split(sums[1].reshape(1152, 128), 2, axis=0), axis=1)
    third = sums[2].reshape(2304, 256)
    packed = jnp.concatenate([third, second, rest], axis=0)
    return jnp.pad(packed, ((0, PACK_ROWS - packed.shape[0]), (0, 0)))


def unpacked_sums(packed):
    third = packed[:2304].reshape(3, 3, 256, 256)
    second = packed[2304:2880]
    second = jnp.concatenate(jnp.split(second, 2, axis=1), axis=0).reshape(3, 3, 128, 128)
    rest = packed[2880:3248]
    rest = jnp.concatenate(jnp.split(rest, 4, axis=1), axis=0)
    first = rest[:576].reshape(3, 3, 64, 64)
    return first, second, third, rest[576:704], rest[704:960], rest[960:1472]


def swapped(block, axis, flip):
    return lax.ppermute(block, axis, [(i, i ^ flip) for i in range(lax.axis_size(axis))])


def kept_half(values, axis, flip, dim):
    bit = (lax.axis_index(axis) // flip) % 2
    half = values.shape[dim] // 2
    keep = lax.dynamic_slice_in_dim(values, bit * half, half, axis=dim)
    send = lax.dynamic_slice_in_dim(values, (1 - bit) * half, half, axis=dim)
    got = swapped(send.astype(jnp.bfloat16), axis, flip)
    return keep + got.astype(jnp.float32)


def both_halves(values, axis, flip, dim):
    bit = (lax.axis_index(axis) // flip) % 2
    got = swapped(values, axis, flip)
    low = jnp.where(bit == 0, values, got)
    high = jnp.where(bit == 0, got, values)
    return jnp.concatenate([low, high], axis=dim)


def summed_over_devices(packed):
    width = packed.shape[1]
    part = kept_half(packed, "core", 1, 0)
    pieces = part.astype(jnp.bfloat16).reshape(16, -1, width)
    pieces = lax.all_to_all(pieces, PLANE, 0, 0)
    part = jnp.sum(pieces.astype(jnp.float32), axis=0)
    part = kept_half(part, "z", 1, 1)
    part = kept_half(part, "z", 2, 0)
    for flip in (4, 8):
        part = part.astype(jnp.bfloat16)
        part = part.astype(jnp.float32) + swapped(part, "z", flip).astype(jnp.float32)
    part = part.astype(jnp.bfloat16)
    part = both_halves(part, "z", 2, 0)
    part = both_halves(part, "z", 1, 1)
    pieces = jnp.broadcast_to(part[None], (16,) + part.shape)
    part = lax.all_to_all(pieces, PLANE, 0, 0).reshape(-1, width)
    return both_halves(part, "core", 1, 0)


def on_device(
    feature_one,
    feature_two,
    feature_three,
    feature_four,
    kernel_one,
    kernel_two,
    kernel_three,
    project_two,
    project_three,
    project_four,
    cotangent,
):
    widths = (FEAT_ONE, FEAT_TWO, FEAT_THREE, FEAT_FOUR)
    inputs = (feature_one, feature_two, feature_three, feature_four)
    maps = [
        arr.reshape(arr.shape[0], arr.shape[1] // chans, chans)
        for arr, chans in zip(inputs, widths)
    ]
    kernels = (kernel_one, kernel_two, kernel_three)
    projects = (project_two, project_three, project_four)
    scales = (2, 4, 8)
    padded_in = []
    pres = []
    acts = []
    for branch in range(3):
        padded = padded_2(maps[branch], ((ROWS, 0), (COLS, 1)), 1)
        pre_act = maps[branch].astype(jnp.float32) + conv_taps(padded, kernels[branch])
        padded_in.append(padded)
        pres.append(pre_act)
        acts.append(jax.nn.gelu(pre_act).astype(jnp.bfloat16))
    coarse_in = (acts[1], acts[2], maps[3])
    merged = acts[0].astype(jnp.float32)
    for branch in range(3):
        source = coarse_in[branch]
        shape_now = source.shape
        edged = edge_fix(padded_2(source, ((ROWS, 0), (COLS, 1)), 1))
        small = jnp.dot(
            edged.reshape(-1, shape_now[2]), projects[branch], preferred_element_type=jnp.float32
        )
        small = small.astype(jnp.bfloat16).reshape(shape_now[0] + 2, shape_now[1] + 2, FEAT_ONE)
        merged = merged + upsample(small.astype(jnp.float32), scales[branch])
    upstream_grad = cotangent.reshape(merged.shape).astype(jnp.float32)
    gate_grad = gelu_back(merged, upstream_grad).astype(jnp.bfloat16)
    gate_float = gate_grad.astype(jnp.float32)
    proj_sums = []
    backs = []
    for branch in range(3):
        source = coarse_in[branch]
        shape_now = source.shape
        small_grad = fold_rims(upsample_back(gate_float, scales[branch])).astype(jnp.bfloat16)
        flat = small_grad.reshape(-1, FEAT_ONE)
        proj_sums.append(
            lax.dot_general(
                source.reshape(-1, shape_now[2]),
                flat,
                (((0,), (0,)), ((), ())),
                preferred_element_type=jnp.float32,
            )
        )
        back = lax.dot_general(
            flat, projects[branch], (((1,), (1,)), ((), ())), preferred_element_type=jnp.float32
        )
        backs.append(back.reshape(shape_now))
    grad_four = backs[2].astype(jnp.bfloat16)
    upstream = (gate_float, backs[0], backs[1])
    feat_grads = []
    kern_sums = []
    for branch in range(3):
        grad_pre = gelu_back(pres[branch], upstream[branch]).astype(jnp.bfloat16)
        grad_padded = padded_2(grad_pre, ((ROWS, 0), (COLS, 1)), 1)
        flipped = jnp.transpose(kernels[branch][::-1, ::-1], (0, 1, 3, 2))
        back = conv_taps(grad_padded, flipped)
        feat_grads.append((grad_pre.astype(jnp.float32) + back).astype(jnp.bfloat16))
        kern_sums.append(kernel_grad(padded_in[branch], grad_pre))
    total_cells = (
        maps[0].shape[0] * lax.axis_size(ROWS) * maps[0].shape[1] * lax.axis_size(COLS)
    )
    factors = [(total_cells // 4**branch) ** (-0.5) for branch in range(3)]
    factors = factors + [(total_cells // 4 ** (branch + 1)) ** (-0.5) for branch in range(3)]
    sums = (kern_sums[0], kern_sums[1], kern_sums[2], proj_sums[0], proj_sums[1], proj_sums[2])
    packed = packed_sums([sums[index] * factors[index] for index in range(6)])
    finals = unpacked_sums(summed_over_devices(packed))
    outputs = [grad.reshape(arr.shape) for grad, arr in zip(feat_grads, inputs[:3])]
    return (
        outputs[0],
        outputs[1],
        outputs[2],
        grad_four.reshape(feature_four.shape),
        finals[0],
        finals[1],
        finals[2],
        finals[3],
        finals[4],
        finals[5],
    )


def solution(mesh):
    mesh = Mesh(mesh.devices.reshape(16, 2, 4, 2, 2), ("z", "x_lo", "y", "x_hi", "core"))
    in_specs = (
        P(ROWS, COLS),
        P(ROWS, COLS),
        P(ROWS, COLS),
        P(ROWS, COLS),
        P(),
        P(),
        P(),
        P(),
        P(),
        P(),
        P(ROWS, COLS),
    )
    out_specs = (
        P(ROWS, COLS),
        P(ROWS, COLS),
        P(ROWS, COLS),
        P(ROWS, COLS),
        P(),
        P(),
        P(),
        P(),
        P(),
        P(),
    )
    return jax.shard_map(
        on_device, mesh=mesh, in_specs=in_specs, out_specs=out_specs, check_vma=False
    )
```

```python
import functools

import jax
import jax.numpy as jnp
from jax import lax
from jax.experimental import pallas as pl
from jax.experimental.pallas import tpu as pltpu
from jax.sharding import Mesh
from jax.sharding import PartitionSpec as P

FEAT_ONE = 64
FEAT_TWO = 128
FEAT_THREE = 256
FEAT_FOUR = 512

ROWS = ("z", "x_lo", "y")
COLS = ("x_hi", "core")
PLANE = ("x_lo", "y", "x_hi")
PACK_ROWS = 3328
HALF = PACK_ROWS // 2
WIDE = 5120
RIM = 1024
BF = jnp.bfloat16
F32 = jnp.float32
NT = (((1,), (1,)), ((), ()))
TN = (((0,), (0,)), ((), ()))


def moved(block, axis, distance):
    count = lax.axis_size(axis)
    route = [(i, i + distance) for i in range(count) if 0 <= i + distance < count]
    return lax.ppermute(block, axis, route)


def halos(x1, x2, x3, x4, cot):
    own = jnp.concatenate([x1, cot, x2, x3, x4, jnp.zeros_like(x4)], axis=0)
    last = jnp.concatenate([x2[-1:], x3[-1:], x4], axis=0)
    first = jnp.concatenate([x2[:1], x3[:1], x4], axis=0)
    above = moved(own, ROWS, 1)
    below = moved(own, ROWS, -1)
    above2 = moved(last, ROWS, 2)
    below2 = moved(first, ROWS, -2)
    parts = (own, above, below, above2, below2)
    left = moved(jnp.concatenate([p[:, -RIM:] for p in parts], axis=0), COLS, 1)
    right = moved(jnp.concatenate([p[:, :RIM] for p in parts], axis=0), COLS, -1)
    return own, above, below, above2, below2, left, right


def gelu_both(v):
    c = 0.7978845608028654
    sq = v * v
    t = jnp.tanh(c * v * (1.0 + 0.044715 * sq))
    half = 0.5 * (1.0 + t)
    slope = half + 0.5 * v * (1.0 - t * t) * (c * (1.0 + 3.0 * 0.044715 * sq))
    return v * half, slope


def tile(wide, at):
    return wide[:, 128 * at : 128 * (at + 1)]


def row_weights(shape, coarse_dim, row_block):
    k = lax.broadcasted_iota(jnp.int32, shape, coarse_dim)
    r = lax.broadcasted_iota(jnp.int32, shape, 1 - coarse_dim)
    two, three = k < 16, k < 24
    scale = jnp.where(two, 2, jnp.where(three, 4, 8))
    count = jnp.where(two, 4, jnp.where(three, 2, 1))
    shift = jnp.where(two, 6, jnp.where(three, 16 + 3, 24 + 2))
    total = (jnp.where(two, 512, jnp.where(three, 256, 128)) - 1).astype(F32)
    coarse = (row_block * count + k - shift).astype(F32)
    fine = (row_block * 8 + r - 8).astype(F32)
    inverse = jnp.where(two, 0.5, jnp.where(three, 0.25, 0.125)).astype(F32)
    place = jnp.clip((fine + 0.5) * inverse - 0.5, 0.0, total)
    return jnp.maximum(0.0, 1.0 - jnp.abs(place - coarse))


def forward_kernel(
    place_ref, own, above, below, above2, below2, left, right,
    t1, k2, k3, p2, p3, p4,
    keep_ref, send_ref, g1_ref, g2_ref, g3_ref, gf4_ref,
    wx1, wc, wx2, wx3, wx4, xw1, xw2, xw3, d1, d2, d3, gm1, gm2, gm3, sums,
):
    row_block = place_ref[0]
    at_left = place_ref[1] == 0
    at_right = place_ref[2] == 1
    core = place_ref[3]
    lane = lax.broadcasted_iota(jnp.int32, (1, 128), 1)
    low = lane < 64

    def lanes(a, b):
        return jnp.where(low, a, b).astype(F32)

    wx2[...] = jnp.zeros_like(wx2)
    wx4[...] = jnp.zeros_like(wx4)
    sources = (
        (own, above, below, above2, below2, 0, WIDE, RIM),
        (left, left, left, left, left, None, RIM, 0),
        (right, right, right, right, right, None, RIM, RIM + WIDE),
    )
    for mid, up, down, up2, down2, flat, width, to in sources:
        cols = slice(to, to + width)
        if flat is None:
            whole = mid[...].astype(F32)
            v_mid, v_up, v_down = whole[0:24], whole[24:48], whole[48:72]
            v_up2, v_down2 = whole[72:75], whole[75:78]
        else:
            v_mid, v_up, v_down = (ref[...].astype(F32) for ref in (mid, up, down))
            v_up2, v_down2 = up2[...].astype(F32), down2[...].astype(F32)
        for n, v in enumerate((v_up, v_mid, v_down)):
            wx1[8 * n : 8 * n + 8, cols] = v[0:8]
            wc[8 * n : 8 * n + 8, cols] = v[8:16]
            wx2[2 + 4 * n : 6 + 4 * n, cols] = v[16:20]
            wx3[1 + 2 * n : 3 + 2 * n, cols] = v[20:22]
            wx4[1 + n : 2 + n, cols] = v[22:23]
        wx2[1:2, cols] = v_up2[0:1]
        wx2[14:15, cols] = v_down2[0:1]
        wx3[0:1, cols] = v_up2[1:2]
        wx3[7:8, cols] = v_down2[1:2]
        wx4[0:1, cols] = v_up2[2:3]
        wx4[4:5, cols] = v_down2[2:3]

    for f in range(-3, 43):
        at = 8 + 24 * (f + 3)
        xw1[at : at + 24, 0:128] = tile(wx1, 8 + f)
        xw1[at : at + 24, 128:256] = jnp.where(low, tile(wx1, 9 + f), tile(wx1, 7 + f))
    xw1[0:8, :] = jnp.zeros((8, 256), F32)
    xw1[1112:1120, :] = jnp.zeros((8, 256), F32)
    pre1 = xw1[8:1112, 0:128]
    for i in range(3):
        pre1 = pre1 + jnp.dot(xw1[7 + i : 1111 + i, :].astype(BF), t1[i], preferred_element_type=F32)
    y1, slope = gelu_both(pre1)
    y1 = y1.astype(BF).astype(F32)
    d1[...] = slope

    for j in range(3):
        for c in range(-4, 44):
            at = 8 + 16 * (c + 4)
            xw2[at : at + 16, 128 * j : 128 * j + 128] = tile(wx2, 7 + c + j)
    xw2[0:8, :] = jnp.zeros((8, 384), F32)
    xw2[776:784, :] = jnp.zeros((8, 384), F32)
    pre2 = xw2[8:776, 128:256]
    for i in range(3):
        pre2 = pre2 + jnp.dot(xw2[7 + i : 775 + i, :].astype(BF), k2[i], preferred_element_type=F32)
    y2, slope = gelu_both(pre2)
    y2 = y2.astype(BF)
    d2[...] = slope

    for j in range(3):
        for c in range(-2, 22):
            at = 8 + 8 * (c + 2)
            first = RIM + 256 * (c + j - 1)
            xw3[at : at + 8, 256 * j : 256 * j + 256] = wx3[:, first : first + 256]
    xw3[0:8, :] = jnp.zeros((8, 768), F32)
    xw3[200:208, :] = jnp.zeros((8, 768), F32)
    pre3 = xw3[8:200, 256:512]
    for i in range(3):
        pre3 = pre3 + jnp.dot(xw3[7 + i : 199 + i, :].astype(BF), k3[i], preferred_element_type=F32)
    y3, slope = gelu_both(pre3)
    y3 = y3.astype(BF)
    d3[...] = slope

    x4 = jnp.concatenate([wx4[:, 512 * c : 512 * c + 512] for c in range(14)], axis=0).astype(BF)

    weights = row_weights((24, 32), 1, row_block).astype(BF)
    rows_up = []
    for y, p, rim, rows, wlo in ((y2, p2, 4, 16, 0), (y3, p3, 2, 8, 16), (x4, p4, 2, 8, 24)):
        twice = jnp.concatenate([p[...], p[...]], axis=1)
        coarse = jnp.dot(y, twice, preferred_element_type=F32).astype(BF).astype(F32)
        cols = [coarse[rows * n : rows * (n + 1)] for n in range(coarse.shape[0] // rows)]
        end = len(cols) - rim
        cols[rim - 1] = jnp.where(at_left, cols[rim], cols[rim - 1])
        cols[end] = jnp.where(at_right, cols[end - 1], cols[end])
        flat = jnp.concatenate(cols, axis=1).astype(BF)
        rows_up.append(jnp.dot(weights[:, wlo : wlo + rows], flat, preferred_element_type=F32))
    up2, up3, up4 = rows_up

    gates = []
    for f in range(-3, 43):
        k = f + 4
        merged = y1[24 * (f + 3) : 24 * (f + 4)]
        merged = merged + 0.75 * tile(up2, k) + 0.25 * jnp.where(low, tile(up2, k - 1), tile(up2, k + 1))
        k, h = f // 2 + 2, f % 2
        if h == 0:
            merged = merged + lanes(0.375, 0.125) * tile(up3, k - 1) + lanes(0.625, 0.875) * tile(up3, k)
        else:
            merged = merged + lanes(0.875, 0.625) * tile(up3, k) + lanes(0.125, 0.375) * tile(up3, k + 1)
        k, h = f // 4 + 2, f % 4
        p_low, p_high = (2 * h + 0.5) / 8 - 0.5, (2 * h + 1.5) / 8 - 0.5
        other = k - 1 if h < 2 else k + 1
        merged = merged + lanes(1 - abs(p_low), 1 - abs(p_high)) * tile(up4, k)
        merged = merged + lanes(abs(p_low), abs(p_high)) * tile(up4, other)
        slope = gelu_both(merged)[1]
        gate = (slope * tile(wc, 8 + f)).astype(BF).astype(F32)
        gates.append(gate)
        if -1 <= f <= 40:
            g = (d1[24 * (f + 3) : 24 * (f + 4)] * gate).astype(BF).astype(F32)
            g1_ref[24 * (f + 1) : 24 * (f + 2), :] = g
            if 0 <= f < 40:
                row = lax.broadcasted_iota(jnp.int32, (24, 1), 0)
                gm1[8 + 24 * f : 32 + 24 * f, :] = jnp.where((row >= 8) & (row < 16), g, 0.0)
    gm1[0:8, :] = jnp.zeros((8, 128), F32)
    gm1[968:976, :] = jnp.zeros((8, 128), F32)

    flat = jnp.concatenate(gates, axis=1).astype(BF)
    weights_back = row_weights((32, 24), 0, row_block).astype(BF)
    down = jnp.dot(weights_back, flat, preferred_element_type=F32)
    down2, down3, down4 = down[0:16], down[16:24], down[24:32]

    def folded(v):
        return v + pltpu.roll(v, 64, 1)

    cg2 = []
    for c in range(-1, 41):
        v = 0.75 * tile(down2, c + 3) + 0.25 * jnp.where(low, tile(down2, c + 4), tile(down2, c + 2))
        cg2.append(folded(v))
    cg3 = []
    for c in range(-1, 21):
        at = 2 * c + 2
        v = lanes(0.125, 0.375) * tile(down3, at) + lanes(0.625, 0.875) * tile(down3, at + 1)
        v = v + lanes(0.875, 0.625) * tile(down3, at + 2) + lanes(0.375, 0.125) * tile(down3, at + 3)
        cg3.append(folded(v))
    cg4 = []
    for c in range(10):
        v = jnp.zeros((8, 128), F32)
        for n in range(8):
            a, b = (2 * n + 0.5) / 8, (2 * n + 1.5) / 8
            a, b = (a, b) if n < 4 else (2 - a, 2 - b)
            v = v + lanes(a, b) * tile(down4, 4 * c + 1 + n)
        if c == 0:
            rim = lanes(0.4375, 0.3125) * tile(down4, 3) + lanes(0.1875, 0.0625) * tile(down4, 4)
            v = v + jnp.where(at_left, rim, 0.0)
        if c == 9:
            rim = lanes(0.0625, 0.1875) * tile(down4, 41) + lanes(0.3125, 0.4375) * tile(down4, 42)
            v = v + jnp.where(at_right, rim, 0.0)
        cg4.append(folded(v))
    for cg in (cg2, cg3):
        cg[1] = cg[1] + jnp.where(at_left, cg[0], 0.0)
        cg[-2] = cg[-2] + jnp.where(at_right, cg[-1], 0.0)
        cg[0] = jnp.where(at_left, 0.0, cg[0])
        cg[-1] = jnp.where(at_right, 0.0, cg[-1])

    flat2 = jnp.concatenate(cg2, axis=0).astype(BF).astype(F32)
    flat3 = jnp.concatenate(cg3, axis=0).astype(BF).astype(F32)
    flat4 = jnp.concatenate(cg4, axis=0).astype(BF).astype(F32)
    back2 = lax.dot_general(flat2[:, 0:64].astype(BF), p2[...], NT, preferred_element_type=F32)
    back3 = lax.dot_general(flat3[:, 0:64].astype(BF), p3[...], NT, preferred_element_type=F32)
    back4 = lax.dot_general(flat4[:, 0:64].astype(BF), p4[...], NT, preferred_element_type=F32)
    for c in range(10):
        gf4_ref[0:1, 512 * c : 512 * c + 512] = back4[8 * c + 2 : 8 * c + 3].astype(BF)
    g2 = (d2[48:720, :] * back2).astype(BF).astype(F32)
    g3 = (d3[8:184, :] * back3).astype(BF).astype(F32)
    g2_ref[...] = g2
    g3_ref[...] = g3

    row2 = lax.broadcasted_iota(jnp.int32, (640, 1), 0) % 16
    own2 = (row2 >= 6) & (row2 < 10)
    row3 = lax.broadcasted_iota(jnp.int32, (160, 1), 0) % 8
    own3 = (row3 >= 3) & (row3 < 5)
    row4 = lax.broadcasted_iota(jnp.int32, (80, 1), 0) % 8
    gm2[0:8, :] = jnp.zeros((8, 128), F32)
    gm2[8:648, :] = jnp.where(own2, g2[16:656], 0.0)
    gm2[648:656, :] = jnp.zeros((8, 128), F32)
    gm3[0:8, :] = jnp.zeros((8, 256), F32)
    gm3[8:168, :] = jnp.where(own3, g3[8:168], 0.0)
    gm3[168:176, :] = jnp.zeros((8, 256), F32)

    cells = 327680
    x = xw3[24:184, :].astype(BF)
    shifted = jnp.concatenate([gm3[9 - i : 169 - i, :] for i in range(3)], axis=1).astype(BF)
    z = lax.dot_general(x, shifted, TN, preferred_element_type=F32) * (cells // 16) ** -0.5
    for i in range(3):
        sums[768 * i : 768 * (i + 1), :] = z[:, 256 * i : 256 * (i + 1)]
    x = xw2[72:712, :].astype(BF)
    shifted = jnp.concatenate([gm2[9 - i : 649 - i, :] for i in range(3)], axis=1).astype(BF)
    z = lax.dot_general(x, shifted, TN, preferred_element_type=F32) * (cells // 4) ** -0.5
    base = 2304
    sums[base : base + 384, 0:128] = z[:, 0:128]
    sums[base + 384 : base + 576, 0:128] = z[0:192, 128:256]
    sums[base : base + 192, 128:256] = z[192:384, 128:256]
    sums[base + 192 : base + 576, 128:256] = z[:, 256:384]
    x = xw1[80:1040, :].astype(BF)
    shifted = jnp.concatenate([gm1[9 - i : 969 - i, :] for i in range(3)], axis=1).astype(BF)
    z = lax.dot_general(x, shifted, TN, preferred_element_type=F32) * cells**-0.5
    window = (192, 0, 64, 128)
    blocks = []
    for i in range(3):
        zi = z[:, 128 * i : 128 * (i + 1)]
        for j in range(3):
            a, b = window[j], window[j + 1]
            blocks.append(zi[a : a + 64] + pltpu.roll(zi[b : b + 64], 64, 1))
    y2_own, y3_own, x4_own = y2[64:704], y3[16:176], x4[16:96]
    for y, flat, mask, branch in (
        (y2_own, flat2[16:656], own2, 1),
        (y3_own, flat3[8:168], own3, 2),
        (x4_own, flat4, row4 == 2, 3),
    ):
        masked = jnp.where(mask, flat, 0.0).astype(BF)
        z = lax.dot_general(y, masked, TN, preferred_element_type=F32) * (cells // 4**branch) ** -0.5
        blocks += [z[64 * n : 64 * (n + 1)] for n in range(z.shape[0] // 64)]
    blocks.append(jnp.zeros((64, 128), F32))
    base = 2880
    for n in range(6):
        for side in range(2):
            a, b = blocks[4 * n + 2 * side], blocks[4 * n + 2 * side + 1]
            if 4 * n + 2 * side + 1 < 9:
                b = pltpu.roll(b, 64, 1)
            at = base + 64 * n
            sums[at : at + 64, 128 * side : 128 * side + 128] = jnp.where(low, a, b)
    sums[3264:3328, :] = jnp.zeros((64, 256), F32)
    keep_ref[...] = sums[pl.ds(pl.multiple_of(core * HALF, 64), HALF), :]
    send_ref[...] = sums[pl.ds(pl.multiple_of((1 - core) * HALF, 64), HALF), :].astype(BF)


def backward_kernel(g1, g2, g3, t1b, k2, k3, gf1_ref, gf2_ref, gf3_ref, xw1, xw2, xw3, out2, out3):
    low = lax.broadcasted_iota(jnp.int32, (1, 128), 1) < 64
    for ref, n in ((xw1, 960), (xw2, 640), (xw3, 160)):
        ref[0:8, :] = jnp.zeros((8, ref.shape[1]), F32)
        ref[8 + n : 16 + n, :] = jnp.zeros((8, ref.shape[1]), F32)

    xw1[8:968, 0:128] = g1[24:984, :]
    xw1[8:968, 128:256] = jnp.where(low, g1[48:1008, :], g1[0:960, :])
    total = xw1[8:968, 0:128]
    for i in range(3):
        total = total + lax.dot_general(
            xw1[9 - i : 969 - i, :].astype(BF), t1b[i], NT, preferred_element_type=F32
        )
    for f in range(40):
        gf1_ref[:, 128 * f : 128 * (f + 1)] = total[24 * f + 8 : 24 * f + 16].astype(BF)

    for j in range(3):
        xw2[8:648, 128 * j : 128 * j + 128] = g2[32 - 16 * j : 672 - 16 * j, :]
    total = xw2[8:648, 128:256]
    for i in range(3):
        kernel = jnp.concatenate([k2[i, 128 * j : 128 * j + 128, :] for j in range(3)], axis=1)
        total = total + lax.dot_general(
            xw2[9 - i : 649 - i, :].astype(BF), kernel, NT, preferred_element_type=F32
        )
    out2[...] = total
    for c in range(40):
        gf2_ref[:, 128 * c : 128 * (c + 1)] = out2[16 * c + 6 : 16 * c + 10, :].astype(BF)

    for j in range(3):
        xw3[8:168, 256 * j : 256 * j + 256] = g3[16 - 8 * j : 176 - 8 * j, :]
    total = xw3[8:168, 256:512]
    for i in range(3):
        kernel = jnp.concatenate([k3[i, 256 * j : 256 * j + 256, :] for j in range(3)], axis=1)
        total = total + lax.dot_general(
            xw3[9 - i : 169 - i, :].astype(BF), kernel, NT, preferred_element_type=F32
        )
    out3[...] = total
    for c in range(20):
        gf3_ref[:, 256 * c : 256 * (c + 1)] = out3[8 * c + 3 : 8 * c + 5, :].astype(BF)


def swapped(block, axis, flip):
    return lax.ppermute(block, axis, [(i, i ^ flip) for i in range(lax.axis_size(axis))])


def kept_half(values, axis, flip, dim):
    bit = (lax.axis_index(axis) // flip) % 2
    half = values.shape[dim] // 2
    keep = lax.dynamic_slice_in_dim(values, bit * half, half, axis=dim)
    send = lax.dynamic_slice_in_dim(values, (1 - bit) * half, half, axis=dim)
    got = swapped(send.astype(BF), axis, flip)
    return keep + got.astype(F32)


def both_halves(values, axis, flip, dim):
    bit = (lax.axis_index(axis) // flip) % 2
    got = swapped(values, axis, flip)
    first = jnp.where(bit == 0, values, got)
    second = jnp.where(bit == 0, got, values)
    return jnp.concatenate([first, second], axis=dim)


def summed_over_devices(keep, send):
    width = keep.shape[1]
    part = keep + swapped(send, "core", 1).astype(F32)
    pieces = part.astype(BF).reshape(16, -1, width)
    pieces = lax.all_to_all(pieces, PLANE, 0, 0)
    part = jnp.sum(pieces.astype(F32), axis=0)
    part = kept_half(part, "z", 1, 1)
    part = kept_half(part, "z", 2, 0)
    for flip in (4, 8):
        part = part.astype(BF)
        part = part.astype(F32) + swapped(part, "z", flip).astype(F32)
    part = part.astype(BF)
    part = both_halves(part, "z", 2, 0)
    part = both_halves(part, "z", 1, 1)
    pieces = jnp.broadcast_to(part[None], (16,) + part.shape)
    part = lax.all_to_all(pieces, PLANE, 0, 0).reshape(-1, width)
    return part, swapped(part, "core", 1)


def unpack_kernel(place_ref, mine, got, k1_ref, k2_ref, k3_ref, p2_ref, p3_ref, p4_ref, whole):
    core = place_ref[3]
    whole[pl.ds(pl.multiple_of(core * HALF, 64), HALF), :] = mine[...]
    whole[pl.ds(pl.multiple_of((1 - core) * HALF, 64), HALF), :] = got[...]
    k3_ref[...] = whole[0:2304, :]
    k2_ref[0:576, :] = whole[2304:2880, 0:128]
    k2_ref[576:1152, :] = whole[2304:2880, 128:256]
    block = 0
    for ref, count in ((k1_ref, 9), (p2_ref, 2), (p3_ref, 4), (p4_ref, 8)):
        for n in range(count):
            at, side = 2880 + 64 * (block // 4), 64 * (block % 4)
            ref[64 * n : 64 * (n + 1), :] = whole[at : at + 64, side : side + 64]
            block += 1


def call(kernel, out_shapes, scratch, count, scalars=0):
    vmem = pl.BlockSpec(memory_space=pltpu.VMEM)
    smem = pl.BlockSpec(memory_space=pltpu.SMEM)
    return pl.pallas_call(
        kernel,
        out_shape=[jax.ShapeDtypeStruct(shape, dtype) for shape, dtype in out_shapes],
        in_specs=[smem] * scalars + [vmem] * count,
        out_specs=[vmem] * len(out_shapes),
        scratch_shapes=[pltpu.VMEM(shape, dtype) for shape, dtype in scratch],
        compiler_params=pltpu.CompilerParams(vmem_limit_bytes=48 * 1024 * 1024),
    )


def pair_weights(kernel_one):
    none = jnp.zeros((3, FEAT_ONE, FEAT_ONE), BF)
    tap = lambda j: kernel_one[:, j] if 0 <= j < 3 else none
    windows = (1, 2, 3, 0)
    ahead = jnp.concatenate(
        [jnp.concatenate([tap(w - e) for w in windows], axis=1) for e in range(2)], axis=2
    )
    back = jnp.concatenate(
        [jnp.concatenate([tap(e - w + 2) for e in range(2)], axis=1) for w in windows], axis=2
    )
    return ahead, back


def local_part(x1, x2, x3, x4, kernel_one, kernel_two, kernel_three, p2, p3, p4, cot):
    place = jnp.stack(
        [
            lax.axis_index(ROWS),
            lax.axis_index(COLS),
            (lax.axis_index(COLS) == lax.axis_size(COLS) - 1).astype(jnp.int32),
            lax.axis_index("core"),
        ]
    ).astype(jnp.int32)
    ahead, back = pair_weights(kernel_one)
    k2 = kernel_two.reshape(3, 384, 128)
    k3 = kernel_three.reshape(3, 768, 256)
    packs = halos(x1, x2, x3, x4, cot)
    total = RIM + WIDE + RIM
    keep, send, g1, g2, g3, gf4 = call(
        forward_kernel,
        [
            ((HALF, 256), F32), ((HALF, 256), BF),
            ((1008, 128), F32), ((672, 128), F32), ((176, 256), F32), ((1, WIDE), BF),
        ],
        [
            ((24, total), F32), ((24, total), F32), ((16, total), F32), ((8, total), F32), ((8, total), F32),
            ((1120, 256), F32), ((784, 384), F32), ((208, 768), F32),
            ((1104, 128), F32), ((768, 128), F32), ((192, 256), F32),
            ((976, 128), F32), ((656, 128), F32), ((176, 256), F32),
            ((PACK_ROWS, 256), F32),
        ],
        13,
        1,
    )(place, *packs, ahead, k2, k3, p2, p3, p4)
    gf1, gf2, gf3 = call(
        backward_kernel,
        [((8, WIDE), BF), ((4, WIDE), BF), ((2, WIDE), BF)],
        [
            ((976, 256), F32), ((656, 384), F32), ((176, 768), F32),
            ((640, 128), F32), ((160, 256), F32),
        ],
        6,
    )(g1, g2, g3, back, k2, k3)
    return place, keep, send, gf1, gf2, gf3, gf4


def unpacked(place, mine, got):
    outs = call(
        unpack_kernel,
        [((576, 64), BF), ((1152, 128), BF), ((2304, 256), BF), ((128, 64), BF), ((256, 64), BF), ((512, 64), BF)],
        [((PACK_ROWS, 256), BF)],
        2,
        1,
    )(place, mine, got)
    return (
        outs[0].reshape(3, 3, 64, 64), outs[1].reshape(3, 3, 128, 128), outs[2].reshape(3, 3, 256, 256),
        outs[3], outs[4], outs[5],
    )


def on_device(*args):
    place, keep, send, gf1, gf2, gf3, gf4 = local_part(*args)
    mine, got = summed_over_devices(keep, send)
    return (gf1, gf2, gf3, gf4) + unpacked(place, mine, got)


def solution(mesh):
    mesh = Mesh(mesh.devices.reshape(16, 2, 4, 2, 2), ("z", "x_lo", "y", "x_hi", "core"))
    split = P(ROWS, COLS)
    in_specs = (split,) * 4 + (P(),) * 6 + (split,)
    out_specs = (split,) * 4 + (P(),) * 6
    return jax.shard_map(on_device, mesh=mesh, in_specs=in_specs, out_specs=out_specs, check_vma=False)
```

```python
import functools

import jax
import jax.numpy as jnp
from jax import lax
from jax.experimental import pallas as pl
from jax.experimental.pallas import tpu as pltpu
from jax.sharding import Mesh
from jax.sharding import PartitionSpec as P

FEAT_ONE = 64
FEAT_TWO = 128
FEAT_THREE = 256
FEAT_FOUR = 512

ROWS = ("z", "x_lo", "y")
COLS = ("x_hi", "core")
PLANE = ("x_lo", "y", "x_hi")
PACK_ROWS = 3328
HALF = PACK_ROWS // 2
WIDE = 5120
RIM = 1024
BF = jnp.bfloat16
F32 = jnp.float32
NT = (((1,), (1,)), ((), ()))
TN = (((0,), (0,)), ((), ()))


def moved(block, axis, distance):
    count = lax.axis_size(axis)
    route = [(i, i + distance) for i in range(count) if 0 <= i + distance < count]
    return lax.ppermute(block, axis, route)


def stacked(parts, rows):
    total, at = None, 0
    for part in parts:
        padded = jnp.pad(part, ((at, rows - at - part.shape[0]), (0, 0)))
        total = padded if total is None else total + padded
        at += part.shape[0]
    return total


def halos(x1, x2, x3, x4, cot):
    own = stacked((x1, cot, x2, x3, x4), 24)
    last = jnp.concatenate([x2[-1:], x3[-1:], x4], axis=0)
    first = jnp.concatenate([x2[:1], x3[:1], x4], axis=0)
    above = moved(own, ROWS, 1)
    below = moved(own, ROWS, -1)
    above2 = moved(last, ROWS, 2)
    below2 = moved(first, ROWS, -2)
    parts = (own, above, below, above2, below2)
    left = moved(jnp.concatenate([p[:, -RIM:] for p in parts], axis=0), COLS, 1)
    right = moved(jnp.concatenate([p[:, :RIM] for p in parts], axis=0), COLS, -1)
    return own, above, below, above2, below2, left, right


def gelu_both(v):
    c = 0.7978845608028654
    sq = v * v
    t = jnp.tanh(c * v * (1.0 + 0.044715 * sq))
    half = 0.5 * (1.0 + t)
    slope = half + 0.5 * v * (1.0 - t * t) * (c * (1.0 + 3.0 * 0.044715 * sq))
    return v * half, slope


def tile(wide, at):
    return wide[:, 128 * at : 128 * (at + 1)]


def row_weights(shape, coarse_dim, row_block):
    k = lax.broadcasted_iota(jnp.int32, shape, coarse_dim)
    r = lax.broadcasted_iota(jnp.int32, shape, 1 - coarse_dim)
    two, three = k < 16, k < 24
    scale = jnp.where(two, 2, jnp.where(three, 4, 8))
    count = jnp.where(two, 4, jnp.where(three, 2, 1))
    shift = jnp.where(two, 6, jnp.where(three, 16 + 3, 24 + 2))
    total = (jnp.where(two, 512, jnp.where(three, 256, 128)) - 1).astype(F32)
    coarse = (row_block * count + k - shift).astype(F32)
    fine = (row_block * 8 + r - 8).astype(F32)
    inverse = jnp.where(two, 0.5, jnp.where(three, 0.25, 0.125)).astype(F32)
    place = jnp.clip((fine + 0.5) * inverse - 0.5, 0.0, total)
    return jnp.maximum(0.0, 1.0 - jnp.abs(place - coarse))


def forward_kernel(
    place_ref, p2, p3, p4, *refs
):
    far, refs = refs[:10], refs[10:]
    keep_ref, send_ref, g1_ref, g2_ref, g3_ref, gf4_ref = refs[:6]
    wx1, wc, wx2, wx3, wx4, xw1, xw2, xw3, d1, d2, d3, gm1, gm2, gm3, sums = refs[6:21]
    near, sems = refs[21:31], refs[31]
    copies = [pltpu.make_async_copy(far[n], near[n], sems.at[n]) for n in range(10)]
    for copy in copies:
        copy.start()
    own, above, below, above2, below2, left, right, t1, k2, k3 = near
    row_block = place_ref[0]
    at_left = place_ref[1] == 0
    at_right = place_ref[2] == 1
    core = place_ref[3]
    lane = lax.broadcasted_iota(jnp.int32, (1, 128), 1)
    low = lane < 64

    def lanes(a, b):
        return jnp.where(low, a, b).astype(F32)

    wx2[...] = jnp.zeros_like(wx2)
    wx4[...] = jnp.zeros_like(wx4)
    for copy in copies[:8]:
        copy.wait()
    sources = (
        (own, above, below, above2, below2, 0, WIDE, RIM),
        (left, left, left, left, left, None, RIM, 0),
        (right, right, right, right, right, None, RIM, RIM + WIDE),
    )
    for mid, up, down, up2, down2, flat, width, to in sources:
        cols = slice(to, to + width)
        if flat is None:
            whole = mid[...].astype(F32)
            v_mid, v_up, v_down = whole[0:24], whole[24:48], whole[48:72]
            v_up2, v_down2 = whole[72:75], whole[75:78]
        else:
            v_mid, v_up, v_down = (ref[...].astype(F32) for ref in (mid, up, down))
            v_up2, v_down2 = up2[...].astype(F32), down2[...].astype(F32)
        for n, v in enumerate((v_up, v_mid, v_down)):
            wx1[8 * n : 8 * n + 8, cols] = v[0:8]
            wc[8 * n : 8 * n + 8, cols] = v[8:16]
            wx2[2 + 4 * n : 6 + 4 * n, cols] = v[16:20]
            wx3[1 + 2 * n : 3 + 2 * n, cols] = v[20:22]
            wx4[1 + n : 2 + n, cols] = v[22:23]
        wx2[1:2, cols] = v_up2[0:1]
        wx2[14:15, cols] = v_down2[0:1]
        wx3[0:1, cols] = v_up2[1:2]
        wx3[7:8, cols] = v_down2[1:2]
        wx4[0:1, cols] = v_up2[2:3]
        wx4[4:5, cols] = v_down2[2:3]

    for f in range(-3, 43):
        at = 8 + 24 * (f + 3)
        xw1[at : at + 24, 0:128] = tile(wx1, 8 + f)
        xw1[at : at + 24, 128:256] = jnp.where(low, tile(wx1, 9 + f), tile(wx1, 7 + f))
    xw1[0:8, :] = jnp.zeros((8, 256), F32)
    xw1[1112:1120, :] = jnp.zeros((8, 256), F32)
    pre1 = xw1[8:1112, 0:128]
    for i in range(3):
        pre1 = pre1 + jnp.dot(xw1[7 + i : 1111 + i, :].astype(BF), t1[i], preferred_element_type=F32)
    y1, slope = gelu_both(pre1)
    y1 = y1.astype(BF).astype(F32)
    d1[...] = slope

    copies[8].wait()
    for j in range(3):
        for c in range(-4, 44):
            at = 8 + 16 * (c + 4)
            xw2[at : at + 16, 128 * j : 128 * j + 128] = tile(wx2, 7 + c + j)
    xw2[0:8, :] = jnp.zeros((8, 384), F32)
    xw2[776:784, :] = jnp.zeros((8, 384), F32)
    pre2 = xw2[8:776, 128:256]
    for i in range(3):
        pre2 = pre2 + jnp.dot(xw2[7 + i : 775 + i, :].astype(BF), k2[i], preferred_element_type=F32)
    y2, slope = gelu_both(pre2)
    y2 = y2.astype(BF)
    d2[...] = slope

    copies[9].wait()
    for j in range(3):
        for c in range(-2, 22):
            at = 8 + 8 * (c + 2)
            first = RIM + 256 * (c + j - 1)
            xw3[at : at + 8, 256 * j : 256 * j + 256] = wx3[:, first : first + 256]
    xw3[0:8, :] = jnp.zeros((8, 768), F32)
    xw3[200:208, :] = jnp.zeros((8, 768), F32)
    pre3 = xw3[8:200, 256:512]
    for i in range(3):
        pre3 = pre3 + jnp.dot(xw3[7 + i : 199 + i, :].astype(BF), k3[i], preferred_element_type=F32)
    y3, slope = gelu_both(pre3)
    y3 = y3.astype(BF)
    d3[...] = slope

    x4 = jnp.concatenate([wx4[:, 512 * c : 512 * c + 512] for c in range(14)], axis=0).astype(BF)

    weights = row_weights((24, 32), 1, row_block).astype(BF)
    rows_up = []
    for y, p, rim, rows, wlo in ((y2, p2, 4, 16, 0), (y3, p3, 2, 8, 16), (x4, p4, 2, 8, 24)):
        twice = jnp.concatenate([p[...], p[...]], axis=0)
        coarse = lax.dot_general(y, twice, NT, preferred_element_type=F32).astype(BF).astype(F32)
        cols = [coarse[rows * n : rows * (n + 1)] for n in range(coarse.shape[0] // rows)]
        end = len(cols) - rim
        cols[rim - 1] = jnp.where(at_left, cols[rim], cols[rim - 1])
        cols[end] = jnp.where(at_right, cols[end - 1], cols[end])
        flat = jnp.concatenate(cols, axis=1).astype(BF)
        rows_up.append(jnp.dot(weights[:, wlo : wlo + rows], flat, preferred_element_type=F32))
    up2, up3, up4 = rows_up

    gates, g1 = [], []
    for f in range(-3, 43):
        k = f + 4
        merged = y1[24 * (f + 3) : 24 * (f + 4)]
        merged = merged + 0.75 * tile(up2, k) + 0.25 * jnp.where(low, tile(up2, k - 1), tile(up2, k + 1))
        k, h = f // 2 + 2, f % 2
        if h == 0:
            merged = merged + lanes(0.375, 0.125) * tile(up3, k - 1) + lanes(0.625, 0.875) * tile(up3, k)
        else:
            merged = merged + lanes(0.875, 0.625) * tile(up3, k) + lanes(0.125, 0.375) * tile(up3, k + 1)
        k, h = f // 4 + 2, f % 4
        p_low, p_high = (2 * h + 0.5) / 8 - 0.5, (2 * h + 1.5) / 8 - 0.5
        other = k - 1 if h < 2 else k + 1
        merged = merged + lanes(1 - abs(p_low), 1 - abs(p_high)) * tile(up4, k)
        merged = merged + lanes(abs(p_low), abs(p_high)) * tile(up4, other)
        slope = gelu_both(merged)[1]
        gate = (slope * tile(wc, 8 + f)).astype(BF).astype(F32)
        gates.append(gate)
        if -1 <= f <= 40:
            g = (d1[24 * (f + 3) : 24 * (f + 4)] * gate).astype(BF).astype(F32)
            g1.append(g)
            if 0 <= f < 40:
                row = lax.broadcasted_iota(jnp.int32, (24, 1), 0)
                gm1[8 + 24 * f : 32 + 24 * f, :] = jnp.where((row >= 8) & (row < 16), g, 0.0)
    g1_ref[...] = jnp.concatenate(g1, axis=0).astype(BF)
    gm1[0:8, :] = jnp.zeros((8, 128), F32)
    gm1[968:976, :] = jnp.zeros((8, 128), F32)

    flat = jnp.concatenate(gates, axis=1).astype(BF)
    weights_back = row_weights((32, 24), 0, row_block).astype(BF)
    down = jnp.dot(weights_back, flat, preferred_element_type=F32)
    down2, down3, down4 = down[0:16], down[16:24], down[24:32]

    def folded(v):
        return v + pltpu.roll(v, 64, 1)

    cg2 = []
    for c in range(-1, 41):
        v = 0.75 * tile(down2, c + 3) + 0.25 * jnp.where(low, tile(down2, c + 4), tile(down2, c + 2))
        cg2.append(folded(v))
    cg3 = []
    for c in range(-1, 21):
        at = 2 * c + 2
        v = lanes(0.125, 0.375) * tile(down3, at) + lanes(0.625, 0.875) * tile(down3, at + 1)
        v = v + lanes(0.875, 0.625) * tile(down3, at + 2) + lanes(0.375, 0.125) * tile(down3, at + 3)
        cg3.append(folded(v))
    cg4 = []
    for c in range(10):
        v = jnp.zeros((8, 128), F32)
        for n in range(8):
            a, b = (2 * n + 0.5) / 8, (2 * n + 1.5) / 8
            a, b = (a, b) if n < 4 else (2 - a, 2 - b)
            v = v + lanes(a, b) * tile(down4, 4 * c + 1 + n)
        if c == 0:
            rim = lanes(0.4375, 0.3125) * tile(down4, 3) + lanes(0.1875, 0.0625) * tile(down4, 4)
            v = v + jnp.where(at_left, rim, 0.0)
        if c == 9:
            rim = lanes(0.0625, 0.1875) * tile(down4, 41) + lanes(0.3125, 0.4375) * tile(down4, 42)
            v = v + jnp.where(at_right, rim, 0.0)
        cg4.append(folded(v))
    for cg in (cg2, cg3):
        cg[1] = cg[1] + jnp.where(at_left, cg[0], 0.0)
        cg[-2] = cg[-2] + jnp.where(at_right, cg[-1], 0.0)
        cg[0] = jnp.where(at_left, 0.0, cg[0])
        cg[-1] = jnp.where(at_right, 0.0, cg[-1])

    flat2 = jnp.concatenate(cg2, axis=0).astype(BF).astype(F32)
    flat3 = jnp.concatenate(cg3, axis=0).astype(BF).astype(F32)
    flat4 = jnp.concatenate(cg4, axis=0).astype(BF).astype(F32)
    back2 = jnp.dot(flat2[:, 0:64].astype(BF), p2[...], preferred_element_type=F32)
    back3 = jnp.dot(flat3[:, 0:64].astype(BF), p3[...], preferred_element_type=F32)
    back4 = jnp.dot(flat4[:, 0:64].astype(BF), p4[...], preferred_element_type=F32)
    for c in range(10):
        gf4_ref[0:1, 512 * c : 512 * c + 512] = back4[8 * c + 2 : 8 * c + 3].astype(BF)
    g2 = (d2[48:720, :] * back2).astype(BF).astype(F32)
    g3 = (d3[8:184, :] * back3).astype(BF).astype(F32)
    g2_ref[...] = g2.astype(BF)
    g3_ref[...] = g3.astype(BF)

    row2 = lax.broadcasted_iota(jnp.int32, (640, 1), 0) % 16
    own2 = (row2 >= 6) & (row2 < 10)
    row3 = lax.broadcasted_iota(jnp.int32, (160, 1), 0) % 8
    own3 = (row3 >= 3) & (row3 < 5)
    row4 = lax.broadcasted_iota(jnp.int32, (80, 1), 0) % 8
    gm2[0:8, :] = jnp.zeros((8, 128), F32)
    gm2[8:648, :] = jnp.where(own2, g2[16:656], 0.0)
    gm2[648:656, :] = jnp.zeros((8, 128), F32)
    gm3[0:8, :] = jnp.zeros((8, 256), F32)
    gm3[8:168, :] = jnp.where(own3, g3[8:168], 0.0)
    gm3[168:176, :] = jnp.zeros((8, 256), F32)

    cells = 327680
    x = xw3[24:184, :].astype(BF)
    shifted = jnp.concatenate([gm3[9 - i : 169 - i, :] for i in range(3)], axis=1).astype(BF)
    z = lax.dot_general(x, shifted, TN, preferred_element_type=F32) * (cells // 16) ** -0.5
    for i in range(3):
        sums[768 * i : 768 * (i + 1), :] = z[:, 256 * i : 256 * (i + 1)]
    x = xw2[72:712, :].astype(BF)
    shifted = jnp.concatenate([gm2[9 - i : 649 - i, :] for i in range(3)], axis=1).astype(BF)
    z = lax.dot_general(x, shifted, TN, preferred_element_type=F32) * (cells // 4) ** -0.5
    base = 2304
    sums[base : base + 384, 0:128] = z[:, 0:128]
    sums[base + 384 : base + 576, 0:128] = z[0:192, 128:256]
    sums[base : base + 192, 128:256] = z[192:384, 128:256]
    sums[base + 192 : base + 576, 128:256] = z[:, 256:384]
    x = xw1[80:1040, :].astype(BF)
    shifted = jnp.concatenate([gm1[9 - i : 969 - i, :] for i in range(3)], axis=1).astype(BF)
    z = lax.dot_general(x, shifted, TN, preferred_element_type=F32) * cells**-0.5
    window = (192, 0, 64, 128)
    blocks = []
    for i in range(3):
        zi = z[:, 128 * i : 128 * (i + 1)]
        for j in range(3):
            a, b = window[j], window[j + 1]
            blocks.append(zi[a : a + 64] + pltpu.roll(zi[b : b + 64], 64, 1))
    blocks.append(jnp.zeros((64, 128), F32))
    pairs = [jnp.where(low, blocks[n], pltpu.roll(blocks[n + 1], 64, 1)) for n in range(0, 10, 2)]
    y2_own, y3_own, x4_own = y2[64:704], y3[16:176], x4[16:96]
    for y, flat, mask, branch in (
        (y2_own, flat2[16:656], own2, 1),
        (y3_own, flat3[8:168], own3, 2),
        (x4_own, flat4, row4 == 2, 3),
    ):
        masked = jnp.where(mask, flat, 0.0).astype(BF)
        z = lax.dot_general(masked, y, TN, preferred_element_type=F32) * (cells // 4**branch) ** -0.5
        pairs += [z[0:64, 128 * n : 128 * (n + 1)] for n in range(z.shape[1] // 128)]
    base = 2880
    for n in range(12):
        at, side = base + 64 * (n // 2), 128 * (n % 2)
        sums[at : at + 64, side : side + 128] = pairs[n]
    sums[3264:3328, :] = jnp.zeros((64, 256), F32)
    keep_ref[...] = sums[pl.ds(pl.multiple_of(core * HALF, 64), HALF), :].astype(BF)
    send_ref[...] = sums[pl.ds(pl.multiple_of((1 - core) * HALF, 64), HALF), :].astype(BF)


def backward_kernel(g1_ref, g2_ref, g3_ref, t1b, k2, k3, gf1_ref, gf2_ref, gf3_ref, xw1, xw2, xw3, out2, out3):
    low = lax.broadcasted_iota(jnp.int32, (1, 128), 1) < 64
    for ref, n in ((xw1, 960), (xw2, 640), (xw3, 160)):
        ref[0:8, :] = jnp.zeros((8, ref.shape[1]), F32)
        ref[8 + n : 16 + n, :] = jnp.zeros((8, ref.shape[1]), F32)

    g1, g2, g3 = (ref[...].astype(F32) for ref in (g1_ref, g2_ref, g3_ref))
    xw1[8:968, 0:128] = g1[24:984, :]
    xw1[8:968, 128:256] = jnp.where(low, g1[48:1008, :], g1[0:960, :])
    total = xw1[8:968, 0:128]
    for i in range(3):
        total = total + lax.dot_general(
            xw1[9 - i : 969 - i, :].astype(BF), t1b[i], NT, preferred_element_type=F32
        )
    for f in range(40):
        gf1_ref[:, 128 * f : 128 * (f + 1)] = total[24 * f + 8 : 24 * f + 16].astype(BF)

    for j in range(3):
        xw2[8:648, 128 * j : 128 * j + 128] = g2[32 - 16 * j : 672 - 16 * j, :]
    total = xw2[8:648, 128:256]
    for i in range(3):
        kernel = jnp.concatenate([k2[i, 128 * j : 128 * j + 128, :] for j in range(3)], axis=1)
        total = total + lax.dot_general(
            xw2[9 - i : 649 - i, :].astype(BF), kernel, NT, preferred_element_type=F32
        )
    out2[...] = total
    for c in range(40):
        gf2_ref[:, 128 * c : 128 * (c + 1)] = out2[16 * c + 6 : 16 * c + 10, :].astype(BF)

    for j in range(3):
        xw3[8:168, 256 * j : 256 * j + 256] = g3[16 - 8 * j : 176 - 8 * j, :]
    total = xw3[8:168, 256:512]
    for i in range(3):
        kernel = jnp.concatenate([k3[i, 256 * j : 256 * j + 256, :] for j in range(3)], axis=1)
        total = total + lax.dot_general(
            xw3[9 - i : 169 - i, :].astype(BF), kernel, NT, preferred_element_type=F32
        )
    out3[...] = total
    for c in range(20):
        gf3_ref[:, 256 * c : 256 * (c + 1)] = out3[8 * c + 3 : 8 * c + 5, :].astype(BF)


def swapped(block, axis, flip):
    return lax.ppermute(block, axis, [(i, i ^ flip) for i in range(lax.axis_size(axis))])


def summed_over_devices(keep, send, others):
    width = keep.shape[1]
    part = keep.astype(F32) + swapped(send, "core", 1).astype(F32)
    pieces = part.astype(BF).reshape(16, -1, width)
    pieces = lax.all_to_all(pieces, PLANE, 0, 0)
    pieces, others = lax.optimization_barrier((pieces, others))
    part = jnp.sum(pieces.astype(F32), axis=0).astype(BF)
    pieces = lax.all_gather(part, "z")
    part = jnp.sum(pieces.astype(F32), axis=0).astype(BF)
    pieces = jnp.broadcast_to(part[None], (16,) + part.shape)
    part = lax.all_to_all(pieces, PLANE, 0, 0).reshape(-1, width)
    return part, swapped(part, "core", 1), others


def unpack_kernel(place_ref, mine, got, k1_ref, k2_ref, k3_ref, p2_ref, p3_ref, p4_ref, whole):
    core = place_ref[3]
    whole[pl.ds(pl.multiple_of(core * HALF, 64), HALF), :] = mine[...]
    whole[pl.ds(pl.multiple_of((1 - core) * HALF, 64), HALF), :] = got[...]
    k3_ref[...] = whole[0:2304, :]
    k2_ref[0:576, :] = whole[2304:2880, 0:128]
    k2_ref[576:1152, :] = whole[2304:2880, 128:256]
    for n in range(9):
        at, side = 2880 + 64 * (n // 4), 64 * (n % 4)
        k1_ref[64 * n : 64 * (n + 1), :] = whole[at : at + 64, side : side + 64]
    n = 5
    for ref, count in ((p2_ref, 1), (p3_ref, 2), (p4_ref, 4)):
        for m in range(count):
            at, side = 2880 + 64 * (n // 2), 128 * (n % 2)
            ref[:, 128 * m : 128 * (m + 1)] = whole[at : at + 64, side : side + 128]
            n += 1


def call(kernel, out_shapes, scratch, count, scalars=0, far=0):
    vmem = pl.BlockSpec(memory_space=pltpu.VMEM)
    smem = pl.BlockSpec(memory_space=pltpu.SMEM)
    return pl.pallas_call(
        kernel,
        out_shape=[jax.ShapeDtypeStruct(shape, dtype) for shape, dtype in out_shapes],
        in_specs=[smem] * scalars + [vmem] * count + [pl.BlockSpec(memory_space=pl.ANY)] * far,
        out_specs=[vmem] * len(out_shapes),
        scratch_shapes=[pltpu.VMEM(shape, dtype) for shape, dtype in scratch]
        + ([pltpu.SemaphoreType.DMA((far,))] if far else []),
        compiler_params=pltpu.CompilerParams(vmem_limit_bytes=48 * 1024 * 1024),
    )


def pair_weights(kernel_one):
    none = jnp.zeros((3, FEAT_ONE, FEAT_ONE), BF)
    tap = lambda j: kernel_one[:, j] if 0 <= j < 3 else none
    windows = (1, 2, 3, 0)
    ahead = jnp.concatenate(
        [jnp.concatenate([tap(w - e) for w in windows], axis=1) for e in range(2)], axis=2
    )
    back = jnp.concatenate(
        [jnp.concatenate([tap(e - w + 2) for e in range(2)], axis=1) for w in windows], axis=2
    )
    return ahead, back


def local_part(x1, x2, x3, x4, kernel_one, kernel_two, kernel_three, p2, p3, p4, cot):
    place = jnp.stack(
        [
            lax.axis_index(ROWS),
            lax.axis_index(COLS),
            (lax.axis_index(COLS) == lax.axis_size(COLS) - 1).astype(jnp.int32),
            lax.axis_index("core"),
        ]
    ).astype(jnp.int32)
    ahead, back = pair_weights(kernel_one)
    k2 = kernel_two.reshape(3, 384, 128)
    k3 = kernel_three.reshape(3, 768, 256)
    fars = halos(x1, x2, x3, x4, cot) + (ahead, k2, k3)
    total = RIM + WIDE + RIM
    keep, send, g1, g2, g3, gf4 = call(
        forward_kernel,
        [
            ((HALF, 256), BF), ((HALF, 256), BF),
            ((1008, 128), BF), ((672, 128), BF), ((176, 256), BF), ((1, WIDE), BF),
        ],
        [
            ((24, total), F32), ((24, total), F32), ((16, total), F32), ((8, total), F32), ((8, total), F32),
            ((1120, 256), F32), ((784, 384), F32), ((208, 768), F32),
            ((1104, 128), F32), ((768, 128), F32), ((192, 256), F32),
            ((976, 128), F32), ((656, 128), F32), ((176, 256), F32),
            ((PACK_ROWS, 256), F32),
        ]
        + [(far.shape, BF) for far in fars],
        3,
        1,
        10,
    )(place, p2.T, p3.T, p4.T, *fars)
    gf1, gf2, gf3 = call(
        backward_kernel,
        [((8, WIDE), BF), ((4, WIDE), BF), ((2, WIDE), BF)],
        [
            ((976, 256), F32), ((656, 384), F32), ((176, 768), F32),
            ((640, 128), F32), ((160, 256), F32),
        ],
        6,
    )(g1, g2, g3, back, k2, k3)
    return place, keep, send, gf1, gf2, gf3, gf4


def unpacked(place, mine, got):
    outs = call(
        unpack_kernel,
        [((576, 64), BF), ((1152, 128), BF), ((2304, 256), BF), ((64, 128), BF), ((64, 256), BF), ((64, 512), BF)],
        [((PACK_ROWS, 256), BF)],
        2,
        1,
    )(place, mine, got)
    return (
        outs[0].reshape(3, 3, 64, 64), outs[1].reshape(3, 3, 128, 128), outs[2].reshape(3, 3, 256, 256),
        outs[3].T, outs[4].T, outs[5].T,
    )


def on_device(*args):
    place, keep, send, gf1, gf2, gf3, gf4 = local_part(*args)
    mine, got, others = summed_over_devices(keep, send, (gf1, gf2, gf3, gf4))
    return others + unpacked(place, mine, got)


def solution(mesh):
    mesh = Mesh(mesh.devices.reshape(16, 2, 4, 2, 2), ("z", "x_lo", "y", "x_hi", "core"))
    split = P(ROWS, COLS)
    in_specs = (split,) * 4 + (P(),) * 6 + (split,)
    out_specs = (split,) * 4 + (P(),) * 6
    return jax.shard_map(on_device, mesh=mesh, in_specs=in_specs, out_specs=out_specs, check_vma=False)
```

```python
import functools

import jax
import jax.numpy as jnp
from jax import lax
from jax.experimental import pallas as pl
from jax.experimental.pallas import tpu as pltpu
from jax.sharding import Mesh
from jax.sharding import PartitionSpec as P

FEAT_ONE = 64
FEAT_TWO = 128
FEAT_THREE = 256
FEAT_FOUR = 512

ROWS = ("z", "x_lo", "y")
COLS = ("x_hi", "core")
PLANE = ("x_lo", "y", "x_hi")
PACK_ROWS = 3328
HALF = PACK_ROWS // 2
WIDE = 5120
RIM = 512
BF = jnp.bfloat16
F32 = jnp.float32
NT = (((1,), (1,)), ((), ()))
TN = (((0,), (0,)), ((), ()))


def moved(block, axis, distance):
    count = lax.axis_size(axis)
    route = [(i, i + distance) for i in range(count) if 0 <= i + distance < count]
    return lax.ppermute(block, axis, route)


def stacked(parts, rows):
    total, at = None, 0
    for part in parts:
        padded = jnp.pad(part, ((at, rows - at - part.shape[0]), (0, 0)))
        total = padded if total is None else total + padded
        at += part.shape[0]
    return total


def halos(x1, x2, x3, x4, cot):
    last = stacked((x1[5:], cot[6:], x2[1:], x3, x4), 16)
    first = stacked((x1[:3], cot[:2], x2[:3], x3, x4), 16)
    above = moved(last, ROWS, 1)
    below = moved(first, ROWS, -1)
    parts = (x1, cot, x2, x3, x4, above[:11], below[:11])
    left = moved(stacked([p[:, -RIM:] for p in parts], 48), COLS, 1)
    right = moved(stacked([p[:, :RIM] for p in parts], 48), COLS, -1)
    return x1, cot, x2, x3, x4, above, below, left, right


def gelu_both(v):
    c = 0.7978845608028654
    sq = v * v
    t = jnp.tanh(c * v * (1.0 + 0.044715 * sq))
    half = 0.5 * (1.0 + t)
    slope = half + 0.5 * v * (1.0 - t * t) * (c * (1.0 + 3.0 * 0.044715 * sq))
    return v * half, slope


def tile(wide, at):
    return wide[:, 128 * at : 128 * (at + 1)]


def row_weights(shape, coarse_dim, row_block):
    k = lax.broadcasted_iota(jnp.int32, shape, coarse_dim)
    r = lax.broadcasted_iota(jnp.int32, shape, 1 - coarse_dim)
    two, three = k < 16, k < 24
    scale = jnp.where(two, 2, jnp.where(three, 4, 8))
    count = jnp.where(two, 4, jnp.where(three, 2, 1))
    shift = jnp.where(two, 3, jnp.where(three, 16 + 2, 24 + 1))
    total = (jnp.where(two, 512, jnp.where(three, 256, 128)) - 1).astype(F32)
    coarse = (row_block * count + k - shift).astype(F32)
    fine = (row_block * 8 + r - 4).astype(F32)
    inverse = jnp.where(two, 0.5, jnp.where(three, 0.25, 0.125)).astype(F32)
    place = jnp.clip((fine + 0.5) * inverse - 0.5, 0.0, total)
    return jnp.maximum(0.0, 1.0 - jnp.abs(place - coarse))


def forward_kernel(
    place_ref, p2, p3, p4, *refs
):
    far, refs = refs[:12], refs[12:]
    keep_ref, send_ref, g1_ref, g2_ref, g3_ref, rim_ref, up_ref, down_ref = refs[:8]
    wx1, wc, wx2, wx3, wx4, xw1, xw2, xw3, d1, d2, d3, gm1, gm2, gm3, sums, upward, downward = refs[8:25]
    near, sems = refs[25:37], refs[37]
    copies = [pltpu.make_async_copy(far[n], near[n], sems.at[n]) for n in range(12)]
    for copy in copies:
        copy.start()
    x1, cot, x2, x3, x4, above, below, left, right, t1, k2, k3 = near
    row_block = place_ref[0]
    at_left = place_ref[1] == 0
    at_right = place_ref[2] == 1
    core = place_ref[3]
    lane = lax.broadcasted_iota(jnp.int32, (1, 128), 1)
    low = lane < 64

    def lanes(a, b):
        return jnp.where(low, a, b).astype(F32)

    for ref in (wx1, wc, wx2, wx3, wx4, upward, downward):
        ref[...] = jnp.zeros_like(ref)
    for copy in copies[:10]:
        copy.wait()
    for side, to in ((None, RIM), (left, 0), (right, RIM + WIDE)):
        if side is None:
            cols = slice(to, to + WIDE)
            mid = [ref[...].astype(F32) for ref in (x1, cot, x2, x3, x4)]
            up, down = above[...].astype(F32), below[...].astype(F32)
        else:
            cols = slice(to, to + RIM)
            v = side[...].astype(F32)
            mid = [v[0:8], v[8:16], v[16:20], v[20:22], v[22:23]]
            up, down = v[23:34], v[34:45]
        wx1[1:4, cols] = up[0:3]
        wx1[4:12, cols] = mid[0]
        wx1[12:15, cols] = down[0:3]
        wc[2:4, cols] = up[3:5]
        wc[4:12, cols] = mid[1]
        wc[12:14, cols] = down[3:5]
        wx2[0:3, cols] = up[5:8]
        wx2[3:7, cols] = mid[2]
        wx2[7:10, cols] = down[5:8]
        wx3[0:2, cols] = up[8:10]
        wx3[2:4, cols] = mid[3]
        wx3[4:6, cols] = down[8:10]
        wx4[0:1, cols] = up[10:11]
        wx4[1:2, cols] = mid[4]
        wx4[2:3, cols] = down[10:11]

    for f in range(-1, 41):
        at = 8 + 16 * (f + 1)
        xw1[at : at + 16, 0:128] = tile(wx1, 4 + f)
        xw1[at : at + 16, 128:256] = jnp.where(low, tile(wx1, 5 + f), tile(wx1, 3 + f))
    xw1[0:8, :] = jnp.zeros((8, 256), F32)
    xw1[680:688, :] = jnp.zeros((8, 256), F32)
    pre1 = xw1[8:680, 0:128]
    for i in range(3):
        pre1 = pre1 + jnp.dot(xw1[7 + i : 679 + i, :].astype(BF), t1[i], preferred_element_type=F32)
    y1, slope = gelu_both(pre1)
    y1 = y1.astype(BF).astype(F32)
    d1[...] = slope

    copies[10].wait()
    for j in range(3):
        for c in range(-2, 42):
            at = 8 + 16 * (c + 2)
            xw2[at : at + 16, 128 * j : 128 * j + 128] = tile(wx2, 3 + c + j)
    xw2[0:8, :] = jnp.zeros((8, 384), F32)
    xw2[712:720, :] = jnp.zeros((8, 384), F32)
    pre2 = xw2[8:712, 128:256]
    for i in range(3):
        pre2 = pre2 + jnp.dot(xw2[7 + i : 711 + i, :].astype(BF), k2[i], preferred_element_type=F32)
    y2, slope = gelu_both(pre2)
    y2 = y2.astype(BF)
    d2[...] = slope

    copies[11].wait()
    for j in range(3):
        for c in range(-1, 21):
            at = 8 + 8 * (c + 1)
            first = RIM + 256 * (c + j - 1)
            xw3[at : at + 8, 256 * j : 256 * j + 256] = wx3[:, first : first + 256]
    xw3[0:8, :] = jnp.zeros((8, 768), F32)
    xw3[184:192, :] = jnp.zeros((8, 768), F32)
    pre3 = xw3[8:184, 256:512]
    for i in range(3):
        pre3 = pre3 + jnp.dot(xw3[7 + i : 183 + i, :].astype(BF), k3[i], preferred_element_type=F32)
    y3, slope = gelu_both(pre3)
    y3 = y3.astype(BF)
    d3[...] = slope

    y4 = jnp.concatenate([wx4[:, 512 * c : 512 * c + 512] for c in range(12)], axis=0).astype(BF)

    weights = row_weights((16, 32), 1, row_block).astype(BF)
    rows_up = []
    for y, p, rim, rows, wlo in ((y2, p2, 2, 16, 0), (y3, p3, 1, 8, 16), (y4, p4, 1, 8, 24)):
        twice = jnp.concatenate([p[...], p[...]], axis=0)
        coarse = lax.dot_general(y, twice, NT, preferred_element_type=F32).astype(BF).astype(F32)
        cols = [coarse[rows * n : rows * (n + 1)] for n in range(coarse.shape[0] // rows)]
        end = len(cols) - rim
        cols[rim - 1] = jnp.where(at_left, cols[rim], cols[rim - 1])
        cols[end] = jnp.where(at_right, cols[end - 1], cols[end])
        flat = jnp.concatenate(cols, axis=1).astype(BF)
        rows_up.append(jnp.dot(weights[:, wlo : wlo + rows], flat, preferred_element_type=F32))
    up2, up3, up4 = rows_up

    gates = []
    for f in range(-1, 41):
        k = f + 2
        merged = y1[16 * (f + 1) : 16 * (f + 2)]
        merged = merged + 0.75 * tile(up2, k) + 0.25 * jnp.where(low, tile(up2, k - 1), tile(up2, k + 1))
        k, h = f // 2 + 1, f % 2
        if h == 0:
            merged = merged + lanes(0.375, 0.125) * tile(up3, k - 1) + lanes(0.625, 0.875) * tile(up3, k)
        else:
            merged = merged + lanes(0.875, 0.625) * tile(up3, k) + lanes(0.125, 0.375) * tile(up3, k + 1)
        k, h = f // 4 + 1, f % 4
        p_low, p_high = (2 * h + 0.5) / 8 - 0.5, (2 * h + 1.5) / 8 - 0.5
        other = k - 1 if h < 2 else k + 1
        merged = merged + lanes(1 - abs(p_low), 1 - abs(p_high)) * tile(up4, k)
        merged = merged + lanes(abs(p_low), abs(p_high)) * tile(up4, other)
        slope = gelu_both(merged)[1]
        gate = (slope * tile(wc, 4 + f)).astype(BF).astype(F32)
        gates.append(gate)
        if 0 <= f < 40:
            g = (d1[16 * (f + 1) : 16 * (f + 2)] * gate).astype(BF).astype(F32)
            row = lax.broadcasted_iota(jnp.int32, (16, 1), 0)
            gm1[8 + 16 * f : 24 + 16 * f, :] = jnp.where((row >= 4) & (row < 12), g, 0.0)
            cols = slice(128 * f, 128 * (f + 1))
            g1_ref[:, cols] = g[4:12].astype(BF)
            upward[0:1, cols] = g[4:5]
            downward[0:1, cols] = g[11:12]
    gm1[0:8, :] = jnp.zeros((8, 128), F32)
    gm1[648:656, :] = jnp.zeros((8, 128), F32)

    flat = jnp.concatenate(gates, axis=1).astype(BF)
    weights_back = row_weights((32, 16), 0, row_block)
    k = lax.broadcasted_iota(jnp.int32, (32, 16), 0)
    r = lax.broadcasted_iota(jnp.int32, (32, 16), 1)
    weights_back = jnp.where((k < 24) | ((r >= 4) & (r < 12)), weights_back, 0.0).astype(BF)
    down = jnp.dot(weights_back, flat, preferred_element_type=F32)
    down2, down3, down4 = down[0:16], down[16:24], down[24:32]

    def folded(v):
        return v + pltpu.roll(v, 64, 1)

    cg2 = []
    for c in range(40):
        v = 0.75 * tile(down2, c + 1) + 0.25 * jnp.where(low, tile(down2, c + 2), tile(down2, c))
        if c == 0:
            v = v + jnp.where(at_left, lanes(0.25, 0.0) * tile(down2, 1), 0.0)
        if c == 39:
            v = v + jnp.where(at_right, lanes(0.0, 0.25) * tile(down2, 40), 0.0)
        cg2.append(folded(v))
    cg3 = []
    for c in range(20):
        at = 2 * c
        v = lanes(0.125, 0.375) * tile(down3, at) + lanes(0.625, 0.875) * tile(down3, at + 1)
        v = v + lanes(0.875, 0.625) * tile(down3, at + 2) + lanes(0.375, 0.125) * tile(down3, at + 3)
        if c == 0:
            v = v + jnp.where(at_left, lanes(0.375, 0.125) * tile(down3, 1), 0.0)
        if c == 19:
            v = v + jnp.where(at_right, lanes(0.125, 0.375) * tile(down3, 40), 0.0)
        cg3.append(folded(v))
    cg4 = []
    for c in range(-1, 11):
        v = jnp.zeros((8, 128), F32)
        for n in range(8):
            a, b = (2 * n + 0.5) / 8, (2 * n + 1.5) / 8
            a, b = (a, b) if n < 4 else (2 - a, 2 - b)
            pair = 4 * c - 2 + n
            if 0 <= pair < 40:
                v = v + lanes(a, b) * tile(down4, pair + 1)
        cg4.append(folded(v))
    cg4[1] = cg4[1] + jnp.where(at_left, cg4[0], 0.0)
    cg4[-2] = cg4[-2] + jnp.where(at_right, cg4[-1], 0.0)
    cg4[0] = jnp.where(at_left, 0.0, cg4[0])
    cg4[-1] = jnp.where(at_right, 0.0, cg4[-1])
    for n in range(12):
        cols = slice(128 * n, 128 * (n + 1))
        upward[3:4, cols] = cg4[n][0:1]
        rim_ref[0:1, cols] = cg4[n][1:2]
        downward[3:4, cols] = cg4[n][2:3]

    flat2 = jnp.concatenate(cg2, axis=0).astype(BF).astype(F32)
    flat3 = jnp.concatenate(cg3, axis=0).astype(BF).astype(F32)
    flat4 = jnp.concatenate(cg4, axis=0).astype(BF).astype(F32)
    back2 = jnp.dot(flat2[:, 0:64].astype(BF), p2[...], preferred_element_type=F32)
    back3 = jnp.dot(flat3[:, 0:64].astype(BF), p3[...], preferred_element_type=F32)
    g2 = (d2[32:672, :] * back2).astype(BF).astype(F32)
    g3 = (d3[8:168, :] * back3).astype(BF).astype(F32)

    row2 = lax.broadcasted_iota(jnp.int32, (640, 1), 0) % 16
    own2 = (row2 >= 3) & (row2 < 7)
    row3 = lax.broadcasted_iota(jnp.int32, (160, 1), 0) % 8
    own3 = (row3 >= 2) & (row3 < 4)
    gm2[0:8, :] = jnp.zeros((8, 128), F32)
    gm2[8:648, :] = jnp.where(own2, g2, 0.0)
    gm2[648:656, :] = jnp.zeros((8, 128), F32)
    gm3[0:8, :] = jnp.zeros((8, 256), F32)
    gm3[8:168, :] = jnp.where(own3, g3, 0.0)
    gm3[168:176, :] = jnp.zeros((8, 256), F32)
    for c in range(40):
        at, cols = 8 + 16 * c + 3, slice(128 * c, 128 * (c + 1))
        g2_ref[:, cols] = gm2[at : at + 4, :].astype(BF)
        upward[1:2, cols] = gm2[at : at + 1, :]
        downward[1:2, cols] = gm2[at + 3 : at + 4, :]
    for c in range(20):
        at, cols = 8 + 8 * c + 2, slice(256 * c, 256 * (c + 1))
        g3_ref[:, cols] = gm3[at : at + 2, :].astype(BF)
        upward[2:3, cols] = gm3[at : at + 1, :]
        downward[2:3, cols] = gm3[at + 1 : at + 2, :]
    up_ref[...] = upward[...].astype(BF)
    down_ref[...] = downward[...].astype(BF)

    cells = 327680
    x = xw3[16:176, :].astype(BF)
    shifted = jnp.concatenate([gm3[9 - i : 169 - i, :] for i in range(3)], axis=1).astype(BF)
    z = lax.dot_general(x, shifted, TN, preferred_element_type=F32) * (cells // 16) ** -0.5
    for i in range(3):
        sums[768 * i : 768 * (i + 1), :] = z[:, 256 * i : 256 * (i + 1)]
    x = xw2[40:680, :].astype(BF)
    shifted = jnp.concatenate([gm2[9 - i : 649 - i, :] for i in range(3)], axis=1).astype(BF)
    z = lax.dot_general(x, shifted, TN, preferred_element_type=F32) * (cells // 4) ** -0.5
    base = 2304
    sums[base : base + 384, 0:128] = z[:, 0:128]
    sums[base + 384 : base + 576, 0:128] = z[0:192, 128:256]
    sums[base : base + 192, 128:256] = z[192:384, 128:256]
    sums[base + 192 : base + 576, 128:256] = z[:, 256:384]
    x = xw1[24:664, :].astype(BF)
    shifted = jnp.concatenate([gm1[9 - i : 649 - i, :] for i in range(3)], axis=1).astype(BF)
    z = lax.dot_general(x, shifted, TN, preferred_element_type=F32) * cells**-0.5
    window = (192, 0, 64, 128)
    blocks = []
    for i in range(3):
        zi = z[:, 128 * i : 128 * (i + 1)]
        for j in range(3):
            a, b = window[j], window[j + 1]
            blocks.append(zi[a : a + 64] + pltpu.roll(zi[b : b + 64], 64, 1))
    blocks.append(jnp.zeros((64, 128), F32))
    pairs = [jnp.where(low, blocks[n], pltpu.roll(blocks[n + 1], 64, 1)) for n in range(0, 10, 2)]
    y2_own, y3_own = y2[32:672], y3.astype(F32)[8:168].astype(BF)
    for y, flat, mask, branch in (
        (y2_own, flat2, own2, 1),
        (y3_own, flat3, own3, 2),
        (y4, flat4, None, 3),
    ):
        masked = (flat if mask is None else jnp.where(mask, flat, 0.0)).astype(BF)
        z = lax.dot_general(masked, y, TN, preferred_element_type=F32) * (cells // 4**branch) ** -0.5
        pairs += [z[0:64, 128 * n : 128 * (n + 1)] for n in range(z.shape[1] // 128)]
    base = 2880
    for n in range(12):
        at, side = base + 64 * (n // 2), 128 * (n % 2)
        sums[at : at + 64, side : side + 128] = pairs[n]
    sums[3264:3328, :] = jnp.zeros((64, 256), F32)
    keep_ref[...] = sums[pl.ds(pl.multiple_of(core * HALF, 64), HALF), :].astype(BF)
    send_ref[...] = sums[pl.ds(pl.multiple_of((1 - core) * HALF, 64), HALF), :].astype(BF)


def rims_kernel(g1_ref, g2_ref, g3_ref, rim_ref, above_ref, below_ref, left_ref, right_ref, out):
    g1, g2, g3, above, below = (ref[...].astype(F32) for ref in (g1_ref, g2_ref, g3_ref, above_ref, below_ref))
    rim = rim_ref[...] + above[3:4, 0:1536] + below[3:4, 0:1536]
    for ref, one, three, four in ((left_ref, 0, 0, 0), (right_ref, WIDE - 128, WIDE - 256, 1408)):
        ones, threes = slice(one, one + 128), slice(three, three + 256)
        out[...] = jnp.zeros_like(out)
        out[0:1, 0:128] = above[0:1, ones]
        out[1:9, 0:128] = g1[:, ones]
        out[9:10, 0:128] = below[0:1, ones]
        out[10:11, 0:128] = above[1:2, ones]
        out[11:15, 0:128] = g2[:, ones]
        out[15:16, 0:128] = below[1:2, ones]
        out[16:17, :] = above[2:3, threes]
        out[17:19, :] = g3[:, threes]
        out[19:20, :] = below[2:3, threes]
        out[20:21, 0:128] = rim[:, four : four + 128]
        ref[...] = out[...].astype(BF)


def backward_kernel(
    g1_ref, g2_ref, g3_ref, rim_ref, above_ref, below_ref, left_ref, right_ref, t1b, k2, k3, p4,
    gf1_ref, gf2_ref, gf3_ref, gf4_ref, wide1, wide2, wide3, xw1, xw2, xw3, out2, out3,
):
    low = lax.broadcasted_iota(jnp.int32, (1, 128), 1) < 64
    for ref, n in ((xw1, 640), (xw2, 320), (xw3, 160)):
        ref[0:8, :] = jnp.zeros((8, ref.shape[1]), F32)
        ref[8 + n : 16 + n, :] = jnp.zeros((8, ref.shape[1]), F32)
    above, below, left, right = (ref[...].astype(F32) for ref in (above_ref, below_ref, left_ref, right_ref))
    for n, (wide, g_ref, top, rows, start, step) in enumerate(
        ((wide1, g1_ref, 3, 8, 0, 128), (wide2, g2_ref, 0, 4, 10, 128), (wide3, g3_ref, 0, 2, 16, 256))
    ):
        wide[...] = jnp.zeros_like(wide)
        mid, end = slice(step, step + WIDE), step + WIDE
        wide[top : top + 1, mid] = above[n : n + 1]
        wide[top + 1 : top + 1 + rows, mid] = g_ref[...].astype(F32)
        wide[top + 1 + rows : top + 2 + rows, mid] = below[n : n + 1]
        wide[top : top + 2 + rows, 0:step] = left[start : start + 2 + rows, 0:step]
        wide[top : top + 2 + rows, end : end + step] = right[start : start + 2 + rows, 0:step]

    for f in range(40):
        at = 8 + 16 * f
        xw1[at : at + 16, 0:128] = tile(wide1, f + 1)
        xw1[at : at + 16, 128:256] = jnp.where(low, tile(wide1, f + 2), tile(wide1, f))
    total = xw1[8:648, 0:128]
    for i in range(3):
        total = total + lax.dot_general(
            xw1[9 - i : 649 - i, :].astype(BF), t1b[i], NT, preferred_element_type=F32
        )
    for f in range(40):
        gf1_ref[:, 128 * f : 128 * (f + 1)] = total[16 * f + 4 : 16 * f + 12].astype(BF)

    for j in range(3):
        for c in range(40):
            xw2[8 + 8 * c : 16 + 8 * c, 128 * j : 128 * j + 128] = tile(wide2, c + 2 - j)
    total = xw2[8:328, 128:256]
    for i in range(3):
        kernel = jnp.concatenate([k2[i, 128 * j : 128 * j + 128, :] for j in range(3)], axis=1)
        total = total + lax.dot_general(
            xw2[9 - i : 329 - i, :].astype(BF), kernel, NT, preferred_element_type=F32
        )
    out2[...] = total
    for c in range(40):
        gf2_ref[:, 128 * c : 128 * (c + 1)] = out2[8 * c + 1 : 8 * c + 5, :].astype(BF)

    for j in range(3):
        for c in range(20):
            first = 256 * (c + 2 - j)
            xw3[8 + 8 * c : 16 + 8 * c, 256 * j : 256 * j + 256] = wide3[:, first : first + 256]
    total = xw3[8:168, 256:512]
    for i in range(3):
        kernel = jnp.concatenate([k3[i, 256 * j : 256 * j + 256, :] for j in range(3)], axis=1)
        total = total + lax.dot_general(
            xw3[9 - i : 169 - i, :].astype(BF), kernel, NT, preferred_element_type=F32
        )
    out3[...] = total
    for c in range(20):
        gf3_ref[:, 256 * c : 256 * (c + 1)] = out3[8 * c + 1 : 8 * c + 3, :].astype(BF)

    rim = rim_ref[...] + above[3:4, 0:1536] + below[3:4, 0:1536]
    for c in range(10):
        cg = rim[:, 128 * (c + 1) : 128 * (c + 2)]
        if c == 0:
            cg = cg + left[20:21, 0:128]
        if c == 9:
            cg = cg + right[20:21, 0:128]
        cg = jnp.broadcast_to(cg[:, 0:64], (8, 64)).astype(BF)
        back = jnp.dot(cg, p4[...], preferred_element_type=F32)
        gf4_ref[0:1, 512 * c : 512 * c + 512] = back[0:1].astype(BF)


def swapped(block, axis, flip):
    return lax.ppermute(block, axis, [(i, i ^ flip) for i in range(lax.axis_size(axis))])


def unpack_kernel(place_ref, mine, got, k1_ref, k2_ref, k3_ref, p2_ref, p3_ref, p4_ref, whole):
    core = place_ref[3]
    whole[pl.ds(pl.multiple_of(core * HALF, 64), HALF), :] = mine[...]
    whole[pl.ds(pl.multiple_of((1 - core) * HALF, 64), HALF), :] = got[...]
    k3_ref[...] = whole[0:2304, :]
    k2_ref[0:576, :] = whole[2304:2880, 0:128]
    k2_ref[576:1152, :] = whole[2304:2880, 128:256]
    for n in range(9):
        at, side = 2880 + 64 * (n // 4), 64 * (n % 4)
        k1_ref[64 * n : 64 * (n + 1), :] = whole[at : at + 64, side : side + 64]
    n = 5
    for ref, count in ((p2_ref, 1), (p3_ref, 2), (p4_ref, 4)):
        for m in range(count):
            at, side = 2880 + 64 * (n // 2), 128 * (n % 2)
            ref[:, 128 * m : 128 * (m + 1)] = whole[at : at + 64, side : side + 128]
            n += 1


def call(kernel, out_shapes, scratch, count, scalars=0, far=0):
    vmem = pl.BlockSpec(memory_space=pltpu.VMEM)
    smem = pl.BlockSpec(memory_space=pltpu.SMEM)
    return pl.pallas_call(
        kernel,
        out_shape=[jax.ShapeDtypeStruct(shape, dtype) for shape, dtype in out_shapes],
        in_specs=[smem] * scalars + [vmem] * count + [pl.BlockSpec(memory_space=pl.ANY)] * far,
        out_specs=[vmem] * len(out_shapes),
        scratch_shapes=[pltpu.VMEM(shape, dtype) for shape, dtype in scratch]
        + ([pltpu.SemaphoreType.DMA((far,))] if far else []),
        compiler_params=pltpu.CompilerParams(vmem_limit_bytes=48 * 1024 * 1024),
    )


def pair_weights(kernel_one):
    none = jnp.zeros((3, FEAT_ONE, FEAT_ONE), BF)
    tap = lambda j: kernel_one[:, j] if 0 <= j < 3 else none
    windows = (1, 2, 3, 0)
    ahead = jnp.concatenate(
        [jnp.concatenate([tap(w - e) for w in windows], axis=1) for e in range(2)], axis=2
    )
    back = jnp.concatenate(
        [jnp.concatenate([tap(e - w + 2) for e in range(2)], axis=1) for w in windows], axis=2
    )
    return ahead, back


def local_part(x1, x2, x3, x4, kernel_one, kernel_two, kernel_three, p2, p3, p4, cot):
    place = jnp.stack(
        [
            lax.axis_index(ROWS),
            lax.axis_index(COLS),
            (lax.axis_index(COLS) == lax.axis_size(COLS) - 1).astype(jnp.int32),
            lax.axis_index("core"),
        ]
    ).astype(jnp.int32)
    ahead, back = pair_weights(kernel_one)
    k2 = kernel_two.reshape(3, 384, 128)
    k3 = kernel_three.reshape(3, 768, 256)
    fars = halos(x1, x2, x3, x4, cot) + (ahead, k2, k3)
    total = RIM + WIDE + RIM
    keep, send, g1, g2, g3, rim, up, down = call(
        forward_kernel,
        [
            ((HALF, 256), BF), ((HALF, 256), BF),
            ((8, WIDE), BF), ((4, WIDE), BF), ((2, WIDE), BF), ((1, 1536), F32),
            ((8, WIDE), BF), ((8, WIDE), BF),
        ],
        [
            ((16, total), F32), ((16, total), F32), ((16, total), F32), ((8, total), F32), ((8, total), F32),
            ((688, 256), F32), ((720, 384), F32), ((192, 768), F32),
            ((672, 128), F32), ((704, 128), F32), ((176, 256), F32),
            ((656, 128), F32), ((656, 128), F32), ((176, 256), F32),
            ((PACK_ROWS, 256), F32), ((8, WIDE), F32), ((8, WIDE), F32),
        ]
        + [(far.shape, BF) for far in fars],
        3,
        1,
        12,
    )(place, p2.T, p3.T, p4.T, *fars)
    return place, keep, send, (g1, g2, g3, rim), up, down, (back, k2, k3, p4.T)


def from_beside(grads, above, below):
    left, right = call(
        rims_kernel, [((32, 256), BF), ((32, 256), BF)], [((32, 256), F32)], 6
    )(*grads, above, below)
    return moved(right, COLS, 1), moved(left, COLS, -1)


def input_grads(grads, above, below, left, right, weights):
    return call(
        backward_kernel,
        [((8, WIDE), BF), ((4, WIDE), BF), ((2, WIDE), BF), ((1, WIDE), BF)],
        [
            ((16, 42 * 128), F32), ((8, 42 * 128), F32), ((8, 22 * 256), F32),
            ((656, 256), F32), ((336, 384), F32), ((176, 768), F32),
            ((320, 128), F32), ((160, 256), F32),
        ],
        12,
    )(*grads, above, below, left, right, *weights)


def unpacked(place, mine, got):
    outs = call(
        unpack_kernel,
        [((576, 64), BF), ((1152, 128), BF), ((2304, 256), BF), ((64, 128), BF), ((64, 256), BF), ((64, 512), BF)],
        [((PACK_ROWS, 256), BF)],
        2,
        1,
    )(place, mine, got)
    return (
        outs[0].reshape(3, 3, 64, 64), outs[1].reshape(3, 3, 128, 128), outs[2].reshape(3, 3, 256, 256),
        outs[3].T, outs[4].T, outs[5].T,
    )


def on_device(*args):
    place, keep, send, grads, up, down, weights = local_part(*args)
    part = (keep.astype(F32) + swapped(send, "core", 1).astype(F32)).astype(BF)
    part, up, down = lax.optimization_barrier((part, up, down))

    pieces = lax.all_to_all(part.reshape(16, -1, part.shape[1]), PLANE, 0, 0)
    above, below = moved(down, ROWS, 1), moved(up, ROWS, -1)
    pieces, above, below = lax.optimization_barrier((pieces, above, below))
    part = jnp.sum(pieces.astype(F32), axis=0).astype(BF)

    pieces = lax.all_gather(part, "z")
    part = jnp.sum(pieces.astype(F32), axis=0).astype(BF)
    part, above, below = lax.optimization_barrier((part, above, below))

    pieces = jnp.broadcast_to(part[None], (16,) + part.shape)
    mine = lax.all_to_all(pieces, PLANE, 0, 0).reshape(keep.shape)
    left, right = from_beside(grads, above, below)
    outs = input_grads(grads, above, below, left, right, weights)
    mine, outs = lax.optimization_barrier((mine, outs))
    return tuple(outs) + unpacked(place, mine, swapped(mine, "core", 1))


def solution(mesh):
    mesh = Mesh(mesh.devices.reshape(16, 2, 4, 2, 2), ("z", "x_lo", "y", "x_hi", "core"))
    split = P(ROWS, COLS)
    in_specs = (split,) * 4 + (P(),) * 6 + (split,)
    out_specs = (split,) * 4 + (P(),) * 6
    return jax.shard_map(on_device, mesh=mesh, in_specs=in_specs, out_specs=out_specs, check_vma=False)
```

```python
import functools

import jax
import jax.numpy as jnp
from jax import lax
from jax.experimental import pallas as pl
from jax.experimental.pallas import tpu as pltpu
from jax.sharding import Mesh
from jax.sharding import PartitionSpec as P

FEAT_ONE = 64
FEAT_TWO = 128
FEAT_THREE = 256
FEAT_FOUR = 512

ROWS = ("z_hi", "z_lo", "x_lo", "y")
COLS = ("x_hi", "core")
SLAB = ("z_lo", "x_lo", "y", "x_hi")
PACK_ROWS = 3328
WIDE = 5120
RIM = 512
BF = jnp.bfloat16
F32 = jnp.float32
NT = (((1,), (1,)), ((), ()))
TN = (((0,), (0,)), ((), ()))


def moved(block, axis, distance):
    count = lax.axis_size(axis)
    route = [(i, i + distance) for i in range(count) if 0 <= i + distance < count]
    return lax.ppermute(block, axis, route)


def stacked(parts, rows):
    total, at = None, 0
    for part in parts:
        padded = jnp.pad(part, ((at, rows - at - part.shape[0]), (0, 0)))
        total = padded if total is None else total + padded
        at += part.shape[0]
    return total


def edge_rows_kernel(x1_ref, cot_ref, x2_ref, x3_ref, x4_ref, last_ref, first_ref, last, first):
    x1, cot, x2, x3, x4 = (ref[...].astype(F32) for ref in (x1_ref, cot_ref, x2_ref, x3_ref, x4_ref))
    for out, ref, ones, cots, twos in (
        (last, last_ref, x1[5:8], cot[6:8], x2[1:4]),
        (first, first_ref, x1[0:3], cot[0:2], x2[0:3]),
    ):
        out[0:3, :] = ones
        out[3:5, :] = cots
        out[5:8, :] = twos
        out[8:10, :] = x3
        out[10:11, :] = x4
        out[11:16, :] = jnp.zeros((5, WIDE), F32)
        ref[...] = out[...].astype(BF)


def halos(x1, x2, x3, x4, cot):
    last, first = call(edge_rows_kernel, [((16, WIDE), BF)] * 2, [((16, WIDE), F32)] * 2, 5)(x1, cot, x2, x3, x4)
    above = moved(last, ROWS, 1)
    below = moved(first, ROWS, -1)
    parts = (x1, cot, x2, x3, x4, above[:11], below[:11])
    left = moved(stacked([p[:, -RIM:] for p in parts], 48), COLS, 1)
    right = moved(stacked([p[:, :RIM] for p in parts], 48), COLS, -1)
    return x1, cot, x2, x3, x4, above, below, left, right


def gelu_both(v):
    c = 0.7978845608028654
    sq = v * v
    t = jnp.tanh(c * v * (1.0 + 0.044715 * sq))
    half = 0.5 * (1.0 + t)
    slope = half + 0.5 * v * (1.0 - t * t) * (c * (1.0 + 3.0 * 0.044715 * sq))
    return v * half, slope


def tile(wide, at):
    return wide[:, 128 * at : 128 * (at + 1)]


def row_weights(shape, coarse_dim, row_block):
    k = lax.broadcasted_iota(jnp.int32, shape, coarse_dim)
    r = lax.broadcasted_iota(jnp.int32, shape, 1 - coarse_dim)
    two, three = k < 16, k < 24
    scale = jnp.where(two, 2, jnp.where(three, 4, 8))
    count = jnp.where(two, 4, jnp.where(three, 2, 1))
    shift = jnp.where(two, 3, jnp.where(three, 16 + 2, 24 + 1))
    total = (jnp.where(two, 512, jnp.where(three, 256, 128)) - 1).astype(F32)
    coarse = (row_block * count + k - shift).astype(F32)
    fine = (row_block * 8 + r - 4).astype(F32)
    inverse = jnp.where(two, 0.5, jnp.where(three, 0.25, 0.125)).astype(F32)
    place = jnp.clip((fine + 0.5) * inverse - 0.5, 0.0, total)
    return jnp.maximum(0.0, 1.0 - jnp.abs(place - coarse))


def forward_kernel(
    place_ref, p2, p3, p4, *refs
):
    far, refs = refs[:12], refs[12:]
    keep_ref, send_ref, g1_ref, g2_ref, g3_ref, rim_ref, up_ref, down_ref = refs[:8]
    wx1, wc, wx2, wx3, wx4, xw1, xw2, xw3, d1, d2, d3, gm1, gm2, gm3, sums, upward, downward = refs[8:25]
    near, sems = refs[25:37], refs[37]
    copies = [pltpu.make_async_copy(far[n], near[n], sems.at[n]) for n in range(12)]
    for copy in copies:
        copy.start()
    x1, cot, x2, x3, x4, above, below, left, right, t1, k2, k3 = near
    row_block = place_ref[0]
    at_left = place_ref[1] == 0
    at_right = place_ref[2] == 1
    core = place_ref[3]
    lane = lax.broadcasted_iota(jnp.int32, (1, 128), 1)
    low = lane < 64

    def lanes(a, b):
        return jnp.where(low, a, b).astype(F32)

    for ref in (wx1, wc, wx2, wx3, wx4, upward, downward):
        ref[...] = jnp.zeros_like(ref)
    for copy in copies[:10]:
        copy.wait()
    for side, to in ((None, RIM), (left, 0), (right, RIM + WIDE)):
        if side is None:
            cols = slice(to, to + WIDE)
            mid = [ref[...].astype(F32) for ref in (x1, cot, x2, x3, x4)]
            up, down = above[...].astype(F32), below[...].astype(F32)
        else:
            cols = slice(to, to + RIM)
            v = side[...].astype(F32)
            mid = [v[0:8], v[8:16], v[16:20], v[20:22], v[22:23]]
            up, down = v[23:34], v[34:45]
        wx1[1:4, cols] = up[0:3]
        wx1[4:12, cols] = mid[0]
        wx1[12:15, cols] = down[0:3]
        wc[2:4, cols] = up[3:5]
        wc[4:12, cols] = mid[1]
        wc[12:14, cols] = down[3:5]
        wx2[0:3, cols] = up[5:8]
        wx2[3:7, cols] = mid[2]
        wx2[7:10, cols] = down[5:8]
        wx3[0:2, cols] = up[8:10]
        wx3[2:4, cols] = mid[3]
        wx3[4:6, cols] = down[8:10]
        wx4[0:1, cols] = up[10:11]
        wx4[1:2, cols] = mid[4]
        wx4[2:3, cols] = down[10:11]

    for f in range(-1, 41):
        at = 8 + 16 * (f + 1)
        xw1[at : at + 16, 0:128] = tile(wx1, 4 + f)
        xw1[at : at + 16, 128:256] = jnp.where(low, tile(wx1, 5 + f), tile(wx1, 3 + f))
    xw1[0:8, :] = jnp.zeros((8, 256), F32)
    xw1[680:688, :] = jnp.zeros((8, 256), F32)
    pre1 = xw1[8:680, 0:128]
    for i in range(3):
        pre1 = pre1 + jnp.dot(xw1[7 + i : 679 + i, :].astype(BF), t1[i], preferred_element_type=F32)
    y1, slope = gelu_both(pre1)
    y1 = y1.astype(BF).astype(F32)
    d1[...] = slope

    copies[10].wait()
    for j in range(3):
        for c in range(-2, 42):
            at = 8 + 16 * (c + 2)
            xw2[at : at + 16, 128 * j : 128 * j + 128] = tile(wx2, 3 + c + j)
    xw2[0:8, :] = jnp.zeros((8, 384), F32)
    xw2[712:720, :] = jnp.zeros((8, 384), F32)
    pre2 = xw2[8:712, 128:256]
    for i in range(3):
        pre2 = pre2 + jnp.dot(xw2[7 + i : 711 + i, :].astype(BF), k2[i], preferred_element_type=F32)
    y2, slope = gelu_both(pre2)
    y2 = y2.astype(BF)
    d2[...] = slope

    copies[11].wait()
    for j in range(3):
        for c in range(-1, 21):
            at = 8 + 8 * (c + 1)
            first = RIM + 256 * (c + j - 1)
            xw3[at : at + 8, 256 * j : 256 * j + 256] = wx3[:, first : first + 256]
    xw3[0:8, :] = jnp.zeros((8, 768), F32)
    xw3[184:192, :] = jnp.zeros((8, 768), F32)
    pre3 = xw3[8:184, 256:512]
    for i in range(3):
        pre3 = pre3 + jnp.dot(xw3[7 + i : 183 + i, :].astype(BF), k3[i], preferred_element_type=F32)
    y3, slope = gelu_both(pre3)
    y3 = y3.astype(BF)
    d3[...] = slope

    y4 = jnp.concatenate([wx4[:, 512 * c : 512 * c + 512] for c in range(12)], axis=0).astype(BF)

    weights = row_weights((16, 32), 1, row_block).astype(BF)
    rows_up = []
    for y, p, rim, rows, wlo in ((y2, p2, 2, 16, 0), (y3, p3, 1, 8, 16), (y4, p4, 1, 8, 24)):
        twice = jnp.concatenate([p[...], p[...]], axis=0)
        coarse = lax.dot_general(y, twice, NT, preferred_element_type=F32).astype(BF).astype(F32)
        cols = [coarse[rows * n : rows * (n + 1)] for n in range(coarse.shape[0] // rows)]
        end = len(cols) - rim
        cols[rim - 1] = jnp.where(at_left, cols[rim], cols[rim - 1])
        cols[end] = jnp.where(at_right, cols[end - 1], cols[end])
        flat = jnp.concatenate(cols, axis=1).astype(BF)
        rows_up.append(jnp.dot(weights[:, wlo : wlo + rows], flat, preferred_element_type=F32))
    up2, up3, up4 = rows_up

    gates = []
    for f in range(-1, 41):
        k = f + 2
        merged = y1[16 * (f + 1) : 16 * (f + 2)]
        merged = merged + 0.75 * tile(up2, k) + 0.25 * jnp.where(low, tile(up2, k - 1), tile(up2, k + 1))
        k, h = f // 2 + 1, f % 2
        if h == 0:
            merged = merged + lanes(0.375, 0.125) * tile(up3, k - 1) + lanes(0.625, 0.875) * tile(up3, k)
        else:
            merged = merged + lanes(0.875, 0.625) * tile(up3, k) + lanes(0.125, 0.375) * tile(up3, k + 1)
        k, h = f // 4 + 1, f % 4
        p_low, p_high = (2 * h + 0.5) / 8 - 0.5, (2 * h + 1.5) / 8 - 0.5
        other = k - 1 if h < 2 else k + 1
        merged = merged + lanes(1 - abs(p_low), 1 - abs(p_high)) * tile(up4, k)
        merged = merged + lanes(abs(p_low), abs(p_high)) * tile(up4, other)
        slope = gelu_both(merged)[1]
        gate = (slope * tile(wc, 4 + f)).astype(BF).astype(F32)
        gates.append(gate)
        if 0 <= f < 40:
            g = (d1[16 * (f + 1) : 16 * (f + 2)] * gate).astype(BF).astype(F32)
            row = lax.broadcasted_iota(jnp.int32, (16, 1), 0)
            gm1[8 + 16 * f : 24 + 16 * f, :] = jnp.where((row >= 4) & (row < 12), g, 0.0)
            cols = slice(128 * f, 128 * (f + 1))
            g1_ref[:, cols] = g[4:12].astype(BF)
            upward[0:1, cols] = g[4:5]
            downward[0:1, cols] = g[11:12]
    gm1[0:8, :] = jnp.zeros((8, 128), F32)
    gm1[648:656, :] = jnp.zeros((8, 128), F32)

    flat = jnp.concatenate(gates, axis=1).astype(BF)
    weights_back = row_weights((32, 16), 0, row_block)
    k = lax.broadcasted_iota(jnp.int32, (32, 16), 0)
    r = lax.broadcasted_iota(jnp.int32, (32, 16), 1)
    weights_back = jnp.where((k < 24) | ((r >= 4) & (r < 12)), weights_back, 0.0).astype(BF)
    down = jnp.dot(weights_back, flat, preferred_element_type=F32)
    down2, down3, down4 = down[0:16], down[16:24], down[24:32]

    def folded(v):
        return v + pltpu.roll(v, 64, 1)

    cg2 = []
    for c in range(40):
        v = 0.75 * tile(down2, c + 1) + 0.25 * jnp.where(low, tile(down2, c + 2), tile(down2, c))
        if c == 0:
            v = v + jnp.where(at_left, lanes(0.25, 0.0) * tile(down2, 1), 0.0)
        if c == 39:
            v = v + jnp.where(at_right, lanes(0.0, 0.25) * tile(down2, 40), 0.0)
        cg2.append(folded(v))
    cg3 = []
    for c in range(20):
        at = 2 * c
        v = lanes(0.125, 0.375) * tile(down3, at) + lanes(0.625, 0.875) * tile(down3, at + 1)
        v = v + lanes(0.875, 0.625) * tile(down3, at + 2) + lanes(0.375, 0.125) * tile(down3, at + 3)
        if c == 0:
            v = v + jnp.where(at_left, lanes(0.375, 0.125) * tile(down3, 1), 0.0)
        if c == 19:
            v = v + jnp.where(at_right, lanes(0.125, 0.375) * tile(down3, 40), 0.0)
        cg3.append(folded(v))
    cg4 = []
    for c in range(-1, 11):
        v = jnp.zeros((8, 128), F32)
        for n in range(8):
            a, b = (2 * n + 0.5) / 8, (2 * n + 1.5) / 8
            a, b = (a, b) if n < 4 else (2 - a, 2 - b)
            pair = 4 * c - 2 + n
            if 0 <= pair < 40:
                v = v + lanes(a, b) * tile(down4, pair + 1)
        cg4.append(folded(v))
    cg4[1] = cg4[1] + jnp.where(at_left, cg4[0], 0.0)
    cg4[-2] = cg4[-2] + jnp.where(at_right, cg4[-1], 0.0)
    cg4[0] = jnp.where(at_left, 0.0, cg4[0])
    cg4[-1] = jnp.where(at_right, 0.0, cg4[-1])
    for n in range(12):
        cols = slice(128 * n, 128 * (n + 1))
        upward[3:4, cols] = cg4[n][0:1]
        rim_ref[0:1, cols] = cg4[n][1:2]
        downward[3:4, cols] = cg4[n][2:3]

    flat2 = jnp.concatenate(cg2, axis=0).astype(BF).astype(F32)
    flat3 = jnp.concatenate(cg3, axis=0).astype(BF).astype(F32)
    flat4 = jnp.concatenate(cg4, axis=0).astype(BF).astype(F32)
    back2 = jnp.dot(flat2[:, 0:64].astype(BF), p2[...], preferred_element_type=F32)
    back3 = jnp.dot(flat3[:, 0:64].astype(BF), p3[...], preferred_element_type=F32)
    g2 = (d2[32:672, :] * back2).astype(BF).astype(F32)
    g3 = (d3[8:168, :] * back3).astype(BF).astype(F32)

    row2 = lax.broadcasted_iota(jnp.int32, (640, 1), 0) % 16
    own2 = (row2 >= 3) & (row2 < 7)
    row3 = lax.broadcasted_iota(jnp.int32, (160, 1), 0) % 8
    own3 = (row3 >= 2) & (row3 < 4)
    gm2[0:8, :] = jnp.zeros((8, 128), F32)
    gm2[8:648, :] = jnp.where(own2, g2, 0.0)
    gm2[648:656, :] = jnp.zeros((8, 128), F32)
    gm3[0:8, :] = jnp.zeros((8, 256), F32)
    gm3[8:168, :] = jnp.where(own3, g3, 0.0)
    gm3[168:176, :] = jnp.zeros((8, 256), F32)
    for c in range(40):
        at, cols = 8 + 16 * c + 3, slice(128 * c, 128 * (c + 1))
        g2_ref[:, cols] = gm2[at : at + 4, :].astype(BF)
        upward[1:2, cols] = gm2[at : at + 1, :]
        downward[1:2, cols] = gm2[at + 3 : at + 4, :]
    for c in range(20):
        at, cols = 8 + 8 * c + 2, slice(256 * c, 256 * (c + 1))
        g3_ref[:, cols] = gm3[at : at + 2, :].astype(BF)
        upward[2:3, cols] = gm3[at : at + 1, :]
        downward[2:3, cols] = gm3[at + 1 : at + 2, :]
    up_ref[...] = upward[...].astype(BF)
    down_ref[...] = downward[...].astype(BF)

    cells = 327680
    x = xw3[16:176, :].astype(BF)
    shifted = jnp.concatenate([gm3[9 - i : 169 - i, :] for i in range(3)], axis=1).astype(BF)
    z = lax.dot_general(x, shifted, TN, preferred_element_type=F32) * (cells // 16) ** -0.5
    for i in range(3):
        sums[768 * i : 768 * (i + 1), :] = z[:, 256 * i : 256 * (i + 1)]
    x = xw2[40:680, :].astype(BF)
    shifted = jnp.concatenate([gm2[9 - i : 649 - i, :] for i in range(3)], axis=1).astype(BF)
    z = lax.dot_general(x, shifted, TN, preferred_element_type=F32) * (cells // 4) ** -0.5
    base = 2304
    sums[base : base + 384, 0:128] = z[:, 0:128]
    sums[base + 384 : base + 576, 0:128] = z[0:192, 128:256]
    sums[base : base + 192, 128:256] = z[192:384, 128:256]
    sums[base + 192 : base + 576, 128:256] = z[:, 256:384]
    x = xw1[24:664, :].astype(BF)
    shifted = jnp.concatenate([gm1[9 - i : 649 - i, :] for i in range(3)], axis=1).astype(BF)
    z = lax.dot_general(x, shifted, TN, preferred_element_type=F32) * cells**-0.5
    window = (192, 0, 64, 128)
    blocks = []
    for i in range(3):
        zi = z[:, 128 * i : 128 * (i + 1)]
        for j in range(3):
            a, b = window[j], window[j + 1]
            blocks.append(zi[a : a + 64] + pltpu.roll(zi[b : b + 64], 64, 1))
    blocks.append(jnp.zeros((64, 128), F32))
    pairs = [jnp.where(low, blocks[n], pltpu.roll(blocks[n + 1], 64, 1)) for n in range(0, 10, 2)]
    y2_own, y3_own = y2[32:672], y3.astype(F32)[8:168].astype(BF)
    for y, flat, mask, branch in (
        (y2_own, flat2, own2, 1),
        (y3_own, flat3, own3, 2),
        (y4, flat4, None, 3),
    ):
        masked = (flat if mask is None else jnp.where(mask, flat, 0.0)).astype(BF)
        z = lax.dot_general(masked, y, TN, preferred_element_type=F32) * (cells // 4**branch) ** -0.5
        pairs += [z[0:64, 128 * n : 128 * (n + 1)] for n in range(z.shape[1] // 128)]
    base = 2880
    for n in range(12):
        at, side = base + 64 * (n // 2), 128 * (n % 2)
        sums[at : at + 64, side : side + 128] = pairs[n]
    sums[3264:3328, :] = jnp.zeros((64, 256), F32)
    keep_ref[...] = jnp.where(core == 0, sums[:, 0:128], sums[:, 128:256]).astype(BF)
    send_ref[...] = jnp.where(core == 0, sums[:, 128:256], sums[:, 0:128]).astype(BF)


def rims_kernel(g1_ref, g2_ref, g3_ref, rim_ref, above_ref, below_ref, left_ref, right_ref, out):
    g1, g2, g3, above, below = (ref[...].astype(F32) for ref in (g1_ref, g2_ref, g3_ref, above_ref, below_ref))
    rim = rim_ref[...] + above[3:4, 0:1536] + below[3:4, 0:1536]
    for ref, one, three, four in ((left_ref, 0, 0, 0), (right_ref, WIDE - 128, WIDE - 256, 1408)):
        ones, threes = slice(one, one + 128), slice(three, three + 256)
        out[...] = jnp.zeros_like(out)
        out[0:1, 0:128] = above[0:1, ones]
        out[1:9, 0:128] = g1[:, ones]
        out[9:10, 0:128] = below[0:1, ones]
        out[10:11, 0:128] = above[1:2, ones]
        out[11:15, 0:128] = g2[:, ones]
        out[15:16, 0:128] = below[1:2, ones]
        out[16:17, :] = above[2:3, threes]
        out[17:19, :] = g3[:, threes]
        out[19:20, :] = below[2:3, threes]
        out[20:21, 0:128] = rim[:, four : four + 128]
        ref[...] = out[...].astype(BF)


def backward_kernel(
    g1_ref, g2_ref, g3_ref, rim_ref, above_ref, below_ref, left_ref, right_ref, t1b, k2, k3, p4,
    gf1_ref, gf2_ref, gf3_ref, gf4_ref, wide1, wide2, wide3, xw1, xw2, xw3, out2, out3,
):
    low = lax.broadcasted_iota(jnp.int32, (1, 128), 1) < 64
    for ref, n in ((xw1, 640), (xw2, 320), (xw3, 160)):
        ref[0:8, :] = jnp.zeros((8, ref.shape[1]), F32)
        ref[8 + n : 16 + n, :] = jnp.zeros((8, ref.shape[1]), F32)
    above, below, left, right = (ref[...].astype(F32) for ref in (above_ref, below_ref, left_ref, right_ref))
    for n, (wide, g_ref, top, rows, start, step) in enumerate(
        ((wide1, g1_ref, 3, 8, 0, 128), (wide2, g2_ref, 0, 4, 10, 128), (wide3, g3_ref, 0, 2, 16, 256))
    ):
        wide[...] = jnp.zeros_like(wide)
        mid, end = slice(step, step + WIDE), step + WIDE
        wide[top : top + 1, mid] = above[n : n + 1]
        wide[top + 1 : top + 1 + rows, mid] = g_ref[...].astype(F32)
        wide[top + 1 + rows : top + 2 + rows, mid] = below[n : n + 1]
        wide[top : top + 2 + rows, 0:step] = left[start : start + 2 + rows, 0:step]
        wide[top : top + 2 + rows, end : end + step] = right[start : start + 2 + rows, 0:step]

    for f in range(40):
        at = 8 + 16 * f
        xw1[at : at + 16, 0:128] = tile(wide1, f + 1)
        xw1[at : at + 16, 128:256] = jnp.where(low, tile(wide1, f + 2), tile(wide1, f))
    total = xw1[8:648, 0:128]
    for i in range(3):
        total = total + lax.dot_general(
            xw1[9 - i : 649 - i, :].astype(BF), t1b[i], NT, preferred_element_type=F32
        )
    for f in range(40):
        gf1_ref[:, 128 * f : 128 * (f + 1)] = total[16 * f + 4 : 16 * f + 12].astype(BF)

    for j in range(3):
        for c in range(40):
            xw2[8 + 8 * c : 16 + 8 * c, 128 * j : 128 * j + 128] = tile(wide2, c + 2 - j)
    total = xw2[8:328, 128:256]
    for i in range(3):
        kernel = jnp.concatenate([k2[i, 128 * j : 128 * j + 128, :] for j in range(3)], axis=1)
        total = total + lax.dot_general(
            xw2[9 - i : 329 - i, :].astype(BF), kernel, NT, preferred_element_type=F32
        )
    out2[...] = total
    for c in range(40):
        gf2_ref[:, 128 * c : 128 * (c + 1)] = out2[8 * c + 1 : 8 * c + 5, :].astype(BF)

    for j in range(3):
        for c in range(20):
            first = 256 * (c + 2 - j)
            xw3[8 + 8 * c : 16 + 8 * c, 256 * j : 256 * j + 256] = wide3[:, first : first + 256]
    total = xw3[8:168, 256:512]
    for i in range(3):
        kernel = jnp.concatenate([k3[i, 256 * j : 256 * j + 256, :] for j in range(3)], axis=1)
        total = total + lax.dot_general(
            xw3[9 - i : 169 - i, :].astype(BF), kernel, NT, preferred_element_type=F32
        )
    out3[...] = total
    for c in range(20):
        gf3_ref[:, 256 * c : 256 * (c + 1)] = out3[8 * c + 1 : 8 * c + 3, :].astype(BF)

    rim = rim_ref[...] + above[3:4, 0:1536] + below[3:4, 0:1536]
    for c in range(10):
        cg = rim[:, 128 * (c + 1) : 128 * (c + 2)]
        if c == 0:
            cg = cg + left[20:21, 0:128]
        if c == 9:
            cg = cg + right[20:21, 0:128]
        cg = jnp.broadcast_to(cg[:, 0:64], (8, 64)).astype(BF)
        back = jnp.dot(cg, p4[...], preferred_element_type=F32)
        gf4_ref[0:1, 512 * c : 512 * c + 512] = back[0:1].astype(BF)


def swapped(block, axis, flip):
    return lax.ppermute(block, axis, [(i, i ^ flip) for i in range(lax.axis_size(axis))])


def unpack_kernel(place_ref, mine, got, k1_ref, k2_ref, k3_ref, p2_ref, p3_ref, p4_ref, whole):
    core = place_ref[3]
    whole[:, 0:128] = jnp.where(core == 0, mine[...], got[...])
    whole[:, 128:256] = jnp.where(core == 0, got[...], mine[...])
    k3_ref[...] = whole[0:2304, :]
    k2_ref[0:576, :] = whole[2304:2880, 0:128]
    k2_ref[576:1152, :] = whole[2304:2880, 128:256]
    for n in range(9):
        at, side = 2880 + 64 * (n // 4), 64 * (n % 4)
        k1_ref[64 * n : 64 * (n + 1), :] = whole[at : at + 64, side : side + 64]
    n = 5
    for ref, count in ((p2_ref, 1), (p3_ref, 2), (p4_ref, 4)):
        for m in range(count):
            at, side = 2880 + 64 * (n // 2), 128 * (n % 2)
            ref[:, 128 * m : 128 * (m + 1)] = whole[at : at + 64, side : side + 128]
            n += 1


def call(kernel, out_shapes, scratch, count, scalars=0, far=0):
    vmem = pl.BlockSpec(memory_space=pltpu.VMEM)
    smem = pl.BlockSpec(memory_space=pltpu.SMEM)
    return pl.pallas_call(
        kernel,
        out_shape=[jax.ShapeDtypeStruct(shape, dtype) for shape, dtype in out_shapes],
        in_specs=[smem] * scalars + [vmem] * count + [pl.BlockSpec(memory_space=pl.ANY)] * far,
        out_specs=[vmem] * len(out_shapes),
        scratch_shapes=[pltpu.VMEM(shape, dtype) for shape, dtype in scratch]
        + ([pltpu.SemaphoreType.DMA((far,))] if far else []),
        compiler_params=pltpu.CompilerParams(vmem_limit_bytes=48 * 1024 * 1024),
    )


def pair_weights(kernel_one):
    none = jnp.zeros((3, FEAT_ONE, FEAT_ONE), BF)
    tap = lambda j: kernel_one[:, j] if 0 <= j < 3 else none
    windows = (1, 2, 3, 0)
    ahead = jnp.concatenate(
        [jnp.concatenate([tap(w - e) for w in windows], axis=1) for e in range(2)], axis=2
    )
    back = jnp.concatenate(
        [jnp.concatenate([tap(e - w + 2) for e in range(2)], axis=1) for w in windows], axis=2
    )
    return ahead, back


def local_part(x1, x2, x3, x4, kernel_one, kernel_two, kernel_three, p2, p3, p4, cot):
    place = jnp.stack(
        [
            lax.axis_index(ROWS),
            lax.axis_index(COLS),
            (lax.axis_index(COLS) == lax.axis_size(COLS) - 1).astype(jnp.int32),
            lax.axis_index("core"),
        ]
    ).astype(jnp.int32)
    ahead, back = pair_weights(kernel_one)
    k2 = kernel_two.reshape(3, 384, 128)
    k3 = kernel_three.reshape(3, 768, 256)
    fars = halos(x1, x2, x3, x4, cot) + (ahead, k2, k3)
    total = RIM + WIDE + RIM
    keep, send, g1, g2, g3, rim, up, down = call(
        forward_kernel,
        [
            ((PACK_ROWS, 128), BF), ((PACK_ROWS, 128), BF),
            ((8, WIDE), BF), ((4, WIDE), BF), ((2, WIDE), BF), ((1, 1536), F32),
            ((8, WIDE), BF), ((8, WIDE), BF),
        ],
        [
            ((16, total), F32), ((16, total), F32), ((16, total), F32), ((8, total), F32), ((8, total), F32),
            ((688, 256), F32), ((720, 384), F32), ((192, 768), F32),
            ((672, 128), F32), ((704, 128), F32), ((176, 256), F32),
            ((656, 128), F32), ((656, 128), F32), ((176, 256), F32),
            ((PACK_ROWS, 256), F32), ((8, WIDE), F32), ((8, WIDE), F32),
        ]
        + [(far.shape, BF) for far in fars],
        3,
        1,
        12,
    )(place, p2.T, p3.T, p4.T, *fars)
    return place, keep, send, (g1, g2, g3, rim), up, down, (back, k2, k3, p4.T)


def from_beside(grads, above, below):
    left, right = call(
        rims_kernel, [((32, 256), BF), ((32, 256), BF)], [((32, 256), F32)], 6
    )(*grads, above, below)
    return moved(right, COLS, 1), moved(left, COLS, -1)


def input_grads(grads, above, below, left, right, weights):
    return call(
        backward_kernel,
        [((8, WIDE), BF), ((4, WIDE), BF), ((2, WIDE), BF), ((1, WIDE), BF)],
        [
            ((16, 42 * 128), F32), ((8, 42 * 128), F32), ((8, 22 * 256), F32),
            ((656, 256), F32), ((336, 384), F32), ((176, 768), F32),
            ((320, 128), F32), ((160, 256), F32),
        ],
        12,
    )(*grads, above, below, left, right, *weights)


def unpacked(place, mine, got):
    outs = call(
        unpack_kernel,
        [((576, 64), BF), ((1152, 128), BF), ((2304, 256), BF), ((64, 128), BF), ((64, 256), BF), ((64, 512), BF)],
        [((PACK_ROWS, 256), BF)],
        2,
        1,
    )(place, mine, got)
    return (
        outs[0].reshape(3, 3, 64, 64), outs[1].reshape(3, 3, 128, 128), outs[2].reshape(3, 3, 256, 256),
        outs[3].T, outs[4].T, outs[5].T,
    )


def on_device(*args):
    place, keep, send, grads, up, down, weights = local_part(*args)
    part = (keep.astype(F32) + swapped(send, "core", 1).astype(F32)).astype(BF)
    part, up, down = lax.optimization_barrier((part, up, down))

    pieces = lax.all_to_all(part.reshape(32, -1, 128), SLAB, 0, 0)
    above, below = moved(down, ROWS, 1), moved(up, ROWS, -1)
    part = jnp.sum(pieces.astype(F32), axis=0).astype(BF)

    pieces = lax.all_to_all(jnp.broadcast_to(part[None], (8,) + part.shape), "z_hi", 0, 0)
    part = jnp.sum(pieces.astype(F32), axis=0).astype(BF)
    part, above, below = lax.optimization_barrier((part, above, below))

    pieces = jnp.broadcast_to(part[None], (32,) + part.shape)
    mine = lax.all_to_all(pieces, SLAB, 0, 0).reshape(keep.shape)
    left, right = from_beside(grads, above, below)
    outs = input_grads(grads, above, below, left, right, weights)
    mine, outs = lax.optimization_barrier((mine, outs))
    return tuple(outs) + unpacked(place, mine, swapped(mine, "core", 1))


def solution(mesh):
    mesh = Mesh(mesh.devices.reshape(8, 2, 2, 4, 2, 2), ROWS + COLS)
    split = P(ROWS, COLS)
    in_specs = (split,) * 4 + (P(),) * 6 + (split,)
    out_specs = (split,) * 4 + (P(),) * 6
    return jax.shard_map(on_device, mesh=mesh, in_specs=in_specs, out_specs=out_specs, check_vma=False)
```

```python
import functools

import jax
import jax.numpy as jnp
from jax import lax
from jax.experimental import pallas as pl
from jax.experimental.pallas import tpu as pltpu
from jax.sharding import Mesh
from jax.sharding import PartitionSpec as P

FEAT_ONE = 64
FEAT_TWO = 128
FEAT_THREE = 256
FEAT_FOUR = 512

ROWS = ("z_hi", "z_lo", "x_lo", "y")
COLS = ("x_hi", "core")
SLAB = ("z_lo", "x_lo", "y", "x_hi")
PACK_ROWS = 3328
WIDE = 5120
RIM = 512
BF = jnp.bfloat16
F32 = jnp.float32
NT = (((1,), (1,)), ((), ()))
TN = (((0,), (0,)), ((), ()))


def moved(block, axis, distance):
    count = lax.axis_size(axis)
    route = [(i, i + distance) for i in range(count) if 0 <= i + distance < count]
    return lax.ppermute(block, axis, route)


def stacked(parts, rows):
    total, at = None, 0
    for part in parts:
        padded = jnp.pad(part, ((at, rows - at - part.shape[0]), (0, 0)))
        total = padded if total is None else total + padded
        at += part.shape[0]
    return total


def in_hbm(x):
    return pltpu.with_memory_space_constraint(x, pltpu.HBM)


def edge_rows_kernel(last_ref, first_ref, last, first, near, copies):
    for copy in copies:
        copy.wait()
    x1, cot, x2, x3, x4 = (ref[...].astype(F32) for ref in near)
    for out, ref, ones, cots, twos in (
        (last, last_ref, x1[5:8], cot[6:8], x2[1:4]),
        (first, first_ref, x1[0:3], cot[0:2], x2[0:3]),
    ):
        out[0:3, :] = ones
        out[3:5, :] = cots
        out[5:8, :] = twos
        out[8:10, :] = x3
        out[10:11, :] = x4
        out[11:16, :] = jnp.zeros((5, WIDE), F32)
        ref[...] = out[...].astype(BF)


def halos(x1, x2, x3, x4, cot):
    own = tuple(in_hbm(x) for x in (x1, cot, x2, x3, x4))
    last, first = call(edge_rows_kernel, [((16, WIDE), BF)] * 2, [((16, WIDE), F32)] * 2, *own, far=5)
    above = moved(last, ROWS, 1)
    below = moved(first, ROWS, -1)
    parts = (x1, cot, x2, x3, x4, above[:11], below[:11])
    left = moved(stacked([p[:, -RIM:] for p in parts], 48), COLS, 1)
    right = moved(stacked([p[:, :RIM] for p in parts], 48), COLS, -1)
    return own + (above, below, left, right)


def gelu_both(v):
    c = 0.7978845608028654
    sq = v * v
    t = jnp.tanh(c * v * (1.0 + 0.044715 * sq))
    half = 0.5 * (1.0 + t)
    slope = half + 0.5 * v * (1.0 - t * t) * (c * (1.0 + 3.0 * 0.044715 * sq))
    return v * half, slope


def tile(wide, at):
    return wide[:, 128 * at : 128 * (at + 1)]


def row_weights(shape, coarse_dim, row_block):
    k = lax.broadcasted_iota(jnp.int32, shape, coarse_dim)
    r = lax.broadcasted_iota(jnp.int32, shape, 1 - coarse_dim)
    two, three = k < 16, k < 24
    scale = jnp.where(two, 2, jnp.where(three, 4, 8))
    count = jnp.where(two, 4, jnp.where(three, 2, 1))
    shift = jnp.where(two, 3, jnp.where(three, 16 + 2, 24 + 1))
    total = (jnp.where(two, 512, jnp.where(three, 256, 128)) - 1).astype(F32)
    coarse = (row_block * count + k - shift).astype(F32)
    fine = (row_block * 8 + r - 4).astype(F32)
    inverse = jnp.where(two, 0.5, jnp.where(three, 0.25, 0.125)).astype(F32)
    place = jnp.clip((fine + 0.5) * inverse - 0.5, 0.0, total)
    return jnp.maximum(0.0, 1.0 - jnp.abs(place - coarse))


def forward_kernel(
    place_ref, keep_ref, send_ref, g1_ref, g2_ref, g3_ref, rim_ref, up_ref, down_ref,
    wx1, wc, wx2, wx3, wx4, xw1, xw2, xw3, d1, d2, d3, gm1, gm2, gm3, sums, upward, downward,
    near, copies,
):
    x1, cot, x2, x3, x4, above, below, left, right, t1, k2, k3, p2, p3, p4 = near
    row_block = place_ref[0]
    at_left = place_ref[1] == 0
    at_right = place_ref[2] == 1
    core = place_ref[3]
    lane = lax.broadcasted_iota(jnp.int32, (1, 128), 1)
    low = lane < 64

    def lanes(a, b):
        return jnp.where(low, a, b).astype(F32)

    for ref in (wx1, wc, wx2, wx3, wx4, upward, downward):
        ref[...] = jnp.zeros_like(ref)
    for copy in copies[:10]:
        copy.wait()
    for side, to in ((None, RIM), (left, 0), (right, RIM + WIDE)):
        if side is None:
            cols = slice(to, to + WIDE)
            mid = [ref[...].astype(F32) for ref in (x1, cot, x2, x3, x4)]
            up, down = above[...].astype(F32), below[...].astype(F32)
        else:
            cols = slice(to, to + RIM)
            v = side[...].astype(F32)
            mid = [v[0:8], v[8:16], v[16:20], v[20:22], v[22:23]]
            up, down = v[23:34], v[34:45]
        wx1[1:4, cols] = up[0:3]
        wx1[4:12, cols] = mid[0]
        wx1[12:15, cols] = down[0:3]
        wc[2:4, cols] = up[3:5]
        wc[4:12, cols] = mid[1]
        wc[12:14, cols] = down[3:5]
        wx2[0:3, cols] = up[5:8]
        wx2[3:7, cols] = mid[2]
        wx2[7:10, cols] = down[5:8]
        wx3[0:2, cols] = up[8:10]
        wx3[2:4, cols] = mid[3]
        wx3[4:6, cols] = down[8:10]
        wx4[0:1, cols] = up[10:11]
        wx4[1:2, cols] = mid[4]
        wx4[2:3, cols] = down[10:11]

    for f in range(-1, 41):
        at = 8 + 16 * (f + 1)
        xw1[at : at + 16, 0:128] = tile(wx1, 4 + f)
        xw1[at : at + 16, 128:256] = jnp.where(low, tile(wx1, 5 + f), tile(wx1, 3 + f))
    xw1[0:8, :] = jnp.zeros((8, 256), F32)
    xw1[680:688, :] = jnp.zeros((8, 256), F32)
    pre1 = xw1[8:680, 0:128]
    for i in range(3):
        pre1 = pre1 + jnp.dot(xw1[7 + i : 679 + i, :].astype(BF), t1[i], preferred_element_type=F32)
    y1, slope = gelu_both(pre1)
    y1 = y1.astype(BF).astype(F32)
    d1[...] = slope

    copies[10].wait()
    for j in range(3):
        for c in range(-2, 42):
            at = 8 + 16 * (c + 2)
            xw2[at : at + 16, 128 * j : 128 * j + 128] = tile(wx2, 3 + c + j)
    xw2[0:8, :] = jnp.zeros((8, 384), F32)
    xw2[712:720, :] = jnp.zeros((8, 384), F32)
    pre2 = xw2[8:712, 128:256]
    for i in range(3):
        pre2 = pre2 + jnp.dot(xw2[7 + i : 711 + i, :].astype(BF), k2[i], preferred_element_type=F32)
    y2, slope = gelu_both(pre2)
    y2 = y2.astype(BF)
    d2[...] = slope

    copies[11].wait()
    for j in range(3):
        for c in range(-1, 21):
            at = 8 + 8 * (c + 1)
            first = RIM + 256 * (c + j - 1)
            xw3[at : at + 8, 256 * j : 256 * j + 256] = wx3[:, first : first + 256]
    xw3[0:8, :] = jnp.zeros((8, 768), F32)
    xw3[184:192, :] = jnp.zeros((8, 768), F32)
    pre3 = xw3[8:184, 256:512]
    for i in range(3):
        pre3 = pre3 + jnp.dot(xw3[7 + i : 183 + i, :].astype(BF), k3[i], preferred_element_type=F32)
    y3, slope = gelu_both(pre3)
    y3 = y3.astype(BF)
    d3[...] = slope

    y4 = jnp.concatenate([wx4[:, 512 * c : 512 * c + 512] for c in range(12)], axis=0).astype(BF)

    for copy in copies[12:]:
        copy.wait()
    weights = row_weights((16, 32), 1, row_block).astype(BF)
    rows_up = []
    for y, p, rim, rows, wlo in ((y2, p2, 2, 16, 0), (y3, p3, 1, 8, 16), (y4, p4, 1, 8, 24)):
        twice = jnp.concatenate([p[...], p[...]], axis=0)
        coarse = lax.dot_general(y, twice, NT, preferred_element_type=F32).astype(BF).astype(F32)
        cols = [coarse[rows * n : rows * (n + 1)] for n in range(coarse.shape[0] // rows)]
        end = len(cols) - rim
        cols[rim - 1] = jnp.where(at_left, cols[rim], cols[rim - 1])
        cols[end] = jnp.where(at_right, cols[end - 1], cols[end])
        flat = jnp.concatenate(cols, axis=1).astype(BF)
        rows_up.append(jnp.dot(weights[:, wlo : wlo + rows], flat, preferred_element_type=F32))
    up2, up3, up4 = rows_up

    gates = []
    for f in range(-1, 41):
        k = f + 2
        merged = y1[16 * (f + 1) : 16 * (f + 2)]
        merged = merged + 0.75 * tile(up2, k) + 0.25 * jnp.where(low, tile(up2, k - 1), tile(up2, k + 1))
        k, h = f // 2 + 1, f % 2
        if h == 0:
            merged = merged + lanes(0.375, 0.125) * tile(up3, k - 1) + lanes(0.625, 0.875) * tile(up3, k)
        else:
            merged = merged + lanes(0.875, 0.625) * tile(up3, k) + lanes(0.125, 0.375) * tile(up3, k + 1)
        k, h = f // 4 + 1, f % 4
        p_low, p_high = (2 * h + 0.5) / 8 - 0.5, (2 * h + 1.5) / 8 - 0.5
        other = k - 1 if h < 2 else k + 1
        merged = merged + lanes(1 - abs(p_low), 1 - abs(p_high)) * tile(up4, k)
        merged = merged + lanes(abs(p_low), abs(p_high)) * tile(up4, other)
        slope = gelu_both(merged)[1]
        gate = (slope * tile(wc, 4 + f)).astype(BF).astype(F32)
        gates.append(gate)
        if 0 <= f < 40:
            g = (d1[16 * (f + 1) : 16 * (f + 2)] * gate).astype(BF).astype(F32)
            row = lax.broadcasted_iota(jnp.int32, (16, 1), 0)
            gm1[8 + 16 * f : 24 + 16 * f, :] = jnp.where((row >= 4) & (row < 12), g, 0.0)
            cols = slice(128 * f, 128 * (f + 1))
            g1_ref[:, cols] = g[4:12].astype(BF)
            upward[0:1, cols] = g[4:5]
            downward[0:1, cols] = g[11:12]
    gm1[0:8, :] = jnp.zeros((8, 128), F32)
    gm1[648:656, :] = jnp.zeros((8, 128), F32)

    flat = jnp.concatenate(gates, axis=1).astype(BF)
    weights_back = row_weights((32, 16), 0, row_block)
    k = lax.broadcasted_iota(jnp.int32, (32, 16), 0)
    r = lax.broadcasted_iota(jnp.int32, (32, 16), 1)
    weights_back = jnp.where((k < 24) | ((r >= 4) & (r < 12)), weights_back, 0.0).astype(BF)
    down = jnp.dot(weights_back, flat, preferred_element_type=F32)
    down2, down3, down4 = down[0:16], down[16:24], down[24:32]

    def folded(v):
        return v + pltpu.roll(v, 64, 1)

    cg2 = []
    for c in range(40):
        v = 0.75 * tile(down2, c + 1) + 0.25 * jnp.where(low, tile(down2, c + 2), tile(down2, c))
        if c == 0:
            v = v + jnp.where(at_left, lanes(0.25, 0.0) * tile(down2, 1), 0.0)
        if c == 39:
            v = v + jnp.where(at_right, lanes(0.0, 0.25) * tile(down2, 40), 0.0)
        cg2.append(folded(v))
    cg3 = []
    for c in range(20):
        at = 2 * c
        v = lanes(0.125, 0.375) * tile(down3, at) + lanes(0.625, 0.875) * tile(down3, at + 1)
        v = v + lanes(0.875, 0.625) * tile(down3, at + 2) + lanes(0.375, 0.125) * tile(down3, at + 3)
        if c == 0:
            v = v + jnp.where(at_left, lanes(0.375, 0.125) * tile(down3, 1), 0.0)
        if c == 19:
            v = v + jnp.where(at_right, lanes(0.125, 0.375) * tile(down3, 40), 0.0)
        cg3.append(folded(v))
    cg4 = []
    for c in range(-1, 11):
        v = jnp.zeros((8, 128), F32)
        for n in range(8):
            a, b = (2 * n + 0.5) / 8, (2 * n + 1.5) / 8
            a, b = (a, b) if n < 4 else (2 - a, 2 - b)
            pair = 4 * c - 2 + n
            if 0 <= pair < 40:
                v = v + lanes(a, b) * tile(down4, pair + 1)
        cg4.append(folded(v))
    cg4[1] = cg4[1] + jnp.where(at_left, cg4[0], 0.0)
    cg4[-2] = cg4[-2] + jnp.where(at_right, cg4[-1], 0.0)
    cg4[0] = jnp.where(at_left, 0.0, cg4[0])
    cg4[-1] = jnp.where(at_right, 0.0, cg4[-1])
    for n in range(12):
        cols = slice(128 * n, 128 * (n + 1))
        upward[3:4, cols] = cg4[n][0:1]
        rim_ref[0:1, cols] = cg4[n][1:2]
        downward[3:4, cols] = cg4[n][2:3]

    flat2 = jnp.concatenate(cg2, axis=0).astype(BF).astype(F32)
    flat3 = jnp.concatenate(cg3, axis=0).astype(BF).astype(F32)
    flat4 = jnp.concatenate(cg4, axis=0).astype(BF).astype(F32)
    back2 = jnp.dot(flat2[:, 0:64].astype(BF), p2[...], preferred_element_type=F32)
    back3 = jnp.dot(flat3[:, 0:64].astype(BF), p3[...], preferred_element_type=F32)
    g2 = (d2[32:672, :] * back2).astype(BF).astype(F32)
    g3 = (d3[8:168, :] * back3).astype(BF).astype(F32)

    row2 = lax.broadcasted_iota(jnp.int32, (640, 1), 0) % 16
    own2 = (row2 >= 3) & (row2 < 7)
    row3 = lax.broadcasted_iota(jnp.int32, (160, 1), 0) % 8
    own3 = (row3 >= 2) & (row3 < 4)
    gm2[0:8, :] = jnp.zeros((8, 128), F32)
    gm2[8:648, :] = jnp.where(own2, g2, 0.0)
    gm2[648:656, :] = jnp.zeros((8, 128), F32)
    gm3[0:8, :] = jnp.zeros((8, 256), F32)
    gm3[8:168, :] = jnp.where(own3, g3, 0.0)
    gm3[168:176, :] = jnp.zeros((8, 256), F32)
    for c in range(40):
        at, cols = 8 + 16 * c + 3, slice(128 * c, 128 * (c + 1))
        g2_ref[:, cols] = gm2[at : at + 4, :].astype(BF)
        upward[1:2, cols] = gm2[at : at + 1, :]
        downward[1:2, cols] = gm2[at + 3 : at + 4, :]
    for c in range(20):
        at, cols = 8 + 8 * c + 2, slice(256 * c, 256 * (c + 1))
        g3_ref[:, cols] = gm3[at : at + 2, :].astype(BF)
        upward[2:3, cols] = gm3[at : at + 1, :]
        downward[2:3, cols] = gm3[at + 1 : at + 2, :]
    up_ref[...] = upward[...].astype(BF)
    down_ref[...] = downward[...].astype(BF)

    cells = 327680
    x = xw3[16:176, :].astype(BF)
    shifted = jnp.concatenate([gm3[9 - i : 169 - i, :] for i in range(3)], axis=1).astype(BF)
    z = lax.dot_general(x, shifted, TN, preferred_element_type=F32) * (cells // 16) ** -0.5
    for i in range(3):
        sums[768 * i : 768 * (i + 1), :] = z[:, 256 * i : 256 * (i + 1)]
    x = xw2[40:680, :].astype(BF)
    shifted = jnp.concatenate([gm2[9 - i : 649 - i, :] for i in range(3)], axis=1).astype(BF)
    z = lax.dot_general(x, shifted, TN, preferred_element_type=F32) * (cells // 4) ** -0.5
    base = 2304
    sums[base : base + 384, 0:128] = z[:, 0:128]
    sums[base + 384 : base + 576, 0:128] = z[0:192, 128:256]
    sums[base : base + 192, 128:256] = z[192:384, 128:256]
    sums[base + 192 : base + 576, 128:256] = z[:, 256:384]
    x = xw1[24:664, :].astype(BF)
    shifted = jnp.concatenate([gm1[9 - i : 649 - i, :] for i in range(3)], axis=1).astype(BF)
    z = lax.dot_general(x, shifted, TN, preferred_element_type=F32) * cells**-0.5
    window = (192, 0, 64, 128)
    blocks = []
    for i in range(3):
        zi = z[:, 128 * i : 128 * (i + 1)]
        for j in range(3):
            a, b = window[j], window[j + 1]
            blocks.append(zi[a : a + 64] + pltpu.roll(zi[b : b + 64], 64, 1))
    blocks.append(jnp.zeros((64, 128), F32))
    pairs = [jnp.where(low, blocks[n], pltpu.roll(blocks[n + 1], 64, 1)) for n in range(0, 10, 2)]
    y2_own, y3_own = y2[32:672], y3.astype(F32)[8:168].astype(BF)
    for y, flat, mask, branch in (
        (y2_own, flat2, own2, 1),
        (y3_own, flat3, own3, 2),
        (y4, flat4, None, 3),
    ):
        masked = (flat if mask is None else jnp.where(mask, flat, 0.0)).astype(BF)
        z = lax.dot_general(masked, y, TN, preferred_element_type=F32) * (cells // 4**branch) ** -0.5
        pairs += [z[0:64, 128 * n : 128 * (n + 1)] for n in range(z.shape[1] // 128)]
    base = 2880
    for n in range(12):
        at, side = base + 64 * (n // 2), 128 * (n % 2)
        sums[at : at + 64, side : side + 128] = pairs[n]
    sums[3264:3328, :] = jnp.zeros((64, 256), F32)
    keep_ref[...] = jnp.where(core == 0, sums[:, 0:128], sums[:, 128:256]).astype(BF)
    send_ref[...] = jnp.where(core == 0, sums[:, 128:256], sums[:, 0:128]).astype(BF)


def rims_kernel(g1_ref, g2_ref, g3_ref, rim_ref, above_ref, below_ref, left_ref, right_ref, out):
    g1, g2, g3, above, below = (ref[...].astype(F32) for ref in (g1_ref, g2_ref, g3_ref, above_ref, below_ref))
    rim = rim_ref[...] + above[3:4, 0:1536] + below[3:4, 0:1536]
    for ref, one, three, four in ((left_ref, 0, 0, 0), (right_ref, WIDE - 128, WIDE - 256, 1408)):
        ones, threes = slice(one, one + 128), slice(three, three + 256)
        out[...] = jnp.zeros_like(out)
        out[0:1, 0:128] = above[0:1, ones]
        out[1:9, 0:128] = g1[:, ones]
        out[9:10, 0:128] = below[0:1, ones]
        out[10:11, 0:128] = above[1:2, ones]
        out[11:15, 0:128] = g2[:, ones]
        out[15:16, 0:128] = below[1:2, ones]
        out[16:17, :] = above[2:3, threes]
        out[17:19, :] = g3[:, threes]
        out[19:20, :] = below[2:3, threes]
        out[20:21, 0:128] = rim[:, four : four + 128]
        ref[...] = out[...].astype(BF)


def backward_kernel(
    g1_ref, g2_ref, g3_ref, rim_ref, above_ref, below_ref, left_ref, right_ref,
    gf1_ref, gf2_ref, gf3_ref, gf4_ref, wide1, wide2, wide3, xw1, xw2, xw3, out2, out3, near, copies,
):
    t1b, k2, k3, p4 = near
    low = lax.broadcasted_iota(jnp.int32, (1, 128), 1) < 64
    for ref, n in ((xw1, 640), (xw2, 320), (xw3, 160)):
        ref[0:8, :] = jnp.zeros((8, ref.shape[1]), F32)
        ref[8 + n : 16 + n, :] = jnp.zeros((8, ref.shape[1]), F32)
    above, below, left, right = (ref[...].astype(F32) for ref in (above_ref, below_ref, left_ref, right_ref))
    for n, (wide, g_ref, top, rows, start, step) in enumerate(
        ((wide1, g1_ref, 3, 8, 0, 128), (wide2, g2_ref, 0, 4, 10, 128), (wide3, g3_ref, 0, 2, 16, 256))
    ):
        wide[...] = jnp.zeros_like(wide)
        mid, end = slice(step, step + WIDE), step + WIDE
        wide[top : top + 1, mid] = above[n : n + 1]
        wide[top + 1 : top + 1 + rows, mid] = g_ref[...].astype(F32)
        wide[top + 1 + rows : top + 2 + rows, mid] = below[n : n + 1]
        wide[top : top + 2 + rows, 0:step] = left[start : start + 2 + rows, 0:step]
        wide[top : top + 2 + rows, end : end + step] = right[start : start + 2 + rows, 0:step]

    for copy in copies:
        copy.wait()
    for f in range(40):
        at = 8 + 16 * f
        xw1[at : at + 16, 0:128] = tile(wide1, f + 1)
        xw1[at : at + 16, 128:256] = jnp.where(low, tile(wide1, f + 2), tile(wide1, f))
    total = xw1[8:648, 0:128]
    for i in range(3):
        total = total + lax.dot_general(
            xw1[9 - i : 649 - i, :].astype(BF), t1b[i], NT, preferred_element_type=F32
        )
    for f in range(40):
        gf1_ref[:, 128 * f : 128 * (f + 1)] = total[16 * f + 4 : 16 * f + 12].astype(BF)

    for j in range(3):
        for c in range(40):
            xw2[8 + 8 * c : 16 + 8 * c, 128 * j : 128 * j + 128] = tile(wide2, c + 2 - j)
    total = xw2[8:328, 128:256]
    for i in range(3):
        kernel = jnp.concatenate([k2[i, 128 * j : 128 * j + 128, :] for j in range(3)], axis=1)
        total = total + lax.dot_general(
            xw2[9 - i : 329 - i, :].astype(BF), kernel, NT, preferred_element_type=F32
        )
    out2[...] = total
    for c in range(40):
        gf2_ref[:, 128 * c : 128 * (c + 1)] = out2[8 * c + 1 : 8 * c + 5, :].astype(BF)

    for j in range(3):
        for c in range(20):
            first = 256 * (c + 2 - j)
            xw3[8 + 8 * c : 16 + 8 * c, 256 * j : 256 * j + 256] = wide3[:, first : first + 256]
    total = xw3[8:168, 256:512]
    for i in range(3):
        kernel = jnp.concatenate([k3[i, 256 * j : 256 * j + 256, :] for j in range(3)], axis=1)
        total = total + lax.dot_general(
            xw3[9 - i : 169 - i, :].astype(BF), kernel, NT, preferred_element_type=F32
        )
    out3[...] = total
    for c in range(20):
        gf3_ref[:, 256 * c : 256 * (c + 1)] = out3[8 * c + 1 : 8 * c + 3, :].astype(BF)

    rim = rim_ref[...] + above[3:4, 0:1536] + below[3:4, 0:1536]
    for c in range(10):
        cg = rim[:, 128 * (c + 1) : 128 * (c + 2)]
        if c == 0:
            cg = cg + left[20:21, 0:128]
        if c == 9:
            cg = cg + right[20:21, 0:128]
        cg = jnp.broadcast_to(cg[:, 0:64], (8, 64)).astype(BF)
        back = jnp.dot(cg, p4[...], preferred_element_type=F32)
        gf4_ref[0:1, 512 * c : 512 * c + 512] = back[0:1].astype(BF)


def swapped(block, axis, flip):
    return lax.ppermute(block, axis, [(i, i ^ flip) for i in range(lax.axis_size(axis))])


def unpack_kernel(place_ref, mine, got, k1_ref, k2_ref, k3_ref, p2_ref, p3_ref, p4_ref, whole):
    core = place_ref[3]
    whole[:, 0:128] = jnp.where(core == 0, mine[...], got[...])
    whole[:, 128:256] = jnp.where(core == 0, got[...], mine[...])
    k3_ref[...] = whole[0:2304, :]
    k2_ref[0:576, :] = whole[2304:2880, 0:128]
    k2_ref[576:1152, :] = whole[2304:2880, 128:256]
    for n in range(9):
        at, side = 2880 + 64 * (n // 4), 64 * (n % 4)
        k1_ref[64 * n : 64 * (n + 1), :] = whole[at : at + 64, side : side + 64]
    n = 5
    for ref, count in ((p2_ref, 1), (p3_ref, 2), (p4_ref, 4)):
        for m in range(count):
            at, side = 2880 + 64 * (n // 2), 128 * (n % 2)
            ref[:, 128 * m : 128 * (m + 1)] = whole[at : at + 64, side : side + 128]
            n += 1


def call(kernel, out_shapes, scratch, *operands, scalars=0, far=0):
    near = len(operands) - scalars - far
    specs = [pl.BlockSpec(memory_space=space) for space in (pltpu.SMEM, pltpu.VMEM, pl.ANY)]
    outs = len(out_shapes)

    def body(*refs):
        first, last = scalars + near, scalars + near + far
        sources = refs[first:last]
        if far:
            buffers, sems = refs[-1 - far : -1], refs[-1]
            copies = [pltpu.make_async_copy(sources[n], buffers[n], sems.at[n]) for n in range(far)]
            for copy in copies:
                copy.start()
            kernel(*refs[:first], *refs[last : -1 - far], buffers, copies)
        else:
            kernel(*refs)

    return pl.pallas_call(
        body,
        out_shape=[jax.ShapeDtypeStruct(shape, dtype) for shape, dtype in out_shapes],
        in_specs=[specs[0]] * scalars + [specs[1]] * near + [specs[2]] * far,
        out_specs=[specs[1]] * outs,
        scratch_shapes=[pltpu.VMEM(shape, dtype) for shape, dtype in scratch]
        + [pltpu.VMEM(operand.shape, operand.dtype) for operand in operands[len(operands) - far :]]
        + ([pltpu.SemaphoreType.DMA((far,))] if far else []),
        compiler_params=pltpu.CompilerParams(vmem_limit_bytes=48 * 1024 * 1024),
    )(*operands)


def pair_weights(kernel_one):
    none = jnp.zeros((3, FEAT_ONE, FEAT_ONE), BF)
    tap = lambda j: kernel_one[:, j] if 0 <= j < 3 else none
    windows = (1, 2, 3, 0)
    ahead = jnp.concatenate(
        [jnp.concatenate([tap(w - e) for w in windows], axis=1) for e in range(2)], axis=2
    )
    back = jnp.concatenate(
        [jnp.concatenate([tap(e - w + 2) for e in range(2)], axis=1) for w in windows], axis=2
    )
    return ahead, back


def local_part(x1, x2, x3, x4, kernel_one, kernel_two, kernel_three, p2, p3, p4, cot):
    place = jnp.stack(
        [
            lax.axis_index(ROWS),
            lax.axis_index(COLS),
            (lax.axis_index(COLS) == lax.axis_size(COLS) - 1).astype(jnp.int32),
            lax.axis_index("core"),
        ]
    ).astype(jnp.int32)
    ahead, back = pair_weights(kernel_one)
    k2 = in_hbm(kernel_two.reshape(3, 384, 128))
    k3 = in_hbm(kernel_three.reshape(3, 768, 256))
    fars = halos(x1, x2, x3, x4, cot) + (ahead, k2, k3, in_hbm(p2.T), in_hbm(p3.T), in_hbm(p4.T))
    total = RIM + WIDE + RIM
    keep, send, g1, g2, g3, rim, up, down = call(
        forward_kernel,
        [
            ((PACK_ROWS, 128), BF), ((PACK_ROWS, 128), BF),
            ((8, WIDE), BF), ((4, WIDE), BF), ((2, WIDE), BF), ((1, 1536), F32),
            ((8, WIDE), BF), ((8, WIDE), BF),
        ],
        [
            ((16, total), F32), ((16, total), F32), ((16, total), F32), ((8, total), F32), ((8, total), F32),
            ((688, 256), F32), ((720, 384), F32), ((192, 768), F32),
            ((672, 128), F32), ((704, 128), F32), ((176, 256), F32),
            ((656, 128), F32), ((656, 128), F32), ((176, 256), F32),
            ((PACK_ROWS, 256), F32), ((8, WIDE), F32), ((8, WIDE), F32),
        ],
        place,
        *fars,
        scalars=1,
        far=15,
    )
    return place, keep, send, (g1, g2, g3, rim), up, down, (back, k2, k3, in_hbm(p4.T))


def from_beside(grads, above, below):
    left, right = call(
        rims_kernel, [((32, 256), BF), ((32, 256), BF)], [((32, 256), F32)], *grads, above, below
    )
    return moved(right, COLS, 1), moved(left, COLS, -1)


def input_grads(grads, above, below, left, right, weights):
    return call(
        backward_kernel,
        [((8, WIDE), BF), ((4, WIDE), BF), ((2, WIDE), BF), ((1, WIDE), BF)],
        [
            ((16, 42 * 128), F32), ((8, 42 * 128), F32), ((8, 22 * 256), F32),
            ((656, 256), F32), ((336, 384), F32), ((176, 768), F32),
            ((320, 128), F32), ((160, 256), F32),
        ],
        *grads, above, below, left, right,
        *weights,
        far=4,
    )


def unpacked(place, mine, got):
    outs = call(
        unpack_kernel,
        [((576, 64), BF), ((1152, 128), BF), ((2304, 256), BF), ((64, 128), BF), ((64, 256), BF), ((64, 512), BF)],
        [((PACK_ROWS, 256), BF)],
        place, mine, got,
        scalars=1,
    )
    return (
        outs[0].reshape(3, 3, 64, 64), outs[1].reshape(3, 3, 128, 128), outs[2].reshape(3, 3, 256, 256),
        outs[3].T, outs[4].T, outs[5].T,
    )


def on_device(*args):
    place, keep, send, grads, up, down, weights = local_part(*args)
    part = (keep.astype(F32) + swapped(send, "core", 1).astype(F32)).astype(BF)
    part, up, down = lax.optimization_barrier((part, up, down))

    pieces = lax.all_to_all(part.reshape(32, -1, 128), SLAB, 0, 0)
    above, below = moved(down, ROWS, 1), moved(up, ROWS, -1)
    part = jnp.sum(pieces.astype(F32), axis=0).astype(BF)

    pieces = lax.all_to_all(jnp.broadcast_to(part[None], (8,) + part.shape), "z_hi", 0, 0)
    part = jnp.sum(pieces.astype(F32), axis=0).astype(BF)
    part, above, below = lax.optimization_barrier((part, above, below))

    pieces = jnp.broadcast_to(part[None], (32,) + part.shape)
    mine = lax.all_to_all(pieces, SLAB, 0, 0).reshape(keep.shape)
    left, right = from_beside(grads, above, below)
    outs = input_grads(grads, above, below, left, right, weights)
    mine, outs = lax.optimization_barrier((mine, outs))
    return tuple(outs) + unpacked(place, mine, swapped(mine, "core", 1))


def solution(mesh):
    mesh = Mesh(mesh.devices.reshape(8, 2, 2, 4, 2, 2), ROWS + COLS)
    split = P(ROWS, COLS)
    in_specs = (split,) * 4 + (P(),) * 6 + (split,)
    out_specs = (split,) * 4 + (P(),) * 6
    return jax.shard_map(on_device, mesh=mesh, in_specs=in_specs, out_specs=out_specs, check_vma=False)
```

```python
import functools

import jax
import jax.numpy as jnp
from jax import lax
from jax.experimental import pallas as pl
from jax.experimental.pallas import tpu as pltpu
from jax.sharding import Mesh
from jax.sharding import PartitionSpec as P

FEAT_ONE = 64
FEAT_TWO = 128
FEAT_THREE = 256
FEAT_FOUR = 512

ROWS = ("z_hi", "z_lo", "x_lo", "y")
COLS = ("x_hi", "core")
SLAB = ("z_lo", "x_lo", "y", "x_hi")
PACK_ROWS = 3328
WIDE = 5120
RIM = 512
BF = jnp.bfloat16
F32 = jnp.float32
NT = (((1,), (1,)), ((), ()))
TN = (((0,), (0,)), ((), ()))


def moved(block, axis, distance):
    count = lax.axis_size(axis)
    route = [(i, i + distance) for i in range(count) if 0 <= i + distance < count]
    return lax.ppermute(block, axis, route)


def stacked(parts, rows):
    total, at = None, 0
    for part in parts:
        padded = jnp.pad(part, ((at, rows - at - part.shape[0]), (0, 0)))
        total = padded if total is None else total + padded
        at += part.shape[0]
    return total


def in_hbm(x):
    return pltpu.with_memory_space_constraint(x, pltpu.HBM)


def edge_kernel(last_ref, first_ref, right_ref, left_ref, last, first, edge, near, copies):
    for copy in copies:
        copy.wait()
    x1, cot, x2, x3, x4 = (ref[...].astype(F32) for ref in near)
    for out, ref, ones, cots, twos in (
        (last, last_ref, x1[5:8], cot[6:8], x2[1:4]),
        (first, first_ref, x1[0:3], cot[0:2], x2[0:3]),
    ):
        out[0:3, :] = ones
        out[3:5, :] = cots
        out[5:8, :] = twos
        out[8:10, :] = x3
        out[10:11, :] = x4
        out[11:16, :] = jnp.zeros((5, WIDE), F32)
        ref[...] = out[...].astype(BF)
    edge[...] = jnp.zeros_like(edge)
    for ref, cols in ((right_ref, slice(WIDE - RIM, WIDE)), (left_ref, slice(0, RIM))):
        edge[0:8, :] = x1[:, cols]
        edge[8:16, :] = cot[:, cols]
        edge[16:20, :] = x2[:, cols]
        edge[20:22, :] = x3[:, cols]
        edge[22:23, :] = x4[:, cols]
        ref[...] = edge[...].astype(BF)


def halos(x1, x2, x3, x4, cot):
    own = tuple(in_hbm(x) for x in (x1, cot, x2, x3, x4))
    last, first, right_edge, left_edge = call(
        edge_kernel,
        [((16, WIDE), BF), ((16, WIDE), BF), ((24, RIM), BF), ((24, RIM), BF)],
        [((16, WIDE), F32), ((16, WIDE), F32), ((24, RIM), F32)],
        *own,
        far=5,
    )
    above = moved(last, ROWS, 1)
    below = moved(first, ROWS, -1)
    left = moved(stacked((right_edge, above[:11, -RIM:], below[:11, -RIM:]), 48), COLS, 1)
    right = moved(stacked((left_edge, above[:11, :RIM], below[:11, :RIM]), 48), COLS, -1)
    return own + (above, below, left, right)


def gelu_both(v):
    c = 0.7978845608028654
    sq = v * v
    t = jnp.tanh(c * v * (1.0 + 0.044715 * sq))
    half = 0.5 * (1.0 + t)
    slope = half + 0.5 * v * (1.0 - t * t) * (c * (1.0 + 3.0 * 0.044715 * sq))
    return v * half, slope


def tile(wide, at):
    return wide[:, 128 * at : 128 * (at + 1)]


def row_weights(shape, coarse_dim, row_block):
    k = lax.broadcasted_iota(jnp.int32, shape, coarse_dim)
    r = lax.broadcasted_iota(jnp.int32, shape, 1 - coarse_dim)
    two, three = k < 16, k < 24
    scale = jnp.where(two, 2, jnp.where(three, 4, 8))
    count = jnp.where(two, 4, jnp.where(three, 2, 1))
    shift = jnp.where(two, 3, jnp.where(three, 16 + 2, 24 + 1))
    total = (jnp.where(two, 512, jnp.where(three, 256, 128)) - 1).astype(F32)
    coarse = (row_block * count + k - shift).astype(F32)
    fine = (row_block * 8 + r - 4).astype(F32)
    inverse = jnp.where(two, 0.5, jnp.where(three, 0.25, 0.125)).astype(F32)
    place = jnp.clip((fine + 0.5) * inverse - 0.5, 0.0, total)
    return jnp.maximum(0.0, 1.0 - jnp.abs(place - coarse))


def forward_kernel(
    place_ref, keep_ref, send_ref, g1_ref, g2_ref, g3_ref, rim_ref, up_ref, down_ref,
    wx1, wc, wx2, wx3, wx4, xw1, xw2, xw3, d1, d2, d3, gm1, gm2, gm3, upward, downward,
    near, copies,
):
    x1, cot, x2, x3, x4, above, below, left, right, t1, k2, k3, p2, p3, p4 = near
    row_block = place_ref[0]
    at_left = place_ref[1] == 0
    at_right = place_ref[2] == 1
    core = place_ref[3]
    lane = lax.broadcasted_iota(jnp.int32, (1, 128), 1)
    low = lane < 64

    def lanes(a, b):
        return jnp.where(low, a, b).astype(F32)

    for ref in (wx1, wc, wx2, wx3, wx4, upward, downward):
        ref[...] = jnp.zeros_like(ref)
    for copy in copies[:10]:
        copy.wait()
    for side, to in ((None, RIM), (left, 0), (right, RIM + WIDE)):
        if side is None:
            cols = slice(to, to + WIDE)
            mid = [ref[...].astype(F32) for ref in (x1, cot, x2, x3, x4)]
            up, down = above[...].astype(F32), below[...].astype(F32)
        else:
            cols = slice(to, to + RIM)
            v = side[...].astype(F32)
            mid = [v[0:8], v[8:16], v[16:20], v[20:22], v[22:23]]
            up, down = v[24:35], v[35:46]
        wx1[1:4, cols] = up[0:3]
        wx1[4:12, cols] = mid[0]
        wx1[12:15, cols] = down[0:3]
        wc[2:4, cols] = up[3:5]
        wc[4:12, cols] = mid[1]
        wc[12:14, cols] = down[3:5]
        wx2[0:3, cols] = up[5:8]
        wx2[3:7, cols] = mid[2]
        wx2[7:10, cols] = down[5:8]
        wx3[0:2, cols] = up[8:10]
        wx3[2:4, cols] = mid[3]
        wx3[4:6, cols] = down[8:10]
        wx4[0:1, cols] = up[10:11]
        wx4[1:2, cols] = mid[4]
        wx4[2:3, cols] = down[10:11]

    for f in range(-1, 41):
        at = 8 + 16 * (f + 1)
        xw1[at : at + 16, 0:128] = tile(wx1, 4 + f)
        xw1[at : at + 16, 128:256] = jnp.where(low, tile(wx1, 5 + f), tile(wx1, 3 + f))
    xw1[0:8, :] = jnp.zeros((8, 256), F32)
    xw1[680:688, :] = jnp.zeros((8, 256), F32)
    pre1 = xw1[8:680, 0:128]
    for i in range(3):
        pre1 = pre1 + jnp.dot(xw1[7 + i : 679 + i, :].astype(BF), t1[i], preferred_element_type=F32)
    y1, slope = gelu_both(pre1)
    y1 = y1.astype(BF).astype(F32)
    d1[...] = slope

    copies[10].wait()
    for j in range(3):
        for c in range(-2, 42):
            at = 8 + 16 * (c + 2)
            xw2[at : at + 16, 128 * j : 128 * j + 128] = tile(wx2, 3 + c + j)
    xw2[0:8, :] = jnp.zeros((8, 384), F32)
    xw2[712:720, :] = jnp.zeros((8, 384), F32)
    pre2 = xw2[8:712, 128:256]
    for i in range(3):
        pre2 = pre2 + jnp.dot(xw2[7 + i : 711 + i, :].astype(BF), k2[i], preferred_element_type=F32)
    y2, slope = gelu_both(pre2)
    y2 = y2.astype(BF)
    d2[...] = slope

    copies[11].wait()
    for j in range(3):
        for c in range(-1, 21):
            at = 8 + 8 * (c + 1)
            first = RIM + 256 * (c + j - 1)
            xw3[at : at + 8, 256 * j : 256 * j + 256] = wx3[:, first : first + 256]
    xw3[0:8, :] = jnp.zeros((8, 768), F32)
    xw3[184:192, :] = jnp.zeros((8, 768), F32)
    pre3 = xw3[8:184, 256:512]
    for i in range(3):
        pre3 = pre3 + jnp.dot(xw3[7 + i : 183 + i, :].astype(BF), k3[i], preferred_element_type=F32)
    y3, slope = gelu_both(pre3)
    y3 = y3.astype(BF)
    d3[...] = slope

    y4 = jnp.concatenate([wx4[:, 512 * c : 512 * c + 512] for c in range(12)], axis=0).astype(BF)

    for copy in copies[12:]:
        copy.wait()
    weights = row_weights((16, 32), 1, row_block).astype(BF)
    rows_up = []
    for y, p, rim, rows, wlo in ((y2, p2, 2, 16, 0), (y3, p3, 1, 8, 16), (y4, p4, 1, 8, 24)):
        twice = jnp.concatenate([p[...], p[...]], axis=0)
        coarse = lax.dot_general(y, twice, NT, preferred_element_type=F32).astype(BF).astype(F32)
        cols = [coarse[rows * n : rows * (n + 1)] for n in range(coarse.shape[0] // rows)]
        end = len(cols) - rim
        cols[rim - 1] = jnp.where(at_left, cols[rim], cols[rim - 1])
        cols[end] = jnp.where(at_right, cols[end - 1], cols[end])
        flat = jnp.concatenate(cols, axis=1).astype(BF)
        rows_up.append(jnp.dot(weights[:, wlo : wlo + rows], flat, preferred_element_type=F32))
    up2, up3, up4 = rows_up

    gates = []
    for f in range(-1, 41):
        k = f + 2
        merged = y1[16 * (f + 1) : 16 * (f + 2)]
        merged = merged + 0.75 * tile(up2, k) + 0.25 * jnp.where(low, tile(up2, k - 1), tile(up2, k + 1))
        k, h = f // 2 + 1, f % 2
        if h == 0:
            merged = merged + lanes(0.375, 0.125) * tile(up3, k - 1) + lanes(0.625, 0.875) * tile(up3, k)
        else:
            merged = merged + lanes(0.875, 0.625) * tile(up3, k) + lanes(0.125, 0.375) * tile(up3, k + 1)
        k, h = f // 4 + 1, f % 4
        p_low, p_high = (2 * h + 0.5) / 8 - 0.5, (2 * h + 1.5) / 8 - 0.5
        other = k - 1 if h < 2 else k + 1
        merged = merged + lanes(1 - abs(p_low), 1 - abs(p_high)) * tile(up4, k)
        merged = merged + lanes(abs(p_low), abs(p_high)) * tile(up4, other)
        slope = gelu_both(merged)[1]
        gate = (slope * tile(wc, 4 + f)).astype(BF).astype(F32)
        gates.append(gate)
        if 0 <= f < 40:
            g = (d1[16 * (f + 1) : 16 * (f + 2)] * gate).astype(BF).astype(F32)
            row = lax.broadcasted_iota(jnp.int32, (16, 1), 0)
            gm1[8 + 16 * f : 24 + 16 * f, :] = jnp.where((row >= 4) & (row < 12), g, 0.0)
            cols = slice(128 * f, 128 * (f + 1))
            g1_ref[:, cols] = g[4:12].astype(BF)
            upward[0:1, cols] = g[4:5]
            downward[0:1, cols] = g[11:12]
    gm1[0:8, :] = jnp.zeros((8, 128), F32)
    gm1[648:656, :] = jnp.zeros((8, 128), F32)

    flat = jnp.concatenate(gates, axis=1).astype(BF)
    weights_back = row_weights((32, 16), 0, row_block)
    k = lax.broadcasted_iota(jnp.int32, (32, 16), 0)
    r = lax.broadcasted_iota(jnp.int32, (32, 16), 1)
    weights_back = jnp.where((k < 24) | ((r >= 4) & (r < 12)), weights_back, 0.0).astype(BF)
    down = jnp.dot(weights_back, flat, preferred_element_type=F32)
    down2, down3, down4 = down[0:16], down[16:24], down[24:32]

    def folded(v):
        return v + pltpu.roll(v, 64, 1)

    cg2 = []
    for c in range(40):
        v = 0.75 * tile(down2, c + 1) + 0.25 * jnp.where(low, tile(down2, c + 2), tile(down2, c))
        if c == 0:
            v = v + jnp.where(at_left, lanes(0.25, 0.0) * tile(down2, 1), 0.0)
        if c == 39:
            v = v + jnp.where(at_right, lanes(0.0, 0.25) * tile(down2, 40), 0.0)
        cg2.append(folded(v))
    cg3 = []
    for c in range(20):
        at = 2 * c
        v = lanes(0.125, 0.375) * tile(down3, at) + lanes(0.625, 0.875) * tile(down3, at + 1)
        v = v + lanes(0.875, 0.625) * tile(down3, at + 2) + lanes(0.375, 0.125) * tile(down3, at + 3)
        if c == 0:
            v = v + jnp.where(at_left, lanes(0.375, 0.125) * tile(down3, 1), 0.0)
        if c == 19:
            v = v + jnp.where(at_right, lanes(0.125, 0.375) * tile(down3, 40), 0.0)
        cg3.append(folded(v))
    cg4 = []
    for c in range(-1, 11):
        v = jnp.zeros((8, 128), F32)
        for n in range(8):
            a, b = (2 * n + 0.5) / 8, (2 * n + 1.5) / 8
            a, b = (a, b) if n < 4 else (2 - a, 2 - b)
            pair = 4 * c - 2 + n
            if 0 <= pair < 40:
                v = v + lanes(a, b) * tile(down4, pair + 1)
        cg4.append(folded(v))
    cg4[1] = cg4[1] + jnp.where(at_left, cg4[0], 0.0)
    cg4[-2] = cg4[-2] + jnp.where(at_right, cg4[-1], 0.0)
    cg4[0] = jnp.where(at_left, 0.0, cg4[0])
    cg4[-1] = jnp.where(at_right, 0.0, cg4[-1])
    for n in range(12):
        cols = slice(128 * n, 128 * (n + 1))
        upward[3:4, cols] = cg4[n][0:1]
        rim_ref[0:1, cols] = cg4[n][1:2]
        downward[3:4, cols] = cg4[n][2:3]

    flat2 = jnp.concatenate(cg2, axis=0).astype(BF).astype(F32)
    flat3 = jnp.concatenate(cg3, axis=0).astype(BF).astype(F32)
    flat4 = jnp.concatenate(cg4, axis=0).astype(BF).astype(F32)
    back2 = jnp.dot(flat2[:, 0:64].astype(BF), p2[...], preferred_element_type=F32)
    back3 = jnp.dot(flat3[:, 0:64].astype(BF), p3[...], preferred_element_type=F32)
    g2 = (d2[32:672, :] * back2).astype(BF).astype(F32)
    g3 = (d3[8:168, :] * back3).astype(BF).astype(F32)

    row2 = lax.broadcasted_iota(jnp.int32, (640, 1), 0) % 16
    own2 = (row2 >= 3) & (row2 < 7)
    row3 = lax.broadcasted_iota(jnp.int32, (160, 1), 0) % 8
    own3 = (row3 >= 2) & (row3 < 4)
    gm2[0:8, :] = jnp.zeros((8, 128), F32)
    gm2[8:648, :] = jnp.where(own2, g2, 0.0)
    gm2[648:656, :] = jnp.zeros((8, 128), F32)
    gm3[0:8, :] = jnp.zeros((8, 256), F32)
    gm3[8:168, :] = jnp.where(own3, g3, 0.0)
    gm3[168:176, :] = jnp.zeros((8, 256), F32)
    for c in range(40):
        at, cols = 8 + 16 * c + 3, slice(128 * c, 128 * (c + 1))
        g2_ref[:, cols] = gm2[at : at + 4, :].astype(BF)
        upward[1:2, cols] = gm2[at : at + 1, :]
        downward[1:2, cols] = gm2[at + 3 : at + 4, :]
    for c in range(20):
        at, cols = 8 + 8 * c + 2, slice(256 * c, 256 * (c + 1))
        g3_ref[:, cols] = gm3[at : at + 2, :].astype(BF)
        upward[2:3, cols] = gm3[at : at + 1, :]
        downward[2:3, cols] = gm3[at + 1 : at + 2, :]
    up_ref[...] = upward[0:4, :].astype(BF)
    down_ref[...] = downward[0:4, :].astype(BF)

    def put(at, first, second):
        rows = slice(at, at + first.shape[0])
        keep_ref[rows, :] = jnp.where(core == 0, first, second).astype(BF)
        send_ref[rows, :] = jnp.where(core == 0, second, first).astype(BF)

    cells = 327680
    x = xw3[16:176, :].astype(BF)
    shifted = jnp.concatenate([gm3[9 - i : 169 - i, :] for i in range(3)], axis=1).astype(BF)
    z = lax.dot_general(x, shifted, TN, preferred_element_type=F32) * (cells // 16) ** -0.5
    for i in range(3):
        put(768 * i, z[:, 256 * i : 256 * i + 128], z[:, 256 * i + 128 : 256 * i + 256])
    x = xw2[40:680, :].astype(BF)
    shifted = jnp.concatenate([gm2[9 - i : 649 - i, :] for i in range(3)], axis=1).astype(BF)
    z = lax.dot_general(x, shifted, TN, preferred_element_type=F32) * (cells // 4) ** -0.5
    put(2304, z[0:192, 0:128], z[192:384, 128:256])
    put(2496, z[192:384, 0:128], z[0:192, 256:384])
    put(2688, z[0:192, 128:256], z[192:384, 256:384])
    x = xw1[24:664, :].astype(BF)
    shifted = jnp.concatenate([gm1[9 - i : 649 - i, :] for i in range(3)], axis=1).astype(BF)
    z = lax.dot_general(x, shifted, TN, preferred_element_type=F32) * cells**-0.5
    window = (192, 0, 64, 128)
    blocks = []
    for i in range(3):
        zi = z[:, 128 * i : 128 * (i + 1)]
        for j in range(3):
            a, b = window[j], window[j + 1]
            blocks.append(zi[a : a + 64] + pltpu.roll(zi[b : b + 64], 64, 1))
    blocks.append(jnp.zeros((64, 128), F32))
    pairs = [jnp.where(low, blocks[n], pltpu.roll(blocks[n + 1], 64, 1)) for n in range(0, 10, 2)]
    y2_own, y3_own = y2[32:672], y3.astype(F32)[8:168].astype(BF)
    for y, flat, mask, branch in (
        (y2_own, flat2, own2, 1),
        (y3_own, flat3, own3, 2),
        (y4, flat4, None, 3),
    ):
        masked = (flat if mask is None else jnp.where(mask, flat, 0.0)).astype(BF)
        z = lax.dot_general(masked, y, TN, preferred_element_type=F32) * (cells // 4**branch) ** -0.5
        pairs += [z[0:64, 128 * n : 128 * (n + 1)] for n in range(z.shape[1] // 128)]
    for n in range(6):
        put(2880 + 64 * n, pairs[2 * n], pairs[2 * n + 1])
    put(3264, jnp.zeros((64, 128), F32), jnp.zeros((64, 128), F32))


def rims_kernel(g1_ref, g2_ref, g3_ref, rim_ref, above_ref, below_ref, left_ref, right_ref, out):
    g1, g2, g3, above, below = (ref[...].astype(F32) for ref in (g1_ref, g2_ref, g3_ref, above_ref, below_ref))
    rim = rim_ref[...] + above[3:4, 0:1536] + below[3:4, 0:1536]
    for ref, one, three, four in ((left_ref, 0, 0, 0), (right_ref, WIDE - 128, WIDE - 256, 1408)):
        ones, threes = slice(one, one + 128), slice(three, three + 256)
        out[...] = jnp.zeros_like(out)
        out[0:1, 0:128] = above[0:1, ones]
        out[1:9, 0:128] = g1[:, ones]
        out[9:10, 0:128] = below[0:1, ones]
        out[10:11, 0:128] = above[1:2, ones]
        out[11:15, 0:128] = g2[:, ones]
        out[15:16, 0:128] = below[1:2, ones]
        out[16:17, :] = above[2:3, threes]
        out[17:19, :] = g3[:, threes]
        out[19:20, :] = below[2:3, threes]
        out[20:21, 0:128] = rim[:, four : four + 128]
        ref[...] = out[...].astype(BF)


def backward_kernel(
    g1_ref, g2_ref, g3_ref, rim_ref, above_ref, below_ref, left_ref, right_ref,
    gf1_ref, gf2_ref, gf3_ref, gf4_ref, wide1, wide2, wide3, xw1, xw2, xw3, out2, out3, near, copies,
):
    t1b, k2, k3, p4 = near
    low = lax.broadcasted_iota(jnp.int32, (1, 128), 1) < 64
    for ref, n in ((xw1, 640), (xw2, 320), (xw3, 160)):
        ref[0:8, :] = jnp.zeros((8, ref.shape[1]), F32)
        ref[8 + n : 16 + n, :] = jnp.zeros((8, ref.shape[1]), F32)
    above, below, left, right = (ref[...].astype(F32) for ref in (above_ref, below_ref, left_ref, right_ref))
    for n, (wide, g_ref, top, rows, start, step) in enumerate(
        ((wide1, g1_ref, 3, 8, 0, 128), (wide2, g2_ref, 0, 4, 10, 128), (wide3, g3_ref, 0, 2, 16, 256))
    ):
        wide[...] = jnp.zeros_like(wide)
        mid, end = slice(step, step + WIDE), step + WIDE
        wide[top : top + 1, mid] = above[n : n + 1]
        wide[top + 1 : top + 1 + rows, mid] = g_ref[...].astype(F32)
        wide[top + 1 + rows : top + 2 + rows, mid] = below[n : n + 1]
        wide[top : top + 2 + rows, 0:step] = left[start : start + 2 + rows, 0:step]
        wide[top : top + 2 + rows, end : end + step] = right[start : start + 2 + rows, 0:step]

    for copy in copies:
        copy.wait()
    for f in range(40):
        at = 8 + 16 * f
        xw1[at : at + 16, 0:128] = tile(wide1, f + 1)
        xw1[at : at + 16, 128:256] = jnp.where(low, tile(wide1, f + 2), tile(wide1, f))
    total = xw1[8:648, 0:128]
    for i in range(3):
        total = total + lax.dot_general(
            xw1[9 - i : 649 - i, :].astype(BF), t1b[i], NT, preferred_element_type=F32
        )
    for f in range(40):
        gf1_ref[:, 128 * f : 128 * (f + 1)] = total[16 * f + 4 : 16 * f + 12].astype(BF)

    for j in range(3):
        for c in range(40):
            xw2[8 + 8 * c : 16 + 8 * c, 128 * j : 128 * j + 128] = tile(wide2, c + 2 - j)
    total = xw2[8:328, 128:256]
    for i in range(3):
        kernel = jnp.concatenate([k2[i, 128 * j : 128 * j + 128, :] for j in range(3)], axis=1)
        total = total + lax.dot_general(
            xw2[9 - i : 329 - i, :].astype(BF), kernel, NT, preferred_element_type=F32
        )
    out2[...] = total
    for c in range(40):
        gf2_ref[:, 128 * c : 128 * (c + 1)] = out2[8 * c + 1 : 8 * c + 5, :].astype(BF)

    for j in range(3):
        for c in range(20):
            first = 256 * (c + 2 - j)
            xw3[8 + 8 * c : 16 + 8 * c, 256 * j : 256 * j + 256] = wide3[:, first : first + 256]
    total = xw3[8:168, 256:512]
    for i in range(3):
        kernel = jnp.concatenate([k3[i, 256 * j : 256 * j + 256, :] for j in range(3)], axis=1)
        total = total + lax.dot_general(
            xw3[9 - i : 169 - i, :].astype(BF), kernel, NT, preferred_element_type=F32
        )
    out3[...] = total
    for c in range(20):
        gf3_ref[:, 256 * c : 256 * (c + 1)] = out3[8 * c + 1 : 8 * c + 3, :].astype(BF)

    rim = rim_ref[...] + above[3:4, 0:1536] + below[3:4, 0:1536]
    for c in range(10):
        cg = rim[:, 128 * (c + 1) : 128 * (c + 2)]
        if c == 0:
            cg = cg + left[20:21, 0:128]
        if c == 9:
            cg = cg + right[20:21, 0:128]
        cg = jnp.broadcast_to(cg[:, 0:64], (8, 64)).astype(BF)
        back = jnp.dot(cg, p4[...], preferred_element_type=F32)
        gf4_ref[0:1, 512 * c : 512 * c + 512] = back[0:1].astype(BF)


def swapped(block, axis, flip):
    return lax.ppermute(block, axis, [(i, i ^ flip) for i in range(lax.axis_size(axis))])


def unpack_kernel(place_ref, mine, got, k1_ref, k2_ref, k3_ref, p2_ref, p3_ref, p4_ref):
    core = place_ref[3]

    def take(side, at, count):
        rows = slice(at, at + count)
        return jnp.where(core == side, mine[rows, :], got[rows, :])

    k3_ref[:, 0:128] = take(0, 0, 2304)
    k3_ref[:, 128:256] = take(1, 0, 2304)
    k2_ref[0:576, :] = take(0, 2304, 576)
    k2_ref[576:1152, :] = take(1, 2304, 576)
    pairs = [take(n % 2, 2880 + 64 * (n // 2), 64) for n in range(12)]
    for n in range(9):
        k1_ref[64 * n : 64 * (n + 1), :] = pairs[n // 2][:, 64 * (n % 2) : 64 * (n % 2) + 64]
    n = 5
    for ref, count in ((p2_ref, 1), (p3_ref, 2), (p4_ref, 4)):
        for m in range(count):
            ref[:, 128 * m : 128 * (m + 1)] = pairs[n]
            n += 1


def call(kernel, out_shapes, scratch, *operands, scalars=0, far=0):
    near = len(operands) - scalars - far
    specs = [pl.BlockSpec(memory_space=space) for space in (pltpu.SMEM, pltpu.VMEM, pl.ANY)]
    outs = len(out_shapes)

    def body(*refs):
        first, last = scalars + near, scalars + near + far
        sources = refs[first:last]
        if far:
            buffers, sems = refs[-1 - far : -1], refs[-1]
            copies = [pltpu.make_async_copy(sources[n], buffers[n], sems.at[n]) for n in range(far)]
            for copy in copies:
                copy.start()
            kernel(*refs[:first], *refs[last : -1 - far], buffers, copies)
        else:
            kernel(*refs)

    return pl.pallas_call(
        body,
        out_shape=[jax.ShapeDtypeStruct(shape, dtype) for shape, dtype in out_shapes],
        in_specs=[specs[0]] * scalars + [specs[1]] * near + [specs[2]] * far,
        out_specs=[specs[1]] * outs,
        scratch_shapes=[pltpu.VMEM(shape, dtype) for shape, dtype in scratch]
        + [pltpu.VMEM(operand.shape, operand.dtype) for operand in operands[len(operands) - far :]]
        + ([pltpu.SemaphoreType.DMA((far,))] if far else []),
        compiler_params=pltpu.CompilerParams(vmem_limit_bytes=48 * 1024 * 1024),
    )(*operands)


def pair_weights(kernel_one):
    none = jnp.zeros((3, FEAT_ONE, FEAT_ONE), BF)
    tap = lambda j: kernel_one[:, j] if 0 <= j < 3 else none
    windows = (1, 2, 3, 0)
    ahead = jnp.concatenate(
        [jnp.concatenate([tap(w - e) for w in windows], axis=1) for e in range(2)], axis=2
    )
    back = jnp.concatenate(
        [jnp.concatenate([tap(e - w + 2) for e in range(2)], axis=1) for w in windows], axis=2
    )
    return ahead, back


def local_part(x1, x2, x3, x4, kernel_one, kernel_two, kernel_three, p2, p3, p4, cot):
    place = jnp.stack(
        [
            lax.axis_index(ROWS),
            lax.axis_index(COLS),
            (lax.axis_index(COLS) == lax.axis_size(COLS) - 1).astype(jnp.int32),
            lax.axis_index("core"),
        ]
    ).astype(jnp.int32)
    ahead, back = pair_weights(kernel_one)
    k2 = in_hbm(kernel_two.reshape(3, 384, 128))
    k3 = in_hbm(kernel_three.reshape(3, 768, 256))
    fars = halos(x1, x2, x3, x4, cot) + (ahead, k2, k3, in_hbm(p2.T), in_hbm(p3.T), in_hbm(p4.T))
    total = RIM + WIDE + RIM
    keep, send, g1, g2, g3, rim, up, down = call(
        forward_kernel,
        [
            ((PACK_ROWS, 128), BF), ((PACK_ROWS, 128), BF),
            ((8, WIDE), BF), ((4, WIDE), BF), ((2, WIDE), BF), ((1, 1536), F32),
            ((4, WIDE), BF), ((4, WIDE), BF),
        ],
        [
            ((16, total), F32), ((16, total), F32), ((16, total), F32), ((8, total), F32), ((8, total), F32),
            ((688, 256), F32), ((720, 384), F32), ((192, 768), F32),
            ((672, 128), F32), ((704, 128), F32), ((176, 256), F32),
            ((656, 128), F32), ((656, 128), F32), ((176, 256), F32),
            ((8, WIDE), F32), ((8, WIDE), F32),
        ],
        place,
        *fars,
        scalars=1,
        far=15,
    )
    return place, keep, send, (g1, g2, g3, rim), up, down, (back, k2, k3, in_hbm(p4.T))


def from_beside(grads, above, below):
    left, right = call(
        rims_kernel, [((32, 256), BF), ((32, 256), BF)], [((32, 256), F32)], *grads, above, below
    )
    return moved(right, COLS, 1), moved(left, COLS, -1)


def input_grads(grads, above, below, left, right, weights):
    return call(
        backward_kernel,
        [((8, WIDE), BF), ((4, WIDE), BF), ((2, WIDE), BF), ((1, WIDE), BF)],
        [
            ((16, 42 * 128), F32), ((8, 42 * 128), F32), ((8, 22 * 256), F32),
            ((656, 256), F32), ((336, 384), F32), ((176, 768), F32),
            ((320, 128), F32), ((160, 256), F32),
        ],
        *grads, above, below, left, right,
        *weights,
        far=4,
    )


def unpacked(place, mine, got):
    outs = call(
        unpack_kernel,
        [((576, 64), BF), ((1152, 128), BF), ((2304, 256), BF), ((64, 128), BF), ((64, 256), BF), ((64, 512), BF)],
        [],
        place, mine, got,
        scalars=1,
    )
    return (
        outs[0].reshape(3, 3, 64, 64), outs[1].reshape(3, 3, 128, 128), outs[2].reshape(3, 3, 256, 256),
        outs[3].T, outs[4].T, outs[5].T,
    )


def on_device(*args):
    place, keep, send, grads, up, down, weights = local_part(*args)
    part = (keep.astype(F32) + swapped(send, "core", 1).astype(F32)).astype(BF)
    part, up, down = lax.optimization_barrier((part, up, down))

    pieces = lax.all_to_all(part.reshape(32, -1, 128), SLAB, 0, 0)
    above, below = moved(down, ROWS, 1), moved(up, ROWS, -1)
    pieces, above, below = lax.optimization_barrier((pieces, above, below))
    part = jnp.sum(pieces.astype(F32), axis=0).astype(BF)

    pieces = lax.all_to_all(jnp.broadcast_to(part[None], (8,) + part.shape), "z_hi", 0, 0)
    left, right = from_beside(grads, above, below)
    pieces, left, right = lax.optimization_barrier((pieces, left, right))
    part = jnp.sum(pieces.astype(F32), axis=0).astype(BF)

    pieces = jnp.broadcast_to(part[None], (32,) + part.shape)
    mine = lax.all_to_all(pieces, SLAB, 0, 0).reshape(keep.shape)
    outs = input_grads(grads, above, below, left, right, weights)
    mine, outs = lax.optimization_barrier((mine, outs))
    return tuple(outs) + unpacked(place, mine, swapped(mine, "core", 1))


def solution(mesh):
    mesh = Mesh(mesh.devices.reshape(8, 2, 2, 4, 2, 2), ROWS + COLS)
    split = P(ROWS, COLS)
    in_specs = (split,) * 4 + (P(),) * 6 + (split,)
    out_specs = (split,) * 4 + (P(),) * 6
    return jax.shard_map(on_device, mesh=mesh, in_specs=in_specs, out_specs=out_specs, check_vma=False)
```

```python
import functools

import jax
import jax.numpy as jnp
from jax import lax
from jax.experimental import pallas as pl
from jax.experimental.pallas import tpu as pltpu
from jax.sharding import Mesh
from jax.sharding import PartitionSpec as P

FEAT_ONE = 64
FEAT_TWO = 128
FEAT_THREE = 256
FEAT_FOUR = 512

ROWS = ("z_hi", "z_lo", "x_lo", "y")
COLS = ("x_hi", "core")
SLAB = ("z_lo", "x_lo", "y", "x_hi")
PACK_ROWS = 3328
WIDE = 5120
RIM = 512
BF = jnp.bfloat16
F32 = jnp.float32
NT = (((1,), (1,)), ((), ()))
TN = (((0,), (0,)), ((), ()))


def moved(block, axis, distance):
    count = lax.axis_size(axis)
    route = [(i, i + distance) for i in range(count) if 0 <= i + distance < count]
    return lax.ppermute(block, axis, route)


def stacked(parts, rows):
    total, at = None, 0
    for part in parts:
        padded = jnp.pad(part, ((at, rows - at - part.shape[0]), (0, 0)))
        total = padded if total is None else total + padded
        at += part.shape[0]
    return total


def in_hbm(x):
    return pltpu.with_memory_space_constraint(x, pltpu.HBM)


def edge_kernel(last_ref, first_ref, right_ref, left_ref, last, first, edge, near, copies):
    for copy in copies:
        copy.wait()
    x1, cot, x2, x3, x4 = (ref[...].astype(F32) for ref in near)
    for out, ref, ones, cots, twos in (
        (last, last_ref, x1[5:8], cot[6:8], x2[1:4]),
        (first, first_ref, x1[0:3], cot[0:2], x2[0:3]),
    ):
        out[0:3, :] = ones
        out[3:5, :] = cots
        out[5:8, :] = twos
        out[8:10, :] = x3
        out[10:11, :] = x4
        out[11:16, :] = jnp.zeros((5, WIDE), F32)
        ref[...] = out[...].astype(BF)
    edge[...] = jnp.zeros_like(edge)
    for ref, cols in ((right_ref, slice(WIDE - RIM, WIDE)), (left_ref, slice(0, RIM))):
        edge[0:8, :] = x1[:, cols]
        edge[8:16, :] = cot[:, cols]
        edge[16:20, :] = x2[:, cols]
        edge[20:22, :] = x3[:, cols]
        edge[22:23, :] = x4[:, cols]
        ref[...] = edge[...].astype(BF)


def halos(x1, x2, x3, x4, cot):
    own = tuple(in_hbm(x) for x in (x1, cot, x2, x3, x4))
    last, first, right_edge, left_edge = call(
        edge_kernel,
        [((16, WIDE), BF), ((16, WIDE), BF), ((24, RIM), BF), ((24, RIM), BF)],
        [((16, WIDE), F32), ((16, WIDE), F32), ((24, RIM), F32)],
        *own,
        far=5,
    )
    above = moved(last, ROWS, 1)
    below = moved(first, ROWS, -1)
    left = moved(stacked((right_edge, above[:11, -RIM:], below[:11, -RIM:]), 48), COLS, 1)
    right = moved(stacked((left_edge, above[:11, :RIM], below[:11, :RIM]), 48), COLS, -1)
    return own + (above, below, left, right)


def gelu_both(v):
    c = 0.7978845608028654
    sq = v * v
    t = jnp.tanh(c * v * (1.0 + 0.044715 * sq))
    half = 0.5 * (1.0 + t)
    slope = half + 0.5 * v * (1.0 - t * t) * (c * (1.0 + 3.0 * 0.044715 * sq))
    return v * half, slope


def tile(wide, at):
    return wide[:, 128 * at : 128 * (at + 1)]


def row_weights(shape, coarse_dim, row_block):
    k = lax.broadcasted_iota(jnp.int32, shape, coarse_dim)
    r = lax.broadcasted_iota(jnp.int32, shape, 1 - coarse_dim)
    two, three = k < 16, k < 24
    scale = jnp.where(two, 2, jnp.where(three, 4, 8))
    count = jnp.where(two, 4, jnp.where(three, 2, 1))
    shift = jnp.where(two, 3, jnp.where(three, 16 + 2, 24 + 1))
    total = (jnp.where(two, 512, jnp.where(three, 256, 128)) - 1).astype(F32)
    coarse = (row_block * count + k - shift).astype(F32)
    fine = (row_block * 8 + r - 4).astype(F32)
    inverse = jnp.where(two, 0.5, jnp.where(three, 0.25, 0.125)).astype(F32)
    place = jnp.clip((fine + 0.5) * inverse - 0.5, 0.0, total)
    return jnp.maximum(0.0, 1.0 - jnp.abs(place - coarse))


def forward_kernel(
    place_ref, keep_ref, send_ref, g1_ref, g2_ref, g3_ref, rim_ref, up_ref, down_ref,
    wx1, wc, wx2, wx3, wx4, xw1, xw2, xw3, d1, d2, d3, gm1, gm2, gm3, upward, downward,
    near, copies,
):
    x1, cot, x2, x3, x4, above, below, left, right, t1, k2, k3, p2, p3, p4 = near
    row_block = place_ref[0]
    at_left = place_ref[1] == 0
    at_right = place_ref[2] == 1
    core = place_ref[3]
    lane = lax.broadcasted_iota(jnp.int32, (1, 128), 1)
    low = lane < 64

    def lanes(a, b):
        return jnp.where(low, a, b).astype(F32)

    for ref in (wx1, wc, wx2, wx3, wx4, upward, downward):
        ref[...] = jnp.zeros_like(ref)
    for copy in copies[:10]:
        copy.wait()
    for side, to in ((None, RIM), (left, 0), (right, RIM + WIDE)):
        if side is None:
            cols = slice(to, to + WIDE)
            mid = [ref[...].astype(F32) for ref in (x1, cot, x2, x3, x4)]
            up, down = above[...].astype(F32), below[...].astype(F32)
        else:
            cols = slice(to, to + RIM)
            v = side[...].astype(F32)
            mid = [v[0:8], v[8:16], v[16:20], v[20:22], v[22:23]]
            up, down = v[24:35], v[35:46]
        wx1[1:4, cols] = up[0:3]
        wx1[4:12, cols] = mid[0]
        wx1[12:15, cols] = down[0:3]
        wc[2:4, cols] = up[3:5]
        wc[4:12, cols] = mid[1]
        wc[12:14, cols] = down[3:5]
        wx2[0:3, cols] = up[5:8]
        wx2[3:7, cols] = mid[2]
        wx2[7:10, cols] = down[5:8]
        wx3[0:2, cols] = up[8:10]
        wx3[2:4, cols] = mid[3]
        wx3[4:6, cols] = down[8:10]
        wx4[0:1, cols] = up[10:11]
        wx4[1:2, cols] = mid[4]
        wx4[2:3, cols] = down[10:11]

    for f in range(-1, 41):
        at = 8 + 16 * (f + 1)
        xw1[at : at + 16, 0:128] = tile(wx1, 4 + f)
        xw1[at : at + 16, 128:256] = jnp.where(low, tile(wx1, 5 + f), tile(wx1, 3 + f))
    xw1[0:8, :] = jnp.zeros((8, 256), F32)
    xw1[680:688, :] = jnp.zeros((8, 256), F32)
    pre1 = xw1[8:680, 0:128]
    for i in range(3):
        pre1 = pre1 + jnp.dot(xw1[7 + i : 679 + i, :].astype(BF), t1[i], preferred_element_type=F32)
    y1, slope = gelu_both(pre1)
    y1 = y1.astype(BF).astype(F32)
    d1[...] = slope

    copies[10].wait()
    for j in range(3):
        for c in range(-2, 42):
            at = 8 + 16 * (c + 2)
            xw2[at : at + 16, 128 * j : 128 * j + 128] = tile(wx2, 3 + c + j)
    xw2[0:8, :] = jnp.zeros((8, 384), F32)
    xw2[712:720, :] = jnp.zeros((8, 384), F32)
    pre2 = xw2[8:712, 128:256]
    for i in range(3):
        pre2 = pre2 + jnp.dot(xw2[7 + i : 711 + i, :].astype(BF), k2[i], preferred_element_type=F32)
    y2, slope = gelu_both(pre2)
    y2 = y2.astype(BF)
    d2[...] = slope

    copies[11].wait()
    for j in range(3):
        for c in range(-1, 21):
            at = 8 + 8 * (c + 1)
            first = RIM + 256 * (c + j - 1)
            xw3[at : at + 8, 256 * j : 256 * j + 256] = wx3[:, first : first + 256]
    xw3[0:8, :] = jnp.zeros((8, 768), F32)
    xw3[184:192, :] = jnp.zeros((8, 768), F32)
    pre3 = xw3[8:184, 256:512]
    for i in range(3):
        pre3 = pre3 + jnp.dot(xw3[7 + i : 183 + i, :].astype(BF), k3[i], preferred_element_type=F32)
    y3, slope = gelu_both(pre3)
    y3 = y3.astype(BF)
    d3[...] = slope

    y4 = jnp.concatenate([wx4[:, 512 * c : 512 * c + 512] for c in range(12)], axis=0).astype(BF)

    for copy in copies[12:]:
        copy.wait()
    weights = row_weights((16, 32), 1, row_block).astype(BF)
    rows_up = []
    for y, p, rim, rows, wlo in ((y2, p2, 2, 16, 0), (y3, p3, 1, 8, 16), (y4, p4, 1, 8, 24)):
        twice = jnp.concatenate([p[...], p[...]], axis=0)
        coarse = lax.dot_general(y, twice, NT, preferred_element_type=F32).astype(BF).astype(F32)
        cols = [coarse[rows * n : rows * (n + 1)] for n in range(coarse.shape[0] // rows)]
        end = len(cols) - rim
        cols[rim - 1] = jnp.where(at_left, cols[rim], cols[rim - 1])
        cols[end] = jnp.where(at_right, cols[end - 1], cols[end])
        flat = jnp.concatenate(cols, axis=1).astype(BF)
        rows_up.append(jnp.dot(weights[:, wlo : wlo + rows], flat, preferred_element_type=F32))
    up2, up3, up4 = rows_up

    gates = []
    for f in range(-1, 41):
        k = f + 2
        merged = y1[16 * (f + 1) : 16 * (f + 2)]
        merged = merged + 0.75 * tile(up2, k) + 0.25 * jnp.where(low, tile(up2, k - 1), tile(up2, k + 1))
        k, h = f // 2 + 1, f % 2
        if h == 0:
            merged = merged + lanes(0.375, 0.125) * tile(up3, k - 1) + lanes(0.625, 0.875) * tile(up3, k)
        else:
            merged = merged + lanes(0.875, 0.625) * tile(up3, k) + lanes(0.125, 0.375) * tile(up3, k + 1)
        k, h = f // 4 + 1, f % 4
        p_low, p_high = (2 * h + 0.5) / 8 - 0.5, (2 * h + 1.5) / 8 - 0.5
        other = k - 1 if h < 2 else k + 1
        merged = merged + lanes(1 - abs(p_low), 1 - abs(p_high)) * tile(up4, k)
        merged = merged + lanes(abs(p_low), abs(p_high)) * tile(up4, other)
        slope = gelu_both(merged)[1]
        gate = (slope * tile(wc, 4 + f)).astype(BF).astype(F32)
        gates.append(gate)
        if 0 <= f < 40:
            g = (d1[16 * (f + 1) : 16 * (f + 2)] * gate).astype(BF).astype(F32)
            row = lax.broadcasted_iota(jnp.int32, (16, 1), 0)
            gm1[8 + 16 * f : 24 + 16 * f, :] = jnp.where((row >= 4) & (row < 12), g, 0.0)
            cols = slice(128 * f, 128 * (f + 1))
            g1_ref[:, cols] = g[4:12].astype(BF)
            upward[0:1, cols] = g[4:5]
            downward[0:1, cols] = g[11:12]
    gm1[0:8, :] = jnp.zeros((8, 128), F32)
    gm1[648:656, :] = jnp.zeros((8, 128), F32)

    flat = jnp.concatenate(gates, axis=1).astype(BF)
    weights_back = row_weights((32, 16), 0, row_block)
    k = lax.broadcasted_iota(jnp.int32, (32, 16), 0)
    r = lax.broadcasted_iota(jnp.int32, (32, 16), 1)
    weights_back = jnp.where((k < 24) | ((r >= 4) & (r < 12)), weights_back, 0.0).astype(BF)
    down = jnp.dot(weights_back, flat, preferred_element_type=F32)
    down2, down3, down4 = down[0:16], down[16:24], down[24:32]

    def folded(v):
        return v + pltpu.roll(v, 64, 1)

    cg2 = []
    for c in range(40):
        v = 0.75 * tile(down2, c + 1) + 0.25 * jnp.where(low, tile(down2, c + 2), tile(down2, c))
        if c == 0:
            v = v + jnp.where(at_left, lanes(0.25, 0.0) * tile(down2, 1), 0.0)
        if c == 39:
            v = v + jnp.where(at_right, lanes(0.0, 0.25) * tile(down2, 40), 0.0)
        cg2.append(folded(v))
    cg3 = []
    for c in range(20):
        at = 2 * c
        v = lanes(0.125, 0.375) * tile(down3, at) + lanes(0.625, 0.875) * tile(down3, at + 1)
        v = v + lanes(0.875, 0.625) * tile(down3, at + 2) + lanes(0.375, 0.125) * tile(down3, at + 3)
        if c == 0:
            v = v + jnp.where(at_left, lanes(0.375, 0.125) * tile(down3, 1), 0.0)
        if c == 19:
            v = v + jnp.where(at_right, lanes(0.125, 0.375) * tile(down3, 40), 0.0)
        cg3.append(folded(v))
    cg4 = []
    for c in range(-1, 11):
        v = jnp.zeros((8, 128), F32)
        for n in range(8):
            a, b = (2 * n + 0.5) / 8, (2 * n + 1.5) / 8
            a, b = (a, b) if n < 4 else (2 - a, 2 - b)
            pair = 4 * c - 2 + n
            if 0 <= pair < 40:
                v = v + lanes(a, b) * tile(down4, pair + 1)
        cg4.append(folded(v))
    cg4[1] = cg4[1] + jnp.where(at_left, cg4[0], 0.0)
    cg4[-2] = cg4[-2] + jnp.where(at_right, cg4[-1], 0.0)
    cg4[0] = jnp.where(at_left, 0.0, cg4[0])
    cg4[-1] = jnp.where(at_right, 0.0, cg4[-1])
    for n in range(12):
        cols = slice(128 * n, 128 * (n + 1))
        upward[3:4, cols] = cg4[n][0:1]
        rim_ref[0:1, cols] = cg4[n][1:2]
        downward[3:4, cols] = cg4[n][2:3]

    flat2 = jnp.concatenate(cg2, axis=0).astype(BF).astype(F32)
    flat3 = jnp.concatenate(cg3, axis=0).astype(BF).astype(F32)
    flat4 = jnp.concatenate(cg4, axis=0).astype(BF).astype(F32)
    back2 = jnp.dot(flat2[:, 0:64].astype(BF), p2[...], preferred_element_type=F32)
    back3 = jnp.dot(flat3[:, 0:64].astype(BF), p3[...], preferred_element_type=F32)
    g2 = (d2[32:672, :] * back2).astype(BF).astype(F32)
    g3 = (d3[8:168, :] * back3).astype(BF).astype(F32)

    row2 = lax.broadcasted_iota(jnp.int32, (640, 1), 0) % 16
    own2 = (row2 >= 3) & (row2 < 7)
    row3 = lax.broadcasted_iota(jnp.int32, (160, 1), 0) % 8
    own3 = (row3 >= 2) & (row3 < 4)
    gm2[0:8, :] = jnp.zeros((8, 128), F32)
    gm2[8:648, :] = jnp.where(own2, g2, 0.0)
    gm2[648:656, :] = jnp.zeros((8, 128), F32)
    gm3[0:8, :] = jnp.zeros((8, 256), F32)
    gm3[8:168, :] = jnp.where(own3, g3, 0.0)
    gm3[168:176, :] = jnp.zeros((8, 256), F32)
    for c in range(40):
        at, cols = 8 + 16 * c + 3, slice(128 * c, 128 * (c + 1))
        g2_ref[:, cols] = gm2[at : at + 4, :].astype(BF)
        upward[1:2, cols] = gm2[at : at + 1, :]
        downward[1:2, cols] = gm2[at + 3 : at + 4, :]
    for c in range(20):
        at, cols = 8 + 8 * c + 2, slice(256 * c, 256 * (c + 1))
        g3_ref[:, cols] = gm3[at : at + 2, :].astype(BF)
        upward[2:3, cols] = gm3[at : at + 1, :]
        downward[2:3, cols] = gm3[at + 1 : at + 2, :]
    up_ref[...] = upward[0:4, :].astype(BF)
    down_ref[...] = downward[0:4, :].astype(BF)

    def put(at, first, second):
        rows = slice(at, at + first.shape[0])
        keep_ref[rows, :] = jnp.where(core == 0, first, second).astype(BF)
        send_ref[rows, :] = jnp.where(core == 0, second, first).astype(BF)

    cells = 327680
    x = xw3[16:176, :].astype(BF)
    shifted = jnp.concatenate([gm3[9 - i : 169 - i, :] for i in range(3)], axis=1).astype(BF)
    z = lax.dot_general(x, shifted, TN, preferred_element_type=F32) * (cells // 16) ** -0.5
    for i in range(3):
        put(768 * i, z[:, 256 * i : 256 * i + 128], z[:, 256 * i + 128 : 256 * i + 256])
    x = xw2[40:680, :].astype(BF)
    shifted = jnp.concatenate([gm2[9 - i : 649 - i, :] for i in range(3)], axis=1).astype(BF)
    z = lax.dot_general(x, shifted, TN, preferred_element_type=F32) * (cells // 4) ** -0.5
    put(2304, z[0:192, 0:128], z[192:384, 128:256])
    put(2496, z[192:384, 0:128], z[0:192, 256:384])
    put(2688, z[0:192, 128:256], z[192:384, 256:384])
    x = xw1[24:664, :].astype(BF)
    shifted = jnp.concatenate([gm1[9 - i : 649 - i, :] for i in range(3)], axis=1).astype(BF)
    z = lax.dot_general(x, shifted, TN, preferred_element_type=F32) * cells**-0.5
    window = (192, 0, 64, 128)
    blocks = []
    for i in range(3):
        zi = z[:, 128 * i : 128 * (i + 1)]
        for j in range(3):
            a, b = window[j], window[j + 1]
            blocks.append(zi[a : a + 64] + pltpu.roll(zi[b : b + 64], 64, 1))
    blocks.append(jnp.zeros((64, 128), F32))
    pairs = [jnp.where(low, blocks[n], pltpu.roll(blocks[n + 1], 64, 1)) for n in range(0, 10, 2)]
    y2_own, y3_own = y2[32:672], y3.astype(F32)[8:168].astype(BF)
    for y, flat, mask, branch in (
        (y2_own, flat2, own2, 1),
        (y3_own, flat3, own3, 2),
        (y4, flat4, None, 3),
    ):
        masked = (flat if mask is None else jnp.where(mask, flat, 0.0)).astype(BF)
        z = lax.dot_general(masked, y, TN, preferred_element_type=F32) * (cells // 4**branch) ** -0.5
        pairs += [z[0:64, 128 * n : 128 * (n + 1)] for n in range(z.shape[1] // 128)]
    for n in range(6):
        put(2880 + 64 * n, pairs[2 * n], pairs[2 * n + 1])
    put(3264, jnp.zeros((64, 128), F32), jnp.zeros((64, 128), F32))


def rims_kernel(g1_ref, g2_ref, g3_ref, rim_ref, above_ref, below_ref, left_ref, right_ref, out):
    g1, g2, g3, above, below = (ref[...].astype(F32) for ref in (g1_ref, g2_ref, g3_ref, above_ref, below_ref))
    rim = rim_ref[...] + above[3:4, 0:1536] + below[3:4, 0:1536]
    for ref, one, three, four in ((left_ref, 0, 0, 0), (right_ref, WIDE - 128, WIDE - 256, 1408)):
        ones, threes = slice(one, one + 128), slice(three, three + 256)
        out[...] = jnp.zeros_like(out)
        out[0:1, 0:128] = above[0:1, ones]
        out[1:9, 0:128] = g1[:, ones]
        out[9:10, 0:128] = below[0:1, ones]
        out[10:11, 0:128] = above[1:2, ones]
        out[11:15, 0:128] = g2[:, ones]
        out[15:16, 0:128] = below[1:2, ones]
        out[16:17, :] = above[2:3, threes]
        out[17:19, :] = g3[:, threes]
        out[19:20, :] = below[2:3, threes]
        out[20:21, 0:128] = rim[:, four : four + 128]
        ref[...] = out[...].astype(BF)


def backward_kernel(
    g1_ref, g2_ref, g3_ref, rim_ref, above_ref, below_ref, left_ref, right_ref, t1b, k2, k3, p4,
    gf1_ref, gf2_ref, gf3_ref, gf4_ref, wide1, wide2, wide3, xw1, xw2, xw3, out2, out3,
):
    low = lax.broadcasted_iota(jnp.int32, (1, 128), 1) < 64
    for ref, n in ((xw1, 640), (xw2, 320), (xw3, 160)):
        ref[0:8, :] = jnp.zeros((8, ref.shape[1]), F32)
        ref[8 + n : 16 + n, :] = jnp.zeros((8, ref.shape[1]), F32)
    above, below, left, right = (ref[...].astype(F32) for ref in (above_ref, below_ref, left_ref, right_ref))
    for n, (wide, g_ref, top, rows, start, step) in enumerate(
        ((wide1, g1_ref, 3, 8, 0, 128), (wide2, g2_ref, 0, 4, 10, 128), (wide3, g3_ref, 0, 2, 16, 256))
    ):
        wide[...] = jnp.zeros_like(wide)
        mid, end = slice(step, step + WIDE), step + WIDE
        wide[top : top + 1, mid] = above[n : n + 1]
        wide[top + 1 : top + 1 + rows, mid] = g_ref[...].astype(F32)
        wide[top + 1 + rows : top + 2 + rows, mid] = below[n : n + 1]
        wide[top : top + 2 + rows, 0:step] = left[start : start + 2 + rows, 0:step]
        wide[top : top + 2 + rows, end : end + step] = right[start : start + 2 + rows, 0:step]

    for f in range(40):
        at = 8 + 16 * f
        xw1[at : at + 16, 0:128] = tile(wide1, f + 1)
        xw1[at : at + 16, 128:256] = jnp.where(low, tile(wide1, f + 2), tile(wide1, f))
    total = xw1[8:648, 0:128]
    for i in range(3):
        total = total + lax.dot_general(
            xw1[9 - i : 649 - i, :].astype(BF), t1b[i], NT, preferred_element_type=F32
        )
    for f in range(40):
        gf1_ref[:, 128 * f : 128 * (f + 1)] = total[16 * f + 4 : 16 * f + 12].astype(BF)

    for j in range(3):
        for c in range(40):
            xw2[8 + 8 * c : 16 + 8 * c, 128 * j : 128 * j + 128] = tile(wide2, c + 2 - j)
    total = xw2[8:328, 128:256]
    for i in range(3):
        kernel = jnp.concatenate([k2[i, 128 * j : 128 * j + 128, :] for j in range(3)], axis=1)
        total = total + lax.dot_general(
            xw2[9 - i : 329 - i, :].astype(BF), kernel, NT, preferred_element_type=F32
        )
    out2[...] = total
    for c in range(40):
        gf2_ref[:, 128 * c : 128 * (c + 1)] = out2[8 * c + 1 : 8 * c + 5, :].astype(BF)

    for j in range(3):
        for c in range(20):
            first = 256 * (c + 2 - j)
            xw3[8 + 8 * c : 16 + 8 * c, 256 * j : 256 * j + 256] = wide3[:, first : first + 256]
    total = xw3[8:168, 256:512]
    for i in range(3):
        kernel = jnp.concatenate([k3[i, 256 * j : 256 * j + 256, :] for j in range(3)], axis=1)
        total = total + lax.dot_general(
            xw3[9 - i : 169 - i, :].astype(BF), kernel, NT, preferred_element_type=F32
        )
    out3[...] = total
    for c in range(20):
        gf3_ref[:, 256 * c : 256 * (c + 1)] = out3[8 * c + 1 : 8 * c + 3, :].astype(BF)

    rim = rim_ref[...] + above[3:4, 0:1536] + below[3:4, 0:1536]
    for c in range(10):
        cg = rim[:, 128 * (c + 1) : 128 * (c + 2)]
        if c == 0:
            cg = cg + left[20:21, 0:128]
        if c == 9:
            cg = cg + right[20:21, 0:128]
        cg = jnp.broadcast_to(cg[:, 0:64], (8, 64)).astype(BF)
        back = jnp.dot(cg, p4[...], preferred_element_type=F32)
        gf4_ref[0:1, 512 * c : 512 * c + 512] = back[0:1].astype(BF)


def swapped(block, axis, flip):
    return lax.ppermute(block, axis, [(i, i ^ flip) for i in range(lax.axis_size(axis))])


def unpack_kernel(place_ref, mine, got, k1_ref, k2_ref, k3_ref, p2_ref, p3_ref, p4_ref):
    core = place_ref[3]

    def take(side, at, count):
        rows = slice(at, at + count)
        return jnp.where(core == side, mine[rows, :], got[rows, :])

    k3_ref[:, 0:128] = take(0, 0, 2304)
    k3_ref[:, 128:256] = take(1, 0, 2304)
    k2_ref[0:576, :] = take(0, 2304, 576)
    k2_ref[576:1152, :] = take(1, 2304, 576)
    pairs = [take(n % 2, 2880 + 64 * (n // 2), 64) for n in range(12)]
    for n in range(9):
        k1_ref[64 * n : 64 * (n + 1), :] = pairs[n // 2][:, 64 * (n % 2) : 64 * (n % 2) + 64]
    n = 5
    for ref, count in ((p2_ref, 1), (p3_ref, 2), (p4_ref, 4)):
        for m in range(count):
            ref[:, 128 * m : 128 * (m + 1)] = pairs[n]
            n += 1


def call(kernel, out_shapes, scratch, *operands, scalars=0, far=0):
    near = len(operands) - scalars - far
    specs = [pl.BlockSpec(memory_space=space) for space in (pltpu.SMEM, pltpu.VMEM, pl.ANY)]
    outs = len(out_shapes)

    def body(*refs):
        first, last = scalars + near, scalars + near + far
        sources = refs[first:last]
        if far:
            buffers, sems = refs[-1 - far : -1], refs[-1]
            copies = [pltpu.make_async_copy(sources[n], buffers[n], sems.at[n]) for n in range(far)]
            for copy in copies:
                copy.start()
            kernel(*refs[:first], *refs[last : -1 - far], buffers, copies)
        else:
            kernel(*refs)

    return pl.pallas_call(
        body,
        out_shape=[jax.ShapeDtypeStruct(shape, dtype) for shape, dtype in out_shapes],
        in_specs=[specs[0]] * scalars + [specs[1]] * near + [specs[2]] * far,
        out_specs=[specs[1]] * outs,
        scratch_shapes=[pltpu.VMEM(shape, dtype) for shape, dtype in scratch]
        + [pltpu.VMEM(operand.shape, operand.dtype) for operand in operands[len(operands) - far :]]
        + ([pltpu.SemaphoreType.DMA((far,))] if far else []),
        compiler_params=pltpu.CompilerParams(vmem_limit_bytes=48 * 1024 * 1024),
    )(*operands)


def pair_weights(kernel_one):
    none = jnp.zeros((3, FEAT_ONE, FEAT_ONE), BF)
    tap = lambda j: kernel_one[:, j] if 0 <= j < 3 else none
    windows = (1, 2, 3, 0)
    ahead = jnp.concatenate(
        [jnp.concatenate([tap(w - e) for w in windows], axis=1) for e in range(2)], axis=2
    )
    back = jnp.concatenate(
        [jnp.concatenate([tap(e - w + 2) for e in range(2)], axis=1) for w in windows], axis=2
    )
    return ahead, back


def local_part(x1, x2, x3, x4, kernel_one, kernel_two, kernel_three, p2, p3, p4, cot):
    place = jnp.stack(
        [
            lax.axis_index(ROWS),
            lax.axis_index(COLS),
            (lax.axis_index(COLS) == lax.axis_size(COLS) - 1).astype(jnp.int32),
            lax.axis_index("core"),
        ]
    ).astype(jnp.int32)
    ahead, back = pair_weights(kernel_one)
    k2 = kernel_two.reshape(3, 384, 128)
    k3 = kernel_three.reshape(3, 768, 256)
    fars = halos(x1, x2, x3, x4, cot) + (ahead, in_hbm(k2), in_hbm(k3), in_hbm(p2.T), in_hbm(p3.T), in_hbm(p4.T))
    total = RIM + WIDE + RIM
    keep, send, g1, g2, g3, rim, up, down = call(
        forward_kernel,
        [
            ((PACK_ROWS, 128), BF), ((PACK_ROWS, 128), BF),
            ((8, WIDE), BF), ((4, WIDE), BF), ((2, WIDE), BF), ((1, 1536), F32),
            ((4, WIDE), BF), ((4, WIDE), BF),
        ],
        [
            ((16, total), F32), ((16, total), F32), ((16, total), F32), ((8, total), F32), ((8, total), F32),
            ((688, 256), F32), ((720, 384), F32), ((192, 768), F32),
            ((672, 128), F32), ((704, 128), F32), ((176, 256), F32),
            ((656, 128), F32), ((656, 128), F32), ((176, 256), F32),
            ((8, WIDE), F32), ((8, WIDE), F32),
        ],
        place,
        *fars,
        scalars=1,
        far=15,
    )
    return place, keep, send, (g1, g2, g3, rim), up, down, (back, k2, k3, p4.T)


def from_beside(grads, above, below):
    left, right = call(
        rims_kernel, [((32, 256), BF), ((32, 256), BF)], [((32, 256), F32)], *grads, above, below
    )
    return moved(right, COLS, 1), moved(left, COLS, -1)


def input_grads(grads, above, below, left, right, weights):
    return call(
        backward_kernel,
        [((8, WIDE), BF), ((4, WIDE), BF), ((2, WIDE), BF), ((1, WIDE), BF)],
        [
            ((16, 42 * 128), F32), ((8, 42 * 128), F32), ((8, 22 * 256), F32),
            ((656, 256), F32), ((336, 384), F32), ((176, 768), F32),
            ((320, 128), F32), ((160, 256), F32),
        ],
        *grads, above, below, left, right,
        *weights,
    )


def unpacked(place, mine, got):
    outs = call(
        unpack_kernel,
        [((576, 64), BF), ((1152, 128), BF), ((2304, 256), BF), ((64, 128), BF), ((64, 256), BF), ((64, 512), BF)],
        [],
        place, mine, got,
        scalars=1,
    )
    return (
        outs[0].reshape(3, 3, 64, 64), outs[1].reshape(3, 3, 128, 128), outs[2].reshape(3, 3, 256, 256),
        outs[3].T, outs[4].T, outs[5].T,
    )


def on_device(*args):
    place, keep, send, grads, up, down, weights = local_part(*args)
    part = (keep.astype(F32) + swapped(send, "core", 1).astype(F32)).astype(BF)
    part, up, down = lax.optimization_barrier((part, up, down))

    pieces = lax.all_to_all(part.reshape(32, -1, 128), SLAB, 0, 0)
    above, below = moved(down, ROWS, 1), moved(up, ROWS, -1)
    pieces, above, below = lax.optimization_barrier((pieces, above, below))
    part = jnp.sum(pieces.astype(F32), axis=0).astype(BF)

    pieces = lax.all_to_all(jnp.broadcast_to(part[None], (8,) + part.shape), "z_hi", 0, 0)
    left, right = from_beside(grads, above, below)
    outs = input_grads(grads, above, below, left, right, weights)
    pieces, outs = lax.optimization_barrier((pieces, outs))
    part = jnp.sum(pieces.astype(F32), axis=0).astype(BF)

    pieces = jnp.broadcast_to(part[None], (32,) + part.shape)
    mine = lax.all_to_all(pieces, SLAB, 0, 0).reshape(keep.shape)
    return tuple(outs) + unpacked(place, mine, swapped(mine, "core", 1))


def solution(mesh):
    mesh = Mesh(mesh.devices.reshape(8, 2, 2, 4, 2, 2), ROWS + COLS)
    split = P(ROWS, COLS)
    in_specs = (split,) * 4 + (P(),) * 6 + (split,)
    out_specs = (split,) * 4 + (P(),) * 6
    return jax.shard_map(on_device, mesh=mesh, in_specs=in_specs, out_specs=out_specs, check_vma=False)
```

```python
import functools

import jax
import jax.numpy as jnp
from jax import lax
from jax.experimental import pallas as pl
from jax.experimental.pallas import tpu as pltpu
from jax.sharding import Mesh
from jax.sharding import PartitionSpec as P

FEAT_ONE = 64
FEAT_TWO = 128
FEAT_THREE = 256
FEAT_FOUR = 512

ROWS = ("z_hi", "z_lo", "x_lo", "y")
COLS = ("x_hi", "core")
SLAB = ("z_lo", "x_lo", "y", "x_hi")
PACK_ROWS = 3328
WIDE = 5120
RIM = 512
BF = jnp.bfloat16
F32 = jnp.float32
NT = (((1,), (1,)), ((), ()))
TN = (((0,), (0,)), ((), ()))


def moved(block, axis, distance):
    count = lax.axis_size(axis)
    route = [(i, i + distance) for i in range(count) if 0 <= i + distance < count]
    return lax.ppermute(block, axis, route)


def traded(block, axis, start):
    count = lax.axis_size(axis)
    lower = [i for i in range(start, count - 1, 2)]
    return lax.ppermute(block, axis, [(i, i + 1) for i in lower] + [(i + 1, i) for i in lower])


def stacked(parts, rows):
    total, at = None, 0
    for part in parts:
        padded = jnp.pad(part, ((at, rows - at - part.shape[0]), (0, 0)))
        total = padded if total is None else total + padded
        at += part.shape[0]
    return total


def in_hbm(x):
    return pltpu.with_memory_space_constraint(x, pltpu.HBM)


def edge_kernel(place_ref, odd_ref, even_ref, outer_ref, inner_ref, last, first, right, left, near, copies):
    even = lax.rem(place_ref[0], 2) == 0
    core = place_ref[3]
    right[...] = jnp.zeros_like(right)
    left[...] = jnp.zeros_like(left)
    for copy in copies:
        copy.wait()
    x1, cot, x2, x3, x4 = (ref[...].astype(F32) for ref in near)
    for out, ones, cots, twos in ((last, x1[5:8], cot[6:8], x2[1:4]), (first, x1[0:3], cot[0:2], x2[0:3])):
        out[0:3, :] = ones
        out[3:5, :] = cots
        out[5:8, :] = twos
        out[8:10, :] = x3
        out[10:11, :] = x4
        out[11:16, :] = jnp.zeros((5, WIDE), F32)
    odd_ref[...] = jnp.where(even, first[...], last[...]).astype(BF)
    even_ref[...] = jnp.where(even, last[...], first[...]).astype(BF)
    for out, cols in ((right, slice(WIDE - RIM, WIDE)), (left, slice(0, RIM))):
        out[0:8, :] = x1[:, cols]
        out[8:16, :] = cot[:, cols]
        out[16:20, :] = x2[:, cols]
        out[20:22, :] = x3[:, cols]
        out[22:23, :] = x4[:, cols]
    outer_ref[...] = jnp.where(core == 0, left[...], right[...]).astype(BF)
    inner_ref[...] = jnp.where(core == 0, right[...], left[...]).astype(BF)


def halos(place, x1, x2, x3, x4, cot):
    own = tuple(in_hbm(x) for x in (x1, cot, x2, x3, x4))
    odd, even, outer, inner = call(
        edge_kernel,
        [((16, WIDE), BF), ((16, WIDE), BF), ((24, RIM), BF), ((24, RIM), BF)],
        [((16, WIDE), F32), ((16, WIDE), F32), ((24, RIM), F32), ((24, RIM), F32)],
        place,
        *own,
        scalars=1,
        far=5,
    )
    odd = traded(odd, ROWS, 1)
    even = traded(even, ROWS, 0)
    core = lax.axis_index("core")
    starts = [(v[:11, :RIM], v[:11, -RIM:]) for v in (odd, even)]
    outer = stacked([outer] + [jnp.where(core == 0, a, b) for a, b in starts], 48)
    inner = stacked([inner] + [jnp.where(core == 0, b, a) for a, b in starts], 48)
    return own + (odd, even, traded(outer, COLS, 1), traded(inner, COLS, 0))


def gelu_both(v):
    c = 0.7978845608028654
    sq = v * v
    t = jnp.tanh(c * v * (1.0 + 0.044715 * sq))
    half = 0.5 * (1.0 + t)
    slope = half + 0.5 * v * (1.0 - t * t) * (c * (1.0 + 3.0 * 0.044715 * sq))
    return v * half, slope


def tile(wide, at):
    return wide[:, 128 * at : 128 * (at + 1)]


def row_weights(shape, coarse_dim, row_block):
    k = lax.broadcasted_iota(jnp.int32, shape, coarse_dim)
    r = lax.broadcasted_iota(jnp.int32, shape, 1 - coarse_dim)
    two, three = k < 16, k < 24
    scale = jnp.where(two, 2, jnp.where(three, 4, 8))
    count = jnp.where(two, 4, jnp.where(three, 2, 1))
    shift = jnp.where(two, 3, jnp.where(three, 16 + 2, 24 + 1))
    total = (jnp.where(two, 512, jnp.where(three, 256, 128)) - 1).astype(F32)
    coarse = (row_block * count + k - shift).astype(F32)
    fine = (row_block * 8 + r - 4).astype(F32)
    inverse = jnp.where(two, 0.5, jnp.where(three, 0.25, 0.125)).astype(F32)
    place = jnp.clip((fine + 0.5) * inverse - 0.5, 0.0, total)
    return jnp.maximum(0.0, 1.0 - jnp.abs(place - coarse))


def forward_kernel(
    place_ref, keep_ref, send_ref, g1_ref, g2_ref, g3_ref, rim_ref, up_ref, down_ref,
    wx1, wc, wx2, wx3, wx4, xw1, xw2, xw3, d1, d2, d3, gm1, gm2, gm3, upward, downward,
    near, copies,
):
    x1, cot, x2, x3, x4, odd, even, outer, inner, t1, k2, k3, p2, p3, p4 = near
    row_block = place_ref[0]
    at_left = place_ref[1] == 0
    at_right = place_ref[2] == 1
    core = place_ref[3]
    lane = lax.broadcasted_iota(jnp.int32, (1, 128), 1)
    low = lane < 64

    def lanes(a, b):
        return jnp.where(low, a, b).astype(F32)

    for ref in (wx1, wc, wx2, wx3, wx4, upward, downward):
        ref[...] = jnp.zeros_like(ref)
    for copy in copies[:10]:
        copy.wait()
    is_even = lax.rem(row_block, 2) == 0
    outer, inner = outer[...].astype(F32), inner[...].astype(F32)
    left, right = jnp.where(core == 0, outer, inner), jnp.where(core == 0, inner, outer)
    for side, to in ((None, RIM), (left, 0), (right, RIM + WIDE)):
        if side is None:
            cols = slice(to, to + WIDE)
            mid = [ref[...].astype(F32) for ref in (x1, cot, x2, x3, x4)]
            by_odd, by_even = odd[...].astype(F32), even[...].astype(F32)
        else:
            cols = slice(to, to + RIM)
            mid = [side[0:8], side[8:16], side[16:20], side[20:22], side[22:23]]
            by_odd, by_even = side[24:35], side[35:46]
        up, down = jnp.where(is_even, by_odd, by_even), jnp.where(is_even, by_even, by_odd)
        wx1[1:4, cols] = up[0:3]
        wx1[4:12, cols] = mid[0]
        wx1[12:15, cols] = down[0:3]
        wc[2:4, cols] = up[3:5]
        wc[4:12, cols] = mid[1]
        wc[12:14, cols] = down[3:5]
        wx2[0:3, cols] = up[5:8]
        wx2[3:7, cols] = mid[2]
        wx2[7:10, cols] = down[5:8]
        wx3[0:2, cols] = up[8:10]
        wx3[2:4, cols] = mid[3]
        wx3[4:6, cols] = down[8:10]
        wx4[0:1, cols] = up[10:11]
        wx4[1:2, cols] = mid[4]
        wx4[2:3, cols] = down[10:11]

    for f in range(-1, 41):
        at = 8 + 16 * (f + 1)
        xw1[at : at + 16, 0:128] = tile(wx1, 4 + f)
        xw1[at : at + 16, 128:256] = jnp.where(low, tile(wx1, 5 + f), tile(wx1, 3 + f))
    xw1[0:8, :] = jnp.zeros((8, 256), F32)
    xw1[680:688, :] = jnp.zeros((8, 256), F32)
    pre1 = xw1[8:680, 0:128]
    for i in range(3):
        pre1 = pre1 + jnp.dot(xw1[7 + i : 679 + i, :].astype(BF), t1[i], preferred_element_type=F32)
    y1, slope = gelu_both(pre1)
    y1 = y1.astype(BF).astype(F32)
    d1[...] = slope

    copies[10].wait()
    for j in range(3):
        for c in range(-2, 42):
            at = 8 + 16 * (c + 2)
            xw2[at : at + 16, 128 * j : 128 * j + 128] = tile(wx2, 3 + c + j)
    xw2[0:8, :] = jnp.zeros((8, 384), F32)
    xw2[712:720, :] = jnp.zeros((8, 384), F32)
    pre2 = xw2[8:712, 128:256]
    for i in range(3):
        pre2 = pre2 + jnp.dot(xw2[7 + i : 711 + i, :].astype(BF), k2[i], preferred_element_type=F32)
    y2, slope = gelu_both(pre2)
    y2 = y2.astype(BF)
    d2[...] = slope

    copies[11].wait()
    for j in range(3):
        for c in range(-1, 21):
            at = 8 + 8 * (c + 1)
            first = RIM + 256 * (c + j - 1)
            xw3[at : at + 8, 256 * j : 256 * j + 256] = wx3[:, first : first + 256]
    xw3[0:8, :] = jnp.zeros((8, 768), F32)
    xw3[184:192, :] = jnp.zeros((8, 768), F32)
    pre3 = xw3[8:184, 256:512]
    for i in range(3):
        pre3 = pre3 + jnp.dot(xw3[7 + i : 183 + i, :].astype(BF), k3[i], preferred_element_type=F32)
    y3, slope = gelu_both(pre3)
    y3 = y3.astype(BF)
    d3[...] = slope

    y4 = jnp.concatenate([wx4[:, 512 * c : 512 * c + 512] for c in range(12)], axis=0).astype(BF)

    for copy in copies[12:]:
        copy.wait()
    weights = row_weights((16, 32), 1, row_block).astype(BF)
    rows_up = []
    for y, p, rim, rows, wlo in ((y2, p2, 2, 16, 0), (y3, p3, 1, 8, 16), (y4, p4, 1, 8, 24)):
        twice = jnp.concatenate([p[...], p[...]], axis=0)
        coarse = lax.dot_general(y, twice, NT, preferred_element_type=F32).astype(BF).astype(F32)
        cols = [coarse[rows * n : rows * (n + 1)] for n in range(coarse.shape[0] // rows)]
        end = len(cols) - rim
        cols[rim - 1] = jnp.where(at_left, cols[rim], cols[rim - 1])
        cols[end] = jnp.where(at_right, cols[end - 1], cols[end])
        flat = jnp.concatenate(cols, axis=1).astype(BF)
        rows_up.append(jnp.dot(weights[:, wlo : wlo + rows], flat, preferred_element_type=F32))
    up2, up3, up4 = rows_up

    gates = []
    for f in range(-1, 41):
        k = f + 2
        merged = y1[16 * (f + 1) : 16 * (f + 2)]
        merged = merged + 0.75 * tile(up2, k) + 0.25 * jnp.where(low, tile(up2, k - 1), tile(up2, k + 1))
        k, h = f // 2 + 1, f % 2
        if h == 0:
            merged = merged + lanes(0.375, 0.125) * tile(up3, k - 1) + lanes(0.625, 0.875) * tile(up3, k)
        else:
            merged = merged + lanes(0.875, 0.625) * tile(up3, k) + lanes(0.125, 0.375) * tile(up3, k + 1)
        k, h = f // 4 + 1, f % 4
        p_low, p_high = (2 * h + 0.5) / 8 - 0.5, (2 * h + 1.5) / 8 - 0.5
        other = k - 1 if h < 2 else k + 1
        merged = merged + lanes(1 - abs(p_low), 1 - abs(p_high)) * tile(up4, k)
        merged = merged + lanes(abs(p_low), abs(p_high)) * tile(up4, other)
        slope = gelu_both(merged)[1]
        gate = (slope * tile(wc, 4 + f)).astype(BF).astype(F32)
        gates.append(gate)
        if 0 <= f < 40:
            g = (d1[16 * (f + 1) : 16 * (f + 2)] * gate).astype(BF).astype(F32)
            row = lax.broadcasted_iota(jnp.int32, (16, 1), 0)
            gm1[8 + 16 * f : 24 + 16 * f, :] = jnp.where((row >= 4) & (row < 12), g, 0.0)
            cols = slice(128 * f, 128 * (f + 1))
            g1_ref[:, cols] = g[4:12].astype(BF)
            upward[0:1, cols] = g[4:5]
            downward[0:1, cols] = g[11:12]
    gm1[0:8, :] = jnp.zeros((8, 128), F32)
    gm1[648:656, :] = jnp.zeros((8, 128), F32)

    flat = jnp.concatenate(gates, axis=1).astype(BF)
    weights_back = row_weights((32, 16), 0, row_block)
    k = lax.broadcasted_iota(jnp.int32, (32, 16), 0)
    r = lax.broadcasted_iota(jnp.int32, (32, 16), 1)
    weights_back = jnp.where((k < 24) | ((r >= 4) & (r < 12)), weights_back, 0.0).astype(BF)
    down = jnp.dot(weights_back, flat, preferred_element_type=F32)
    down2, down3, down4 = down[0:16], down[16:24], down[24:32]

    def folded(v):
        return v + pltpu.roll(v, 64, 1)

    cg2 = []
    for c in range(40):
        v = 0.75 * tile(down2, c + 1) + 0.25 * jnp.where(low, tile(down2, c + 2), tile(down2, c))
        if c == 0:
            v = v + jnp.where(at_left, lanes(0.25, 0.0) * tile(down2, 1), 0.0)
        if c == 39:
            v = v + jnp.where(at_right, lanes(0.0, 0.25) * tile(down2, 40), 0.0)
        cg2.append(folded(v))
    cg3 = []
    for c in range(20):
        at = 2 * c
        v = lanes(0.125, 0.375) * tile(down3, at) + lanes(0.625, 0.875) * tile(down3, at + 1)
        v = v + lanes(0.875, 0.625) * tile(down3, at + 2) + lanes(0.375, 0.125) * tile(down3, at + 3)
        if c == 0:
            v = v + jnp.where(at_left, lanes(0.375, 0.125) * tile(down3, 1), 0.0)
        if c == 19:
            v = v + jnp.where(at_right, lanes(0.125, 0.375) * tile(down3, 40), 0.0)
        cg3.append(folded(v))
    cg4 = []
    for c in range(-1, 11):
        v = jnp.zeros((8, 128), F32)
        for n in range(8):
            a, b = (2 * n + 0.5) / 8, (2 * n + 1.5) / 8
            a, b = (a, b) if n < 4 else (2 - a, 2 - b)
            pair = 4 * c - 2 + n
            if 0 <= pair < 40:
                v = v + lanes(a, b) * tile(down4, pair + 1)
        cg4.append(folded(v))
    cg4[1] = cg4[1] + jnp.where(at_left, cg4[0], 0.0)
    cg4[-2] = cg4[-2] + jnp.where(at_right, cg4[-1], 0.0)
    cg4[0] = jnp.where(at_left, 0.0, cg4[0])
    cg4[-1] = jnp.where(at_right, 0.0, cg4[-1])
    for n in range(12):
        cols = slice(128 * n, 128 * (n + 1))
        upward[3:4, cols] = cg4[n][0:1]
        rim_ref[0:1, cols] = cg4[n][1:2]
        downward[3:4, cols] = cg4[n][2:3]

    flat2 = jnp.concatenate(cg2, axis=0).astype(BF).astype(F32)
    flat3 = jnp.concatenate(cg3, axis=0).astype(BF).astype(F32)
    flat4 = jnp.concatenate(cg4, axis=0).astype(BF).astype(F32)
    back2 = jnp.dot(flat2[:, 0:64].astype(BF), p2[...], preferred_element_type=F32)
    back3 = jnp.dot(flat3[:, 0:64].astype(BF), p3[...], preferred_element_type=F32)
    g2 = (d2[32:672, :] * back2).astype(BF).astype(F32)
    g3 = (d3[8:168, :] * back3).astype(BF).astype(F32)

    row2 = lax.broadcasted_iota(jnp.int32, (640, 1), 0) % 16
    own2 = (row2 >= 3) & (row2 < 7)
    row3 = lax.broadcasted_iota(jnp.int32, (160, 1), 0) % 8
    own3 = (row3 >= 2) & (row3 < 4)
    gm2[0:8, :] = jnp.zeros((8, 128), F32)
    gm2[8:648, :] = jnp.where(own2, g2, 0.0)
    gm2[648:656, :] = jnp.zeros((8, 128), F32)
    gm3[0:8, :] = jnp.zeros((8, 256), F32)
    gm3[8:168, :] = jnp.where(own3, g3, 0.0)
    gm3[168:176, :] = jnp.zeros((8, 256), F32)
    for c in range(40):
        at, cols = 8 + 16 * c + 3, slice(128 * c, 128 * (c + 1))
        g2_ref[:, cols] = gm2[at : at + 4, :].astype(BF)
        upward[1:2, cols] = gm2[at : at + 1, :]
        downward[1:2, cols] = gm2[at + 3 : at + 4, :]
    for c in range(20):
        at, cols = 8 + 8 * c + 2, slice(256 * c, 256 * (c + 1))
        g3_ref[:, cols] = gm3[at : at + 2, :].astype(BF)
        upward[2:3, cols] = gm3[at : at + 1, :]
        downward[2:3, cols] = gm3[at + 1 : at + 2, :]
    up_ref[...] = upward[0:4, :].astype(BF)
    down_ref[...] = downward[0:4, :].astype(BF)

    def put(at, first, second):
        rows = slice(at, at + first.shape[0])
        keep_ref[rows, :] = jnp.where(core == 0, first, second).astype(BF)
        send_ref[rows, :] = jnp.where(core == 0, second, first).astype(BF)

    cells = 327680
    x = xw3[16:176, :].astype(BF)
    shifted = jnp.concatenate([gm3[9 - i : 169 - i, :] for i in range(3)], axis=1).astype(BF)
    z = lax.dot_general(x, shifted, TN, preferred_element_type=F32) * (cells // 16) ** -0.5
    for i in range(3):
        put(768 * i, z[:, 256 * i : 256 * i + 128], z[:, 256 * i + 128 : 256 * i + 256])
    x = xw2[40:680, :].astype(BF)
    shifted = jnp.concatenate([gm2[9 - i : 649 - i, :] for i in range(3)], axis=1).astype(BF)
    z = lax.dot_general(x, shifted, TN, preferred_element_type=F32) * (cells // 4) ** -0.5
    put(2304, z[0:192, 0:128], z[192:384, 128:256])
    put(2496, z[192:384, 0:128], z[0:192, 256:384])
    put(2688, z[0:192, 128:256], z[192:384, 256:384])
    x = xw1[24:664, :].astype(BF)
    shifted = jnp.concatenate([gm1[9 - i : 649 - i, :] for i in range(3)], axis=1).astype(BF)
    z = lax.dot_general(x, shifted, TN, preferred_element_type=F32) * cells**-0.5
    window = (192, 0, 64, 128)
    blocks = []
    for i in range(3):
        zi = z[:, 128 * i : 128 * (i + 1)]
        for j in range(3):
            a, b = window[j], window[j + 1]
            blocks.append(zi[a : a + 64] + pltpu.roll(zi[b : b + 64], 64, 1))
    blocks.append(jnp.zeros((64, 128), F32))
    pairs = [jnp.where(low, blocks[n], pltpu.roll(blocks[n + 1], 64, 1)) for n in range(0, 10, 2)]
    y2_own, y3_own = y2[32:672], y3.astype(F32)[8:168].astype(BF)
    for y, flat, mask, branch in (
        (y2_own, flat2, own2, 1),
        (y3_own, flat3, own3, 2),
        (y4, flat4, None, 3),
    ):
        masked = (flat if mask is None else jnp.where(mask, flat, 0.0)).astype(BF)
        z = lax.dot_general(masked, y, TN, preferred_element_type=F32) * (cells // 4**branch) ** -0.5
        pairs += [z[0:64, 128 * n : 128 * (n + 1)] for n in range(z.shape[1] // 128)]
    for n in range(6):
        put(2880 + 64 * n, pairs[2 * n], pairs[2 * n + 1])
    put(3264, jnp.zeros((64, 128), F32), jnp.zeros((64, 128), F32))


def rims_kernel(g1_ref, g2_ref, g3_ref, rim_ref, above_ref, below_ref, left_ref, right_ref, out):
    g1, g2, g3, above, below = (ref[...].astype(F32) for ref in (g1_ref, g2_ref, g3_ref, above_ref, below_ref))
    rim = rim_ref[...] + above[3:4, 0:1536] + below[3:4, 0:1536]
    for ref, one, three, four in ((left_ref, 0, 0, 0), (right_ref, WIDE - 128, WIDE - 256, 1408)):
        ones, threes = slice(one, one + 128), slice(three, three + 256)
        out[...] = jnp.zeros_like(out)
        out[0:1, 0:128] = above[0:1, ones]
        out[1:9, 0:128] = g1[:, ones]
        out[9:10, 0:128] = below[0:1, ones]
        out[10:11, 0:128] = above[1:2, ones]
        out[11:15, 0:128] = g2[:, ones]
        out[15:16, 0:128] = below[1:2, ones]
        out[16:17, :] = above[2:3, threes]
        out[17:19, :] = g3[:, threes]
        out[19:20, :] = below[2:3, threes]
        out[20:21, 0:128] = rim[:, four : four + 128]
        ref[...] = out[...].astype(BF)


def backward_kernel(
    g1_ref, g2_ref, g3_ref, rim_ref, above_ref, below_ref, left_ref, right_ref, t1b, k2, k3, p4,
    gf1_ref, gf2_ref, gf3_ref, gf4_ref, wide1, wide2, wide3, xw1, xw2, xw3, out2, out3,
):
    low = lax.broadcasted_iota(jnp.int32, (1, 128), 1) < 64
    for ref, n in ((xw1, 640), (xw2, 320), (xw3, 160)):
        ref[0:8, :] = jnp.zeros((8, ref.shape[1]), F32)
        ref[8 + n : 16 + n, :] = jnp.zeros((8, ref.shape[1]), F32)
    above, below, left, right = (ref[...].astype(F32) for ref in (above_ref, below_ref, left_ref, right_ref))
    for n, (wide, g_ref, top, rows, start, step) in enumerate(
        ((wide1, g1_ref, 3, 8, 0, 128), (wide2, g2_ref, 0, 4, 10, 128), (wide3, g3_ref, 0, 2, 16, 256))
    ):
        wide[...] = jnp.zeros_like(wide)
        mid, end = slice(step, step + WIDE), step + WIDE
        wide[top : top + 1, mid] = above[n : n + 1]
        wide[top + 1 : top + 1 + rows, mid] = g_ref[...].astype(F32)
        wide[top + 1 + rows : top + 2 + rows, mid] = below[n : n + 1]
        wide[top : top + 2 + rows, 0:step] = left[start : start + 2 + rows, 0:step]
        wide[top : top + 2 + rows, end : end + step] = right[start : start + 2 + rows, 0:step]

    for f in range(40):
        at = 8 + 16 * f
        xw1[at : at + 16, 0:128] = tile(wide1, f + 1)
        xw1[at : at + 16, 128:256] = jnp.where(low, tile(wide1, f + 2), tile(wide1, f))
    total = xw1[8:648, 0:128]
    for i in range(3):
        total = total + lax.dot_general(
            xw1[9 - i : 649 - i, :].astype(BF), t1b[i], NT, preferred_element_type=F32
        )
    for f in range(40):
        gf1_ref[:, 128 * f : 128 * (f + 1)] = total[16 * f + 4 : 16 * f + 12].astype(BF)

    for j in range(3):
        for c in range(40):
            xw2[8 + 8 * c : 16 + 8 * c, 128 * j : 128 * j + 128] = tile(wide2, c + 2 - j)
    total = xw2[8:328, 128:256]
    for i in range(3):
        kernel = jnp.concatenate([k2[i, 128 * j : 128 * j + 128, :] for j in range(3)], axis=1)
        total = total + lax.dot_general(
            xw2[9 - i : 329 - i, :].astype(BF), kernel, NT, preferred_element_type=F32
        )
    out2[...] = total
    for c in range(40):
        gf2_ref[:, 128 * c : 128 * (c + 1)] = out2[8 * c + 1 : 8 * c + 5, :].astype(BF)

    for j in range(3):
        for c in range(20):
            first = 256 * (c + 2 - j)
            xw3[8 + 8 * c : 16 + 8 * c, 256 * j : 256 * j + 256] = wide3[:, first : first + 256]
    total = xw3[8:168, 256:512]
    for i in range(3):
        kernel = jnp.concatenate([k3[i, 256 * j : 256 * j + 256, :] for j in range(3)], axis=1)
        total = total + lax.dot_general(
            xw3[9 - i : 169 - i, :].astype(BF), kernel, NT, preferred_element_type=F32
        )
    out3[...] = total
    for c in range(20):
        gf3_ref[:, 256 * c : 256 * (c + 1)] = out3[8 * c + 1 : 8 * c + 3, :].astype(BF)

    rim = rim_ref[...] + above[3:4, 0:1536] + below[3:4, 0:1536]
    for c in range(10):
        cg = rim[:, 128 * (c + 1) : 128 * (c + 2)]
        if c == 0:
            cg = cg + left[20:21, 0:128]
        if c == 9:
            cg = cg + right[20:21, 0:128]
        cg = jnp.broadcast_to(cg[:, 0:64], (8, 64)).astype(BF)
        back = jnp.dot(cg, p4[...], preferred_element_type=F32)
        gf4_ref[0:1, 512 * c : 512 * c + 512] = back[0:1].astype(BF)


def swapped(block, axis, flip):
    return lax.ppermute(block, axis, [(i, i ^ flip) for i in range(lax.axis_size(axis))])


def unpack_kernel(place_ref, mine, got, k1_ref, k2_ref, k3_ref, p2_ref, p3_ref, p4_ref):
    core = place_ref[3]

    def take(side, at, count):
        rows = slice(at, at + count)
        return jnp.where(core == side, mine[rows, :], got[rows, :])

    k3_ref[:, 0:128] = take(0, 0, 2304)
    k3_ref[:, 128:256] = take(1, 0, 2304)
    k2_ref[0:576, :] = take(0, 2304, 576)
    k2_ref[576:1152, :] = take(1, 2304, 576)
    pairs = [take(n % 2, 2880 + 64 * (n // 2), 64) for n in range(12)]
    for n in range(9):
        k1_ref[64 * n : 64 * (n + 1), :] = pairs[n // 2][:, 64 * (n % 2) : 64 * (n % 2) + 64]
    n = 5
    for ref, count in ((p2_ref, 1), (p3_ref, 2), (p4_ref, 4)):
        for m in range(count):
            ref[:, 128 * m : 128 * (m + 1)] = pairs[n]
            n += 1


def call(kernel, out_shapes, scratch, *operands, scalars=0, far=0):
    near = len(operands) - scalars - far
    specs = [pl.BlockSpec(memory_space=space) for space in (pltpu.SMEM, pltpu.VMEM, pl.ANY)]
    outs = len(out_shapes)

    def body(*refs):
        first, last = scalars + near, scalars + near + far
        sources = refs[first:last]
        if far:
            buffers, sems = refs[-1 - far : -1], refs[-1]
            copies = [pltpu.make_async_copy(sources[n], buffers[n], sems.at[n]) for n in range(far)]
            for copy in copies:
                copy.start()
            kernel(*refs[:first], *refs[last : -1 - far], buffers, copies)
        else:
            kernel(*refs)

    return pl.pallas_call(
        body,
        out_shape=[jax.ShapeDtypeStruct(shape, dtype) for shape, dtype in out_shapes],
        in_specs=[specs[0]] * scalars + [specs[1]] * near + [specs[2]] * far,
        out_specs=[specs[1]] * outs,
        scratch_shapes=[pltpu.VMEM(shape, dtype) for shape, dtype in scratch]
        + [pltpu.VMEM(operand.shape, operand.dtype) for operand in operands[len(operands) - far :]]
        + ([pltpu.SemaphoreType.DMA((far,))] if far else []),
        compiler_params=pltpu.CompilerParams(vmem_limit_bytes=48 * 1024 * 1024),
    )(*operands)


def pair_weights(kernel_one):
    none = jnp.zeros((3, FEAT_ONE, FEAT_ONE), BF)
    tap = lambda j: kernel_one[:, j] if 0 <= j < 3 else none
    windows = (1, 2, 3, 0)
    ahead = jnp.concatenate(
        [jnp.concatenate([tap(w - e) for w in windows], axis=1) for e in range(2)], axis=2
    )
    back = jnp.concatenate(
        [jnp.concatenate([tap(e - w + 2) for e in range(2)], axis=1) for w in windows], axis=2
    )
    return ahead, back


def local_part(x1, x2, x3, x4, kernel_one, kernel_two, kernel_three, p2, p3, p4, cot):
    place = jnp.stack(
        [
            lax.axis_index(ROWS),
            lax.axis_index(COLS),
            (lax.axis_index(COLS) == lax.axis_size(COLS) - 1).astype(jnp.int32),
            lax.axis_index("core"),
        ]
    ).astype(jnp.int32)
    ahead, back = pair_weights(kernel_one)
    k2 = kernel_two.reshape(3, 384, 128)
    k3 = kernel_three.reshape(3, 768, 256)
    fars = halos(place, x1, x2, x3, x4, cot) + (ahead, in_hbm(k2), in_hbm(k3), in_hbm(p2.T), in_hbm(p3.T), in_hbm(p4.T))
    total = RIM + WIDE + RIM
    keep, send, g1, g2, g3, rim, up, down = call(
        forward_kernel,
        [
            ((PACK_ROWS, 128), BF), ((PACK_ROWS, 128), BF),
            ((8, WIDE), BF), ((4, WIDE), BF), ((2, WIDE), BF), ((1, 1536), F32),
            ((4, WIDE), BF), ((4, WIDE), BF),
        ],
        [
            ((16, total), F32), ((16, total), F32), ((16, total), F32), ((8, total), F32), ((8, total), F32),
            ((688, 256), F32), ((720, 384), F32), ((192, 768), F32),
            ((672, 128), F32), ((704, 128), F32), ((176, 256), F32),
            ((656, 128), F32), ((656, 128), F32), ((176, 256), F32),
            ((8, WIDE), F32), ((8, WIDE), F32),
        ],
        place,
        *fars,
        scalars=1,
        far=15,
    )
    return place, keep, send, (g1, g2, g3, rim), up, down, (back, k2, k3, p4.T)


def from_beside(grads, above, below):
    left, right = call(
        rims_kernel, [((32, 256), BF), ((32, 256), BF)], [((32, 256), F32)], *grads, above, below
    )
    return moved(right, COLS, 1), moved(left, COLS, -1)


def input_grads(grads, above, below, left, right, weights):
    return call(
        backward_kernel,
        [((8, WIDE), BF), ((4, WIDE), BF), ((2, WIDE), BF), ((1, WIDE), BF)],
        [
            ((16, 42 * 128), F32), ((8, 42 * 128), F32), ((8, 22 * 256), F32),
            ((656, 256), F32), ((336, 384), F32), ((176, 768), F32),
            ((320, 128), F32), ((160, 256), F32),
        ],
        *grads, above, below, left, right,
        *weights,
    )


def unpacked(place, mine, got):
    outs = call(
        unpack_kernel,
        [((576, 64), BF), ((1152, 128), BF), ((2304, 256), BF), ((64, 128), BF), ((64, 256), BF), ((64, 512), BF)],
        [],
        place, mine, got,
        scalars=1,
    )
    return (
        outs[0].reshape(3, 3, 64, 64), outs[1].reshape(3, 3, 128, 128), outs[2].reshape(3, 3, 256, 256),
        outs[3].T, outs[4].T, outs[5].T,
    )


def on_device(*args):
    place, keep, send, grads, up, down, weights = local_part(*args)
    part = (keep.astype(F32) + swapped(send, "core", 1).astype(F32)).astype(BF)
    part, up, down = lax.optimization_barrier((part, up, down))

    pieces = lax.all_to_all(part.reshape(32, -1, 128), SLAB, 0, 0)
    above, below = moved(down, ROWS, 1), moved(up, ROWS, -1)
    pieces, above, below = lax.optimization_barrier((pieces, above, below))
    part = jnp.sum(pieces.astype(F32), axis=0).astype(BF)

    pieces = lax.all_to_all(jnp.broadcast_to(part[None], (8,) + part.shape), "z_hi", 0, 0)
    left, right = from_beside(grads, above, below)
    outs = input_grads(grads, above, below, left, right, weights)
    pieces, outs = lax.optimization_barrier((pieces, outs))
    part = jnp.sum(pieces.astype(F32), axis=0).astype(BF)

    pieces = jnp.broadcast_to(part[None], (32,) + part.shape)
    mine = lax.all_to_all(pieces, SLAB, 0, 0).reshape(keep.shape)
    return tuple(outs) + unpacked(place, mine, swapped(mine, "core", 1))


def solution(mesh):
    mesh = Mesh(mesh.devices.reshape(8, 2, 2, 4, 2, 2), ROWS + COLS)
    split = P(ROWS, COLS)
    in_specs = (split,) * 4 + (P(),) * 6 + (split,)
    out_specs = (split,) * 4 + (P(),) * 6
    return jax.shard_map(on_device, mesh=mesh, in_specs=in_specs, out_specs=out_specs, check_vma=False)
```

```python
import functools

import jax
import jax.numpy as jnp
from jax import lax
from jax.experimental import pallas as pl
from jax.experimental.pallas import tpu as pltpu
from jax.sharding import Mesh
from jax.sharding import PartitionSpec as P

FEAT_ONE = 64
FEAT_TWO = 128
FEAT_THREE = 256
FEAT_FOUR = 512

ROWS = ("z_hi", "z_lo", "x_lo", "y")
COLS = ("x_hi", "core")
SLAB = ("z_lo", "x_lo", "y", "x_hi")
PACK_ROWS = 3328
WIDE = 5120
RIM = 512
BF = jnp.bfloat16
F32 = jnp.float32
NT = (((1,), (1,)), ((), ()))
TN = (((0,), (0,)), ((), ()))


def traded(block, axis, start):
    count = lax.axis_size(axis)
    lower = [i for i in range(start, count - 1, 2)]
    return lax.ppermute(block, axis, [(i, i + 1) for i in lower] + [(i + 1, i) for i in lower])


def stacked(parts, rows):
    total, at = None, 0
    for part in parts:
        padded = jnp.pad(part, ((at, rows - at - part.shape[0]), (0, 0)))
        total = padded if total is None else total + padded
        at += part.shape[0]
    return total


def in_hbm(x):
    return pltpu.with_memory_space_constraint(x, pltpu.HBM)


def edge_kernel(place_ref, odd_ref, even_ref, outer_ref, inner_ref, last, first, right, left, near, copies):
    even = lax.rem(place_ref[0], 2) == 0
    core = place_ref[3]
    right[...] = jnp.zeros_like(right)
    left[...] = jnp.zeros_like(left)
    for copy in copies:
        copy.wait()
    x1, cot, x2, x3, x4 = (ref[...].astype(F32) for ref in near)
    for out, ones, cots, twos in ((last, x1[5:8], cot[6:8], x2[1:4]), (first, x1[0:3], cot[0:2], x2[0:3])):
        out[0:3, :] = ones
        out[3:5, :] = cots
        out[5:8, :] = twos
        out[8:10, :] = x3
        out[10:11, :] = x4
        out[11:16, :] = jnp.zeros((5, WIDE), F32)
    odd_ref[...] = jnp.where(even, first[...], last[...]).astype(BF)
    even_ref[...] = jnp.where(even, last[...], first[...]).astype(BF)
    for out, cols in ((right, slice(WIDE - RIM, WIDE)), (left, slice(0, RIM))):
        out[0:8, :] = x1[:, cols]
        out[8:16, :] = cot[:, cols]
        out[16:20, :] = x2[:, cols]
        out[20:22, :] = x3[:, cols]
        out[22:23, :] = x4[:, cols]
    outer_ref[...] = jnp.where(core == 0, left[...], right[...]).astype(BF)
    inner_ref[...] = jnp.where(core == 0, right[...], left[...]).astype(BF)


def halos(place, x1, x2, x3, x4, cot):
    own = tuple(in_hbm(x) for x in (x1, cot, x2, x3, x4))
    odd, even, outer, inner = call(
        edge_kernel,
        [((16, WIDE), BF), ((16, WIDE), BF), ((24, RIM), BF), ((24, RIM), BF)],
        [((16, WIDE), F32), ((16, WIDE), F32), ((24, RIM), F32), ((24, RIM), F32)],
        place,
        *own,
        scalars=1,
        far=5,
    )
    odd = traded(odd, ROWS, 1)
    even = traded(even, ROWS, 0)
    core = lax.axis_index("core")
    starts = [(v[:11, :RIM], v[:11, -RIM:]) for v in (odd, even)]
    outer = stacked([outer] + [jnp.where(core == 0, a, b) for a, b in starts], 48)
    inner = stacked([inner] + [jnp.where(core == 0, b, a) for a, b in starts], 48)
    return own + (odd, even, traded(outer, COLS, 1), traded(inner, COLS, 0))


def gelu_both(v):
    c = 0.7978845608028654
    sq = v * v
    t = jnp.tanh(c * v * (1.0 + 0.044715 * sq))
    half = 0.5 * (1.0 + t)
    slope = half + 0.5 * v * (1.0 - t * t) * (c * (1.0 + 3.0 * 0.044715 * sq))
    return v * half, slope


def tile(wide, at):
    return wide[:, 128 * at : 128 * (at + 1)]


def row_weights(shape, coarse_dim, row_block):
    k = lax.broadcasted_iota(jnp.int32, shape, coarse_dim)
    r = lax.broadcasted_iota(jnp.int32, shape, 1 - coarse_dim)
    two, three = k < 16, k < 24
    scale = jnp.where(two, 2, jnp.where(three, 4, 8))
    count = jnp.where(two, 4, jnp.where(three, 2, 1))
    shift = jnp.where(two, 3, jnp.where(three, 16 + 2, 24 + 1))
    total = (jnp.where(two, 512, jnp.where(three, 256, 128)) - 1).astype(F32)
    coarse = (row_block * count + k - shift).astype(F32)
    fine = (row_block * 8 + r - 4).astype(F32)
    inverse = jnp.where(two, 0.5, jnp.where(three, 0.25, 0.125)).astype(F32)
    place = jnp.clip((fine + 0.5) * inverse - 0.5, 0.0, total)
    return jnp.maximum(0.0, 1.0 - jnp.abs(place - coarse))


def forward_kernel(
    place_ref, keep_ref, send_ref, g1_ref, g2_ref, g3_ref, rim_ref, odd_ref, even_ref,
    wx1, wc, wx2, wx3, wx4, xw1, xw2, xw3, d1, d2, d3, gm1, gm2, gm3, upward, downward,
    near, copies,
):
    x1, cot, x2, x3, x4, odd, even, outer, inner, t1, k2, k3, p2, p3, p4 = near
    row_block = place_ref[0]
    at_left = place_ref[1] == 0
    at_right = place_ref[2] == 1
    core = place_ref[3]
    lane = lax.broadcasted_iota(jnp.int32, (1, 128), 1)
    low = lane < 64

    def lanes(a, b):
        return jnp.where(low, a, b).astype(F32)

    for ref in (wx1, wc, wx2, wx3, wx4, upward, downward):
        ref[...] = jnp.zeros_like(ref)
    for copy in copies[:10]:
        copy.wait()
    is_even = lax.rem(row_block, 2) == 0
    outer, inner = outer[...].astype(F32), inner[...].astype(F32)
    left, right = jnp.where(core == 0, outer, inner), jnp.where(core == 0, inner, outer)
    for side, to in ((None, RIM), (left, 0), (right, RIM + WIDE)):
        if side is None:
            cols = slice(to, to + WIDE)
            mid = [ref[...].astype(F32) for ref in (x1, cot, x2, x3, x4)]
            by_odd, by_even = odd[...].astype(F32), even[...].astype(F32)
        else:
            cols = slice(to, to + RIM)
            mid = [side[0:8], side[8:16], side[16:20], side[20:22], side[22:23]]
            by_odd, by_even = side[24:35], side[35:46]
        up, down = jnp.where(is_even, by_odd, by_even), jnp.where(is_even, by_even, by_odd)
        wx1[1:4, cols] = up[0:3]
        wx1[4:12, cols] = mid[0]
        wx1[12:15, cols] = down[0:3]
        wc[2:4, cols] = up[3:5]
        wc[4:12, cols] = mid[1]
        wc[12:14, cols] = down[3:5]
        wx2[0:3, cols] = up[5:8]
        wx2[3:7, cols] = mid[2]
        wx2[7:10, cols] = down[5:8]
        wx3[0:2, cols] = up[8:10]
        wx3[2:4, cols] = mid[3]
        wx3[4:6, cols] = down[8:10]
        wx4[0:1, cols] = up[10:11]
        wx4[1:2, cols] = mid[4]
        wx4[2:3, cols] = down[10:11]

    for f in range(-1, 41):
        at = 8 + 16 * (f + 1)
        xw1[at : at + 16, 0:128] = tile(wx1, 4 + f)
        xw1[at : at + 16, 128:256] = jnp.where(low, tile(wx1, 5 + f), tile(wx1, 3 + f))
    xw1[0:8, :] = jnp.zeros((8, 256), F32)
    xw1[680:688, :] = jnp.zeros((8, 256), F32)
    pre1 = xw1[8:680, 0:128]
    for i in range(3):
        pre1 = pre1 + jnp.dot(xw1[7 + i : 679 + i, :].astype(BF), t1[i], preferred_element_type=F32)
    y1, slope = gelu_both(pre1)
    y1 = y1.astype(BF).astype(F32)
    d1[...] = slope

    copies[10].wait()
    for j in range(3):
        for c in range(-2, 42):
            at = 8 + 16 * (c + 2)
            xw2[at : at + 16, 128 * j : 128 * j + 128] = tile(wx2, 3 + c + j)
    xw2[0:8, :] = jnp.zeros((8, 384), F32)
    xw2[712:720, :] = jnp.zeros((8, 384), F32)
    pre2 = xw2[8:712, 128:256]
    for i in range(3):
        pre2 = pre2 + jnp.dot(xw2[7 + i : 711 + i, :].astype(BF), k2[i], preferred_element_type=F32)
    y2, slope = gelu_both(pre2)
    y2 = y2.astype(BF)
    d2[...] = slope

    copies[11].wait()
    for j in range(3):
        for c in range(-1, 21):
            at = 8 + 8 * (c + 1)
            first = RIM + 256 * (c + j - 1)
            xw3[at : at + 8, 256 * j : 256 * j + 256] = wx3[:, first : first + 256]
    xw3[0:8, :] = jnp.zeros((8, 768), F32)
    xw3[184:192, :] = jnp.zeros((8, 768), F32)
    pre3 = xw3[8:184, 256:512]
    for i in range(3):
        pre3 = pre3 + jnp.dot(xw3[7 + i : 183 + i, :].astype(BF), k3[i], preferred_element_type=F32)
    y3, slope = gelu_both(pre3)
    y3 = y3.astype(BF)
    d3[...] = slope

    y4 = jnp.concatenate([wx4[:, 512 * c : 512 * c + 512] for c in range(12)], axis=0).astype(BF)

    for copy in copies[12:]:
        copy.wait()
    weights = row_weights((16, 32), 1, row_block).astype(BF)
    rows_up = []
    for y, p, rim, rows, wlo in ((y2, p2, 2, 16, 0), (y3, p3, 1, 8, 16), (y4, p4, 1, 8, 24)):
        twice = jnp.concatenate([p[...], p[...]], axis=0)
        coarse = lax.dot_general(y, twice, NT, preferred_element_type=F32).astype(BF).astype(F32)
        cols = [coarse[rows * n : rows * (n + 1)] for n in range(coarse.shape[0] // rows)]
        end = len(cols) - rim
        cols[rim - 1] = jnp.where(at_left, cols[rim], cols[rim - 1])
        cols[end] = jnp.where(at_right, cols[end - 1], cols[end])
        flat = jnp.concatenate(cols, axis=1).astype(BF)
        rows_up.append(jnp.dot(weights[:, wlo : wlo + rows], flat, preferred_element_type=F32))
    up2, up3, up4 = rows_up

    gates = []
    for f in range(-1, 41):
        k = f + 2
        merged = y1[16 * (f + 1) : 16 * (f + 2)]
        merged = merged + 0.75 * tile(up2, k) + 0.25 * jnp.where(low, tile(up2, k - 1), tile(up2, k + 1))
        k, h = f // 2 + 1, f % 2
        if h == 0:
            merged = merged + lanes(0.375, 0.125) * tile(up3, k - 1) + lanes(0.625, 0.875) * tile(up3, k)
        else:
            merged = merged + lanes(0.875, 0.625) * tile(up3, k) + lanes(0.125, 0.375) * tile(up3, k + 1)
        k, h = f // 4 + 1, f % 4
        p_low, p_high = (2 * h + 0.5) / 8 - 0.5, (2 * h + 1.5) / 8 - 0.5
        other = k - 1 if h < 2 else k + 1
        merged = merged + lanes(1 - abs(p_low), 1 - abs(p_high)) * tile(up4, k)
        merged = merged + lanes(abs(p_low), abs(p_high)) * tile(up4, other)
        slope = gelu_both(merged)[1]
        gate = (slope * tile(wc, 4 + f)).astype(BF).astype(F32)
        gates.append(gate)
        if 0 <= f < 40:
            g = (d1[16 * (f + 1) : 16 * (f + 2)] * gate).astype(BF).astype(F32)
            row = lax.broadcasted_iota(jnp.int32, (16, 1), 0)
            gm1[8 + 16 * f : 24 + 16 * f, :] = jnp.where((row >= 4) & (row < 12), g, 0.0)
            cols = slice(128 * f, 128 * (f + 1))
            g1_ref[:, cols] = g[4:12].astype(BF)
            upward[0:1, cols] = g[4:5]
            downward[0:1, cols] = g[11:12]
    gm1[0:8, :] = jnp.zeros((8, 128), F32)
    gm1[648:656, :] = jnp.zeros((8, 128), F32)

    flat = jnp.concatenate(gates, axis=1).astype(BF)
    weights_back = row_weights((32, 16), 0, row_block)
    k = lax.broadcasted_iota(jnp.int32, (32, 16), 0)
    r = lax.broadcasted_iota(jnp.int32, (32, 16), 1)
    weights_back = jnp.where((k < 24) | ((r >= 4) & (r < 12)), weights_back, 0.0).astype(BF)
    down = jnp.dot(weights_back, flat, preferred_element_type=F32)
    down2, down3, down4 = down[0:16], down[16:24], down[24:32]

    def folded(v):
        return v + pltpu.roll(v, 64, 1)

    cg2 = []
    for c in range(40):
        v = 0.75 * tile(down2, c + 1) + 0.25 * jnp.where(low, tile(down2, c + 2), tile(down2, c))
        if c == 0:
            v = v + jnp.where(at_left, lanes(0.25, 0.0) * tile(down2, 1), 0.0)
        if c == 39:
            v = v + jnp.where(at_right, lanes(0.0, 0.25) * tile(down2, 40), 0.0)
        cg2.append(folded(v))
    cg3 = []
    for c in range(20):
        at = 2 * c
        v = lanes(0.125, 0.375) * tile(down3, at) + lanes(0.625, 0.875) * tile(down3, at + 1)
        v = v + lanes(0.875, 0.625) * tile(down3, at + 2) + lanes(0.375, 0.125) * tile(down3, at + 3)
        if c == 0:
            v = v + jnp.where(at_left, lanes(0.375, 0.125) * tile(down3, 1), 0.0)
        if c == 19:
            v = v + jnp.where(at_right, lanes(0.125, 0.375) * tile(down3, 40), 0.0)
        cg3.append(folded(v))
    cg4 = []
    for c in range(-1, 11):
        v = jnp.zeros((8, 128), F32)
        for n in range(8):
            a, b = (2 * n + 0.5) / 8, (2 * n + 1.5) / 8
            a, b = (a, b) if n < 4 else (2 - a, 2 - b)
            pair = 4 * c - 2 + n
            if 0 <= pair < 40:
                v = v + lanes(a, b) * tile(down4, pair + 1)
        cg4.append(folded(v))
    cg4[1] = cg4[1] + jnp.where(at_left, cg4[0], 0.0)
    cg4[-2] = cg4[-2] + jnp.where(at_right, cg4[-1], 0.0)
    cg4[0] = jnp.where(at_left, 0.0, cg4[0])
    cg4[-1] = jnp.where(at_right, 0.0, cg4[-1])
    for n in range(12):
        cols = slice(128 * n, 128 * (n + 1))
        upward[3:4, cols] = cg4[n][0:1]
        rim_ref[0:1, cols] = cg4[n][1:2]
        downward[3:4, cols] = cg4[n][2:3]

    flat2 = jnp.concatenate(cg2, axis=0).astype(BF).astype(F32)
    flat3 = jnp.concatenate(cg3, axis=0).astype(BF).astype(F32)
    flat4 = jnp.concatenate(cg4, axis=0).astype(BF).astype(F32)
    back2 = jnp.dot(flat2[:, 0:64].astype(BF), p2[...], preferred_element_type=F32)
    back3 = jnp.dot(flat3[:, 0:64].astype(BF), p3[...], preferred_element_type=F32)
    g2 = (d2[32:672, :] * back2).astype(BF).astype(F32)
    g3 = (d3[8:168, :] * back3).astype(BF).astype(F32)

    row2 = lax.broadcasted_iota(jnp.int32, (640, 1), 0) % 16
    own2 = (row2 >= 3) & (row2 < 7)
    row3 = lax.broadcasted_iota(jnp.int32, (160, 1), 0) % 8
    own3 = (row3 >= 2) & (row3 < 4)
    gm2[0:8, :] = jnp.zeros((8, 128), F32)
    gm2[8:648, :] = jnp.where(own2, g2, 0.0)
    gm2[648:656, :] = jnp.zeros((8, 128), F32)
    gm3[0:8, :] = jnp.zeros((8, 256), F32)
    gm3[8:168, :] = jnp.where(own3, g3, 0.0)
    gm3[168:176, :] = jnp.zeros((8, 256), F32)
    for c in range(40):
        at, cols = 8 + 16 * c + 3, slice(128 * c, 128 * (c + 1))
        g2_ref[:, cols] = gm2[at : at + 4, :].astype(BF)
        upward[1:2, cols] = gm2[at : at + 1, :]
        downward[1:2, cols] = gm2[at + 3 : at + 4, :]
    for c in range(20):
        at, cols = 8 + 8 * c + 2, slice(256 * c, 256 * (c + 1))
        g3_ref[:, cols] = gm3[at : at + 2, :].astype(BF)
        upward[2:3, cols] = gm3[at : at + 1, :]
        downward[2:3, cols] = gm3[at + 1 : at + 2, :]
    odd_ref[...] = jnp.where(is_even, upward[0:4, :], downward[0:4, :]).astype(BF)
    even_ref[...] = jnp.where(is_even, downward[0:4, :], upward[0:4, :]).astype(BF)

    def put(at, first, second):
        rows = slice(at, at + first.shape[0])
        keep_ref[rows, :] = jnp.where(core == 0, first, second).astype(BF)
        send_ref[rows, :] = jnp.where(core == 0, second, first).astype(BF)

    cells = 327680
    x = xw3[16:176, :].astype(BF)
    shifted = jnp.concatenate([gm3[9 - i : 169 - i, :] for i in range(3)], axis=1).astype(BF)
    z = lax.dot_general(x, shifted, TN, preferred_element_type=F32) * (cells // 16) ** -0.5
    for i in range(3):
        put(768 * i, z[:, 256 * i : 256 * i + 128], z[:, 256 * i + 128 : 256 * i + 256])
    x = xw2[40:680, :].astype(BF)
    shifted = jnp.concatenate([gm2[9 - i : 649 - i, :] for i in range(3)], axis=1).astype(BF)
    z = lax.dot_general(x, shifted, TN, preferred_element_type=F32) * (cells // 4) ** -0.5
    put(2304, z[0:192, 0:128], z[192:384, 128:256])
    put(2496, z[192:384, 0:128], z[0:192, 256:384])
    put(2688, z[0:192, 128:256], z[192:384, 256:384])
    x = xw1[24:664, :].astype(BF)
    shifted = jnp.concatenate([gm1[9 - i : 649 - i, :] for i in range(3)], axis=1).astype(BF)
    z = lax.dot_general(x, shifted, TN, preferred_element_type=F32) * cells**-0.5
    window = (192, 0, 64, 128)
    blocks = []
    for i in range(3):
        zi = z[:, 128 * i : 128 * (i + 1)]
        for j in range(3):
            a, b = window[j], window[j + 1]
            blocks.append(zi[a : a + 64] + pltpu.roll(zi[b : b + 64], 64, 1))
    blocks.append(jnp.zeros((64, 128), F32))
    pairs = [jnp.where(low, blocks[n], pltpu.roll(blocks[n + 1], 64, 1)) for n in range(0, 10, 2)]
    y2_own, y3_own = y2[32:672], y3.astype(F32)[8:168].astype(BF)
    for y, flat, mask, branch in (
        (y2_own, flat2, own2, 1),
        (y3_own, flat3, own3, 2),
        (y4, flat4, None, 3),
    ):
        masked = (flat if mask is None else jnp.where(mask, flat, 0.0)).astype(BF)
        z = lax.dot_general(masked, y, TN, preferred_element_type=F32) * (cells // 4**branch) ** -0.5
        pairs += [z[0:64, 128 * n : 128 * (n + 1)] for n in range(z.shape[1] // 128)]
    for n in range(6):
        put(2880 + 64 * n, pairs[2 * n], pairs[2 * n + 1])
    put(3264, jnp.zeros((64, 128), F32), jnp.zeros((64, 128), F32))


def by_side(flag, one_ref, other_ref):
    one, other = one_ref[...].astype(F32), other_ref[...].astype(F32)
    return jnp.where(flag, one, other), jnp.where(flag, other, one)


def rims_kernel(place_ref, g1_ref, g2_ref, g3_ref, rim_ref, odd_ref, even_ref, outer_ref, inner_ref, left, right):
    core = place_ref[3]
    above, below = by_side(lax.rem(place_ref[0], 2) == 0, odd_ref, even_ref)
    g1, g2, g3 = (ref[...].astype(F32) for ref in (g1_ref, g2_ref, g3_ref))
    rim = rim_ref[...] + above[3:4, 0:1536] + below[3:4, 0:1536]
    for out, one, three, four in ((left, 0, 0, 0), (right, WIDE - 128, WIDE - 256, 1408)):
        ones, threes = slice(one, one + 128), slice(three, three + 256)
        out[...] = jnp.zeros_like(out)
        out[0:1, 0:128] = above[0:1, ones]
        out[1:9, 0:128] = g1[:, ones]
        out[9:10, 0:128] = below[0:1, ones]
        out[10:11, 0:128] = above[1:2, ones]
        out[11:15, 0:128] = g2[:, ones]
        out[15:16, 0:128] = below[1:2, ones]
        out[16:17, :] = above[2:3, threes]
        out[17:19, :] = g3[:, threes]
        out[19:20, :] = below[2:3, threes]
        out[20:21, 0:128] = rim[:, four : four + 128]
    outer_ref[...] = jnp.where(core == 0, left[...], right[...]).astype(BF)
    inner_ref[...] = jnp.where(core == 0, right[...], left[...]).astype(BF)


def backward_kernel(
    place_ref, g1_ref, g2_ref, g3_ref, rim_ref, odd_ref, even_ref, outer_ref, inner_ref, t1b, k2, k3, p4,
    gf1_ref, gf2_ref, gf3_ref, gf4_ref, wide1, wide2, wide3, xw1, xw2, xw3, out2, out3,
):
    low = lax.broadcasted_iota(jnp.int32, (1, 128), 1) < 64
    for ref, n in ((xw1, 640), (xw2, 320), (xw3, 160)):
        ref[0:8, :] = jnp.zeros((8, ref.shape[1]), F32)
        ref[8 + n : 16 + n, :] = jnp.zeros((8, ref.shape[1]), F32)
    above, below = by_side(lax.rem(place_ref[0], 2) == 0, odd_ref, even_ref)
    left, right = by_side(place_ref[3] == 0, outer_ref, inner_ref)
    for n, (wide, g_ref, top, rows, start, step) in enumerate(
        ((wide1, g1_ref, 3, 8, 0, 128), (wide2, g2_ref, 0, 4, 10, 128), (wide3, g3_ref, 0, 2, 16, 256))
    ):
        wide[...] = jnp.zeros_like(wide)
        mid, end = slice(step, step + WIDE), step + WIDE
        wide[top : top + 1, mid] = above[n : n + 1]
        wide[top + 1 : top + 1 + rows, mid] = g_ref[...].astype(F32)
        wide[top + 1 + rows : top + 2 + rows, mid] = below[n : n + 1]
        wide[top : top + 2 + rows, 0:step] = left[start : start + 2 + rows, 0:step]
        wide[top : top + 2 + rows, end : end + step] = right[start : start + 2 + rows, 0:step]

    for f in range(40):
        at = 8 + 16 * f
        xw1[at : at + 16, 0:128] = tile(wide1, f + 1)
        xw1[at : at + 16, 128:256] = jnp.where(low, tile(wide1, f + 2), tile(wide1, f))
    total = xw1[8:648, 0:128]
    for i in range(3):
        total = total + lax.dot_general(
            xw1[9 - i : 649 - i, :].astype(BF), t1b[i], NT, preferred_element_type=F32
        )
    for f in range(40):
        gf1_ref[:, 128 * f : 128 * (f + 1)] = total[16 * f + 4 : 16 * f + 12].astype(BF)

    for j in range(3):
        for c in range(40):
            xw2[8 + 8 * c : 16 + 8 * c, 128 * j : 128 * j + 128] = tile(wide2, c + 2 - j)
    total = xw2[8:328, 128:256]
    for i in range(3):
        kernel = jnp.concatenate([k2[i, 128 * j : 128 * j + 128, :] for j in range(3)], axis=1)
        total = total + lax.dot_general(
            xw2[9 - i : 329 - i, :].astype(BF), kernel, NT, preferred_element_type=F32
        )
    out2[...] = total
    for c in range(40):
        gf2_ref[:, 128 * c : 128 * (c + 1)] = out2[8 * c + 1 : 8 * c + 5, :].astype(BF)

    for j in range(3):
        for c in range(20):
            first = 256 * (c + 2 - j)
            xw3[8 + 8 * c : 16 + 8 * c, 256 * j : 256 * j + 256] = wide3[:, first : first + 256]
    total = xw3[8:168, 256:512]
    for i in range(3):
        kernel = jnp.concatenate([k3[i, 256 * j : 256 * j + 256, :] for j in range(3)], axis=1)
        total = total + lax.dot_general(
            xw3[9 - i : 169 - i, :].astype(BF), kernel, NT, preferred_element_type=F32
        )
    out3[...] = total
    for c in range(20):
        gf3_ref[:, 256 * c : 256 * (c + 1)] = out3[8 * c + 1 : 8 * c + 3, :].astype(BF)

    rim = rim_ref[...] + above[3:4, 0:1536] + below[3:4, 0:1536]
    for c in range(10):
        cg = rim[:, 128 * (c + 1) : 128 * (c + 2)]
        if c == 0:
            cg = cg + left[20:21, 0:128]
        if c == 9:
            cg = cg + right[20:21, 0:128]
        cg = jnp.broadcast_to(cg[:, 0:64], (8, 64)).astype(BF)
        back = jnp.dot(cg, p4[...], preferred_element_type=F32)
        gf4_ref[0:1, 512 * c : 512 * c + 512] = back[0:1].astype(BF)


def swapped(block, axis, flip):
    return lax.ppermute(block, axis, [(i, i ^ flip) for i in range(lax.axis_size(axis))])


def unpack_kernel(place_ref, mine, got, k1_ref, k2_ref, k3_ref, p2_ref, p3_ref, p4_ref):
    core = place_ref[3]

    def take(side, at, count):
        rows = slice(at, at + count)
        return jnp.where(core == side, mine[rows, :], got[rows, :])

    k3_ref[:, 0:128] = take(0, 0, 2304)
    k3_ref[:, 128:256] = take(1, 0, 2304)
    k2_ref[0:576, :] = take(0, 2304, 576)
    k2_ref[576:1152, :] = take(1, 2304, 576)
    pairs = [take(n % 2, 2880 + 64 * (n // 2), 64) for n in range(12)]
    for n in range(9):
        k1_ref[64 * n : 64 * (n + 1), :] = pairs[n // 2][:, 64 * (n % 2) : 64 * (n % 2) + 64]
    n = 5
    for ref, count in ((p2_ref, 1), (p3_ref, 2), (p4_ref, 4)):
        for m in range(count):
            ref[:, 128 * m : 128 * (m + 1)] = pairs[n]
            n += 1


def call(kernel, out_shapes, scratch, *operands, scalars=0, far=0):
    near = len(operands) - scalars - far
    specs = [pl.BlockSpec(memory_space=space) for space in (pltpu.SMEM, pltpu.VMEM, pl.ANY)]
    outs = len(out_shapes)

    def body(*refs):
        first, last = scalars + near, scalars + near + far
        sources = refs[first:last]
        if far:
            buffers, sems = refs[-1 - far : -1], refs[-1]
            copies = [pltpu.make_async_copy(sources[n], buffers[n], sems.at[n]) for n in range(far)]
            for copy in copies:
                copy.start()
            kernel(*refs[:first], *refs[last : -1 - far], buffers, copies)
        else:
            kernel(*refs)

    return pl.pallas_call(
        body,
        out_shape=[jax.ShapeDtypeStruct(shape, dtype) for shape, dtype in out_shapes],
        in_specs=[specs[0]] * scalars + [specs[1]] * near + [specs[2]] * far,
        out_specs=[specs[1]] * outs,
        scratch_shapes=[pltpu.VMEM(shape, dtype) for shape, dtype in scratch]
        + [pltpu.VMEM(operand.shape, operand.dtype) for operand in operands[len(operands) - far :]]
        + ([pltpu.SemaphoreType.DMA((far,))] if far else []),
        compiler_params=pltpu.CompilerParams(vmem_limit_bytes=48 * 1024 * 1024),
    )(*operands)


def pair_weights(kernel_one):
    none = jnp.zeros((3, FEAT_ONE, FEAT_ONE), BF)
    tap = lambda j: kernel_one[:, j] if 0 <= j < 3 else none
    windows = (1, 2, 3, 0)
    ahead = jnp.concatenate(
        [jnp.concatenate([tap(w - e) for w in windows], axis=1) for e in range(2)], axis=2
    )
    back = jnp.concatenate(
        [jnp.concatenate([tap(e - w + 2) for e in range(2)], axis=1) for w in windows], axis=2
    )
    return ahead, back


def local_part(x1, x2, x3, x4, kernel_one, kernel_two, kernel_three, p2, p3, p4, cot):
    place = jnp.stack(
        [
            lax.axis_index(ROWS),
            lax.axis_index(COLS),
            (lax.axis_index(COLS) == lax.axis_size(COLS) - 1).astype(jnp.int32),
            lax.axis_index("core"),
        ]
    ).astype(jnp.int32)
    ahead, back = pair_weights(kernel_one)
    k2 = kernel_two.reshape(3, 384, 128)
    k3 = kernel_three.reshape(3, 768, 256)
    fars = halos(place, x1, x2, x3, x4, cot) + (ahead, in_hbm(k2), in_hbm(k3), in_hbm(p2.T), in_hbm(p3.T), in_hbm(p4.T))
    total = RIM + WIDE + RIM
    keep, send, g1, g2, g3, rim, odd, even = call(
        forward_kernel,
        [
            ((PACK_ROWS, 128), BF), ((PACK_ROWS, 128), BF),
            ((8, WIDE), BF), ((4, WIDE), BF), ((2, WIDE), BF), ((1, 1536), F32),
            ((4, WIDE), BF), ((4, WIDE), BF),
        ],
        [
            ((16, total), F32), ((16, total), F32), ((16, total), F32), ((8, total), F32), ((8, total), F32),
            ((688, 256), F32), ((720, 384), F32), ((192, 768), F32),
            ((672, 128), F32), ((704, 128), F32), ((176, 256), F32),
            ((656, 128), F32), ((656, 128), F32), ((176, 256), F32),
            ((8, WIDE), F32), ((8, WIDE), F32),
        ],
        place,
        *fars,
        scalars=1,
        far=15,
    )
    return place, keep, send, (g1, g2, g3, rim), odd, even, (back, k2, k3, p4.T)


def from_beside(place, grads, odd, even):
    outer, inner = call(
        rims_kernel,
        [((32, 256), BF), ((32, 256), BF)],
        [((32, 256), F32), ((32, 256), F32)],
        place, *grads, odd, even,
        scalars=1,
    )
    return traded(outer, COLS, 1), traded(inner, COLS, 0)


def input_grads(place, grads, odd, even, outer, inner, weights):
    return call(
        backward_kernel,
        [((8, WIDE), BF), ((4, WIDE), BF), ((2, WIDE), BF), ((1, WIDE), BF)],
        [
            ((16, 42 * 128), F32), ((8, 42 * 128), F32), ((8, 22 * 256), F32),
            ((656, 256), F32), ((336, 384), F32), ((176, 768), F32),
            ((320, 128), F32), ((160, 256), F32),
        ],
        place, *grads, odd, even, outer, inner, *weights,
        scalars=1,
    )


def unpacked(place, mine, got):
    outs = call(
        unpack_kernel,
        [((576, 64), BF), ((1152, 128), BF), ((2304, 256), BF), ((64, 128), BF), ((64, 256), BF), ((64, 512), BF)],
        [],
        place, mine, got,
        scalars=1,
    )
    return (
        outs[0].reshape(3, 3, 64, 64), outs[1].reshape(3, 3, 128, 128), outs[2].reshape(3, 3, 256, 256),
        outs[3].T, outs[4].T, outs[5].T,
    )


def on_device(*args):
    place, keep, send, grads, odd, even, weights = local_part(*args)
    part = (keep.astype(F32) + swapped(send, "core", 1).astype(F32)).astype(BF)
    part, odd, even = lax.optimization_barrier((part, odd, even))

    pieces = lax.all_to_all(part.reshape(32, -1, 128), SLAB, 0, 0)
    odd, even = traded(odd, ROWS, 1), traded(even, ROWS, 0)
    part = jnp.sum(pieces.astype(F32), axis=0).astype(BF)

    pieces = lax.all_to_all(jnp.broadcast_to(part[None], (8,) + part.shape), "z_hi", 0, 0)
    pieces, odd, even = lax.optimization_barrier((pieces, odd, even))
    part = jnp.sum(pieces.astype(F32), axis=0).astype(BF)

    pieces = jnp.broadcast_to(part[None], (32,) + part.shape)
    mine = lax.all_to_all(pieces, SLAB, 0, 0).reshape(keep.shape)
    outer, inner = from_beside(place, grads, odd, even)
    outs = input_grads(place, grads, odd, even, outer, inner, weights)
    mine, outs = lax.optimization_barrier((mine, outs))
    return tuple(outs) + unpacked(place, mine, swapped(mine, "core", 1))


def solution(mesh):
    mesh = Mesh(mesh.devices.reshape(8, 2, 2, 4, 2, 2), ROWS + COLS)
    split = P(ROWS, COLS)
    in_specs = (split,) * 4 + (P(),) * 6 + (split,)
    out_specs = (split,) * 4 + (P(),) * 6
    return jax.shard_map(on_device, mesh=mesh, in_specs=in_specs, out_specs=out_specs, check_vma=False)
```
